32 devices in a mesh: context: 8 (over z, core), tensor: 4 (over y, x).
Axes of the slice: x: 2, y: 2, z: 4, core: 2. Of those that a mesh axis runs over, the one named last changes fastest.
Arguments:
- tokens: bfloat16 [4, 2048, 2048], P(None, 'context'), may hold values from -6 to 6
- block_order: int32 [16], replicated, may hold values from 0 to 15, each once
- query_weight: bfloat16 [2048, 2048], P('context', 'tensor'), may hold values from -0.110485435 to 0.110485435
- key_weight: bfloat16 [2048, 2048], P('context', 'tensor'), may hold values from -0.110485435 to 0.110485435
- value_weight: bfloat16 [2048, 2048], P('context', 'tensor'), may hold values from -0.125 to 0.125
- output_weight: bfloat16 [2048, 2048], P('tensor', 'context'), may hold values from -0.125 to 0.125
- gate_weight: bfloat16 [2048, 8192], P('context', 'tensor'), may hold values from -0.125 to 0.125
- up_weight: bfloat16 [2048, 8192], P('context', 'tensor'), may hold values from -0.125 to 0.125
- down_weight: bfloat16 [8192, 2048], P('tensor', 'context'), may hold values from -0.0625 to 0.0625
- query_gain: bfloat16 [2048], P('tensor'), may hold values from 0.25 to 1.75
- key_gain: bfloat16 [2048], P('tensor'), may hold values from 0.25 to 1.75
- attention_gain: bfloat16 [2048], P('context'), may hold values from 0.25 to 1.75
- forward_gain: bfloat16 [2048], P('context'), may hold values from 0.25 to 1.75
- cotangent: bfloat16 [4, 2048, 2048], P(None, 'context'), may hold values from -6 to 6
Outputs:
- layer_output: bfloat16 [4, 2048, 2048], P(None, 'context')
- tokens_grad: float32 [4, 2048, 2048], P(None, 'context')
- query_weight_grad: float32 [2048, 2048], P('context', 'tensor')
- key_weight_grad: float32 [2048, 2048], P('context', 'tensor')
- value_weight_grad: float32 [2048, 2048], P('context', 'tensor')
- output_weight_grad: float32 [2048, 2048], P('tensor', 'context')
- gate_weight_grad: float32 [2048, 8192], P('context', 'tensor')
- up_weight_grad: float32 [2048, 8192], P('context', 'tensor')
- down_weight_grad: float32 [8192, 2048], P('tensor', 'context')
- query_gain_grad: float32 [2048], P('tensor')
- key_gain_grad: float32 [2048], P('tensor')
- attention_gain_grad: float32 [2048], P('context')
- forward_gain_grad: float32 [2048], P('context')
The draws below stay inside these ranges and needn't reach their ends.
Inputs may be any that keep to these rules, and one draw needn't show every extreme that they name: `block_order`: each number once.
All inputs are finite; a program needn't handle non-finite values.
Results may differ from the reference program's by a relative error of at most 0.015.
Values may be sent and summed in bfloat16 or wider, within the bound.
A program may use at most 320 MiB of HBM per device.

```python
import jax
import jax.numpy as jnp
from jax import lax

D = 2048
HEADS = 16
HD = 128
FF = 8192
SEQ_LEN = 2048
SEQS = 4
N_CONTEXT = 8


def draw_query_weight(key, part):
    key = jax.random.fold_in(key, 7)
    column = jnp.arange(D, dtype=jnp.float32) / D
    entries = jnp.clip(jax.random.normal(key, (D, D), jnp.float32), -4.0, 4.0)
    factor = jnp.sqrt(0.5 + column)
    return (entries * factor[None, :] * D ** (-0.5)).astype(jnp.bfloat16)


def draw_key_weight(key, part):
    key = jax.random.fold_in(key, 13)
    column = jnp.arange(D, dtype=jnp.float32) / D
    entries = jnp.clip(jax.random.normal(key, (D, D), jnp.float32), -4.0, 4.0)
    factor = jnp.sqrt(0.5 + column)
    return (entries * factor[None, :] * D ** (-0.5)).astype(jnp.bfloat16)


def block_scale(own_key, extent, shards, smallest, top_value):
    level = 1.0
    for axis_at, shards_of in shards:
        draws = jax.random.uniform(jax.random.fold_in(jax.random.fold_in(own_key, 6), axis_at), (shards_of,), jnp.float32, smallest / len(shards), top_value / len(shards))
        level = level * jnp.repeat(jnp.exp(draws), extent[axis_at] // shards_of).reshape((-1,) + (1,) * (len(extent) - 1 - axis_at))
    return level


def scatter_about(stream_key, extent, spread, bound, split=(), held_as=jnp.bfloat16):
    level = block_scale(stream_key, extent, split, -0.22, 0.18) if split else 1.0
    values = jax.random.normal(stream_key, extent, jnp.float32) * spread * level
    return jnp.minimum(jnp.maximum(values, -bound), bound).astype(held_as)


def setup_inputs(seed: int = 0) -> dict:
    splits = jax.random.split(jax.random.key(seed), 15)
    return {
        "tokens": scatter_about(splits[0], (SEQS, SEQ_LEN, D), 1.0, 6.0, ((1, 8),)),
        "block_order": jax.random.permutation(splits[1], 2 * N_CONTEXT).astype(jnp.int32),
        "query_weight": draw_query_weight(jax.random.fold_in(splits[14], 71), 0),
        "key_weight": draw_key_weight(jax.random.fold_in(splits[14], 71), 0),
        "value_weight": scatter_about(splits[4], (D, D), D ** -0.5, 0.125, ((0, 8), (1, 4))),
        "output_weight": scatter_about(splits[5], (D, D), D ** -0.5, 0.125, ((0, 4), (1, 8))),
        "gate_weight": scatter_about(splits[6], (D, FF), D ** -0.5, 0.125, ((0, 8), (1, 4))),
        "up_weight": scatter_about(splits[7], (D, FF), D ** -0.5, 0.125, ((0, 8), (1, 4))),
        "down_weight": scatter_about(splits[8], (FF, D), FF ** -0.5, 0.0625, ((0, 4), (1, 8))),
        "query_gain": jnp.clip(1.0 + 0.15 * jax.random.normal(splits[9], (D,), jnp.float32), 0.25, 1.75).astype(jnp.bfloat16),
        "key_gain": jnp.clip(1.0 + 0.15 * jax.random.normal(splits[10], (D,), jnp.float32), 0.25, 1.75).astype(jnp.bfloat16),
        "attention_gain": jnp.clip(1.0 + 0.15 * jax.random.normal(splits[11], (D,), jnp.float32), 0.25, 1.75).astype(jnp.bfloat16),
        "forward_gain": jnp.clip(1.0 + 0.15 * jax.random.normal(splits[12], (D,), jnp.float32), 0.25, 1.75).astype(jnp.bfloat16),
        "cotangent": scatter_about(splits[13], (SEQS, SEQ_LEN, D), 1.0, 6.0, ((1, 8),)),
    }


EPS = 1e-06
THETA = 500000.0
HIGH = lax.Precision.HIGHEST

@jax.custom_vjp
def low(v):
    return lax.optimization_barrier(v.astype(jnp.bfloat16)).astype(jnp.float32)

@jax.custom_vjp
def low_back(v):
    return v

def low_keep(v):
    return (low(v), None)

def low_pass(kept, grad):
    return (grad,)

def back_keep(v):
    return (v, None)

def back_low(kept, grad):
    return (low(grad),)
low.defvjp(low_keep, low_pass)
low_back.defvjp(back_keep, back_low)

def rms_scale(values):
    return lax.rsqrt(lax.optimization_barrier(jnp.mean(values * values, axis=-1, keepdims=True)) + EPS)

def rotate(values, cosine, sine):
    half = values.shape[-1] // 2
    turned = jnp.concatenate([-values[..., half:], values[..., :half]], axis=-1)
    return values * cosine + turned * sine

def layer(x_seq, params, cosine, sine, allowed):
    query_weight, key_weight, value_weight, output_weight, gate_weight, up_weight, down_weight, query_gain, key_gain, attention_gain, forward_gain = params
    query_raw = low_back(jnp.dot(x_seq, query_weight, precision=HIGH))
    key_raw = low_back(jnp.dot(x_seq, key_weight, precision=HIGH))
    value = low(low_back(jnp.dot(x_seq, value_weight, precision=HIGH))).reshape(SEQ_LEN, HEADS, HD)
    query_normed = query_raw * rms_scale(query_raw) * query_gain
    key_normed = key_raw * rms_scale(key_raw) * key_gain
    query = low(rotate(query_normed.reshape(SEQ_LEN, HEADS, HD), cosine, sine))
    key = low(rotate(key_normed.reshape(SEQ_LEN, HEADS, HD), cosine, sine))
    scores = low_back(jnp.einsum('qhd,khd->hqk', query, key, precision=HIGH) * HD ** (-0.5))
    scores = jnp.where(allowed[None], scores, -1e+30)
    probs = low(jax.nn.softmax(scores, axis=-1))
    mixed = jnp.einsum('hqk,khd->qhd', probs, value, precision=HIGH).reshape(SEQ_LEN, D)
    mixed = low(low_back(mixed))
    attended = low_back(jnp.dot(mixed, output_weight, precision=HIGH))
    hidden = x_seq + attended * rms_scale(attended) * attention_gain
    hidden_low = low(hidden)
    gate = low_back(jnp.dot(hidden_low, gate_weight, precision=HIGH))
    up = low_back(jnp.dot(hidden_low, up_weight, precision=HIGH))
    act = low(jax.nn.silu(gate) * up)
    fed = low_back(jnp.dot(act, down_weight, precision=HIGH))
    return hidden + fed * rms_scale(fed) * forward_gain

def reference(tokens, block_order, query_weight, key_weight, value_weight, output_weight, gate_weight, up_weight, down_weight, query_gain, key_gain, attention_gain, forward_gain, cotangent):
    piece_len = SEQ_LEN // (2 * N_CONTEXT)
    stored = jnp.arange(SEQ_LEN, dtype=jnp.int32)
    place = block_order[stored // piece_len].astype(jnp.int32) * piece_len + stored % piece_len
    allowed = place[:, None] >= place[None, :]
    freq = THETA ** (-jnp.arange(0, HD, 2, dtype=jnp.float32) / HD)
    angle = place.astype(jnp.float32)[:, None] * freq[None, :]
    cosine = jnp.concatenate([jnp.cos(angle), jnp.cos(angle)], axis=-1)[:, None, :]
    sine = jnp.concatenate([jnp.sin(angle), jnp.sin(angle)], axis=-1)[:, None, :]
    params = tuple((item.astype(jnp.float32) for item in (query_weight, key_weight, value_weight, output_weight, gate_weight, up_weight, down_weight, query_gain, key_gain, attention_gain, forward_gain)))

    def forward(x_all, weights):
        single = jax.checkpoint(lambda x_seq: layer(x_seq, weights, cosine, sine, allowed))
        return lax.map(single, x_all)
    output, pullback = jax.vjp(forward, tokens.astype(jnp.float32), params)
    tokens_grad, grads = pullback(cotangent.astype(jnp.float32))
    return (output.astype(jnp.bfloat16), tokens_grad, grads[0], grads[1], grads[2], grads[3], grads[4], grads[5], grads[6], grads[7], grads[8], grads[9], grads[10])
```

```python
import functools

import jax
import jax.numpy as jnp
from jax import lax
from jax.experimental import pallas as pl
from jax.experimental.pallas import tpu as pltpu
from jax.sharding import PartitionSpec as P

HD = 128
EPS = 1e-06
THETA = 500000.0
BF = jnp.bfloat16
F32 = jnp.float32
VMEM_LIMIT = 60 * 1024 * 1024
MESH = pl.DeviceIdType.MESH


def dot_nn(left, right):
    return jnp.dot(left, right, preferred_element_type=F32)


def dot_nt(left, right):
    return lax.dot_general(left, right, (((1,), (1,)), ((), ())), preferred_element_type=F32)


def dot_tn(left, right):
    return lax.dot_general(left, right, (((0,), (0,)), ((), ())), preferred_element_type=F32)


def after(values, *others):
    return lax.optimization_barrier((values, *others))[0]


def swap(values, axis, mask):
    size = lax.axis_size(axis)
    return lax.ppermute(values, axis, [(i, i ^ mask) for i in range(size)])


def gather_rows(shard):
    return [shard] + [swap(shard, "tensor", k) for k in range(1, lax.axis_size("tensor"))]


def scatter_rows(parts):
    total = parts[0]
    for k in range(1, len(parts)):
        total = total + swap(parts[k].astype(BF), "tensor", k).astype(F32)
    return total


def sum_over_tensor(values):
    size = lax.axis_size("tensor")
    chunks = values.reshape(values.shape[0], size, -1)
    total = chunks
    for m in range(1, size):
        other = swap(chunks, "tensor", m)
        total = total + jnp.stack([other[:, m ^ k] for k in range(size)], axis=1)
    return total.reshape(values.shape)


def to_sequences(values, s, t):
    seqs, local_len, width = values.shape
    size = lax.axis_size("tensor")
    mine = lax.dynamic_index_in_dim(values.reshape(seqs, size, local_len // size, width), t, 1, keepdims=False)
    pieces = []
    for j in range(seqs):
        piece = lax.dynamic_index_in_dim(mine, s ^ j, 0, keepdims=False)
        pieces.append(piece if j == 0 else swap(piece, "context", 2 * j))
    return jnp.concatenate(pieces, axis=0)


def place_kernel(at_ref, in_ref, out_ref):
    for a in range(out_ref.shape[0]):
        out_ref[a, 0] = in_ref[0, a ^ at_ref[0]].astype(out_ref.dtype)


def to_ranks(shard, seqs):
    pieces = shard.reshape(seqs, -1, shard.shape[1])
    return jnp.stack([pieces[0]] + [swap(pieces[j], "context", 2 * j) for j in range(1, seqs)], axis=0)


def in_place(every, s, t, dtype):
    size, seqs, piece, width = every.shape
    full = pl.pallas_call(
        place_kernel,
        grid_spec=pltpu.PrefetchScalarGridSpec(
            num_scalar_prefetch=1,
            grid=(size,),
            in_specs=[pl.BlockSpec((1, seqs, piece, width), lambda b, at: (b ^ at[1], 0, 0, 0))],
            out_specs=pl.BlockSpec((seqs, 1, piece, width), lambda b, at: (0, b, 0, 0)),
        ),
        out_shape=jax.ShapeDtypeStruct((seqs, size, piece, width), dtype),
        name="place_rows",
    )(jnp.stack([s, t]).astype(jnp.int32), every)
    return full.reshape(seqs, size * piece, width)


def norm_factor(values):
    return lax.rsqrt(jnp.mean(values * values, axis=-1, keepdims=True) + EPS)


def norm_back(values, factor, gain, grad):
    scaled = grad * gain
    inner = jnp.mean(values * scaled, axis=-1, keepdims=True)
    return factor * scaled - values * (factor**3 * inner), grad * values * factor


def flip(index, mask):
    bit = 1
    result = index
    while bit <= mask:
        if mask & bit:
            result = result + bit - 2 * bit * ((index // bit) % 2)
        bit *= 2
    return result


def exchange_kernel(size, width, depth, offset, tile, finish, chips, last, n_in, n_out, a_ref, w_ref, *refs):
    ins, rest = refs[:n_in], refs[n_in:]
    every, outs, rest = rest[0], rest[1 : 1 + n_out], rest[1 + n_out :]
    a_buf, w_buf, sent, got, total, mine, a_sem, w_sem, sent_sem, got_sem, out_sem, in_sem, own_sem = rest[:13]
    t = lax.axis_index("tensor")
    c = lax.axis_index("context")
    rows = total.shape[0]
    half = rows // 2

    def a_copy(k):
        at = pl.ds(k * rows, rows)
        return pltpu.make_async_copy(a_ref.at[at, :], a_buf.at[at, :], a_sem.at[k])

    def w_copy(j):
        at = pl.ds(pl.multiple_of(j * tile, tile), tile)
        return pltpu.make_async_copy(w_ref.at[at, pl.ds(offset, depth)], w_buf.at[at, :], w_sem.at[j])

    order = [3, 1, 2, 0] if size == 4 else [*range(1, size), 0]
    tiles = width // tile
    parts = 2 if last and size == 4 else 1
    across = width // parts
    a_copy(order[0]).start()
    for j in range(tiles):
        w_copy(j).start()
    for k in order[1:]:
        a_copy(k).start()
    barrier = pltpu.get_barrier_semaphore()
    for k in range(1, size):
        pl.semaphore_signal(barrier, inc=1, device_id={"tensor": flip(t, k)}, device_id_type=MESH)

    met = range(1, 2 * chips) if last else range(2, 2 * chips, 2)
    for mask in met:
        pl.semaphore_signal(barrier, inc=1, device_id={"context": flip(c, mask)}, device_id_type=MESH)
    for out in outs:
        if out.shape[0] == 8:
            out[...] = jnp.zeros_like(out)

    def cross(j, source, target, sems, base=0):
        if j == 0:
            return pltpu.make_async_copy(source, target, sems[0].at[base])
        return pltpu.make_async_remote_copy(
            src_ref=source,
            dst_ref=target,
            send_sem=sems[0].at[base + j],
            recv_sem=sems[1].at[base + j],
            device_id={"context": flip(c, 2 * j)},
            device_id_type=MESH,
        )

    def send(slot, source, target, partner, sems):
        return pltpu.make_async_remote_copy(
            src_ref=source,
            dst_ref=target,
            send_sem=sems[0].at[slot],
            recv_sem=sems[1].at[slot],
            device_id={"tensor": flip(t, partner)},
            device_id_type=MESH,
        )

    def product(k, first=False, part=0):
        if part == 0:
            a_copy(k).wait()

        def step(j, carry):
            if first:
                w_copy(j).wait()
            at = pl.ds(pl.multiple_of(j * tile, tile), tile)
            value = dot_nt(a_buf[k * rows : (k + 1) * rows, :], w_buf[at, :])
            if k:
                sent[k - 1, :, at] = value.astype(BF)
            else:
                total[:, at] = value
            return carry

        lax.fori_loop(part * tiles // parts, (part + 1) * tiles // parts, step, 0)

    def add(slot, other, first, columns):
        def step(i, carry):
            at = pl.ds(pl.multiple_of(first + i * 16, 16), 16)
            sent[slot, at, columns] = (sent[slot, at, columns].astype(F32) + got[other, at, columns].astype(F32)).astype(BF)
            return carry

        lax.fori_loop(0, half // 16, step, 0)

    def columns_of_part(part):
        return pl.ds(part * across, across)

    low, high = pl.ds(0, half), pl.ds(half, half)
    sums = (sent_sem, got_sem)
    product(order[0], first=True)
    pl.semaphore_wait(barrier, size - 1 + len(met))
    piece = rows // max(1, chips)
    crossing = []
    small = []
    if last:
        gain_rows, head_rows, gain_got, head_got, own_got, small_sent, small_got = rest[18:]
        attn_rows, feed_rows, two_heads = ins[1:]
        gain_rows[...] = jnp.zeros_like(gain_rows)
        head_rows[...] = jnp.zeros_like(head_rows)
        for i, part in enumerate((attn_rows, feed_rows)):
            gain_rows[i : i + 1, :] = jnp.sum(part[...], axis=0, keepdims=True)
            head_rows[i : i + 1, :] = jnp.sum(two_heads[8 * i : 8 * i + 8, :], axis=0, keepdims=True)
        own_width = outs[0].shape[1]

        def tell(source, target, device):
            copy = pltpu.make_async_remote_copy(
                src_ref=source,
                dst_ref=target,
                send_sem=small_sent.at[len(small)],
                recv_sem=small_got.at[len(small)],
                device_id=device,
                device_id_type=MESH,
            )
            copy.start()
            small.append(copy)

        for k in range(1, size):
            tell(gain_rows, gain_got.at[k - 1], {"tensor": flip(t, k)})
        for mask in met:
            tell(head_rows, head_got.at[mask - 1], {"context": flip(c, mask)})
    if chips and not last:
        source, target = ins[0], outs[0]
        for j in range(chips):
            crossing.append(
                cross(
                    j,
                    source.at[flip(c // 2, j), pl.ds(pl.multiple_of(t * piece, piece), piece), :],
                    target.at[pl.ds(j * piece, piece), :],
                    rest[13:15],
                )
            )
            crossing[-1].start()

    def home(part):
        at = columns_of_part(part)
        return [
            cross(j, mine.at[pl.ds(j * piece, piece), at], rest[17].at[pl.ds(j * piece, piece), at], rest[15:17], part * chips)
            for j in range(chips)
        ]

    def finish_last(part, group):
        at = columns_of_part(part)
        for copy in group[2:] if size == 4 else group:
            copy.wait_recv()

        def step(i, carry):
            row = pl.ds(pl.multiple_of(i * 16, 16), 16)
            summed = ins[0][row, at] + total[row, at]
            for other in range(2 if size == 4 else size - 1):
                summed = summed + got[other, row, at].astype(F32)
            mine[row, at] = summed.astype(BF)
            return carry

        lax.fori_loop(0, rows // 16, step, 0)
        for copy in home(part):
            copy.start()

    def sums_of(part):
        at = columns_of_part(part)
        return [
            send(6 * part + 0, sent.at[2, low, at], got.at[2, low, at], 1, sums),
            send(6 * part + 1, sent.at[2, high, at], got.at[2, high, at], 2, sums),
            send(6 * part + 2, sent.at[0, low, at], got.at[0, low, at], 1, sums),
            send(6 * part + 3, sent.at[1, high, at], got.at[1, high, at], 2, sums),
            send(6 * part + 4, sent.at[1, low, at], got.at[1, low, at], 2, sums),
            send(6 * part + 5, sent.at[0, high, at], got.at[0, high, at], 1, sums),
        ]

    if size == 4:
        groups = [sums_of(part) for part in range(parts)]
        copies = sum(groups, [])
        copies[0].start()
        copies[1].start()
        product(1)
        copies[2].start()
        product(2)
        copies[3].start()
        for part in range(1, parts):
            product(3, first=True, part=part)
            product(1, part=part)
            product(2, part=part)
        for part, group in enumerate(groups):
            at = columns_of_part(part)
            group[0].wait_recv()
            add(1, 2, 0, at)
            group[4].start()
            group[1].wait_recv()
            add(0, 2, half, at)
            group[5].start()
            for copy in groups[part + 1][:4] if part + 1 < parts else []:
                copy.start()
            product(0, part=part)
            if part + 1 < parts:
                finish_last(part, group)
        if not last:
            for copy in copies[2:]:
                copy.wait_recv()
        used = 2
    else:
        copies = [send(k - 1, sent.at[k - 1], got.at[k - 1], k, sums) for k in range(1, size)]
        copies[0].start()
        for k in range(2, size):
            product(k)
            copies[k - 1].start()
        product(0)
        groups = [copies]
        if not last:
            for copy in copies:
                copy.wait_recv()
        used = size - 1
    if last:
        finish_last(parts - 1, groups[-1])
    if chips and not last:
        crossing[0].wait()
        for copy in crossing[1:]:
            copy.wait_recv()

    def finish_rows(first, count, part=0):
        def step(i, carry):
            at = pl.ds(pl.multiple_of(first + i * 16, 16), 16)
            summed = total[at, :]
            for other in range(used):
                summed = summed + got[other, at, :].astype(F32)
            mine[at, :] = finish(at, summed, ins, outs).astype(BF)
            return carry

        lax.fori_loop(0, count // 16, step, 0)

    gather = (out_sem, in_sem)
    shared = rest[17] if last else mine
    own = pltpu.make_async_copy(shared, every.at[pl.ds(0, rows), :], own_sem)
    if last:
        going_home = [home(part) for part in range(parts)]
    else:
        going_home = [[cross(j, outs[1].at[pl.ds(j * piece, piece), :], outs[2].at[j], rest[15:17]) for j in range(chips)]]
    if last:
        for copy in small:
            copy.wait()
        for k in range(1, size):
            gain_rows[...] += gain_got[k - 1]
        outs[1][...] = head_rows[...]
        for mask in met:
            outs[1][...] += head_got[mask - 1]
        for mask in met:
            at = pl.ds(pl.multiple_of(flip(c, mask) * own_width, own_width), own_width)
            tell(gain_rows.at[:, at], own_got.at[mask - 1], {"context": flip(c, mask)})

    def came_home(first, count, part=0):
        for j in range(first // piece, (first + count) // piece):
            if j == 0:
                going_home[part][j].wait()
            else:
                going_home[part][j].wait_recv()

    make_ready = came_home if last else finish_rows
    then = [own] if last else [own, *going_home[0]]
    if size == 4:

        def chunk(k, side, part):
            return every.at[pl.ds(k * rows + side * half, half), columns_of_part(part)]

        def share(k, side, part):
            source = shared.at[pl.ds(side * half, half), columns_of_part(part)]
            return send(6 * part + 2 * k + side, source, chunk(k + 1, side, part), k + 1, gather)

        groups = []
        for part in range(parts):
            shares = [share(k, side, part) for k in (0, 1) for side in (0, 1)]
            passed = [
                send(6 * part + 4, chunk(1, 0, part), chunk(3, 0, part), 2, gather),
                send(6 * part + 5, chunk(2, 1, part), chunk(3, 1, part), 1, gather),
            ]
            groups.append(shares + passed)
        for part, group in enumerate(groups):
            make_ready(0, half, part)
            group[0].start()
            group[2].start()
            make_ready(half, half, part)
            group[3].start()
            group[1].start()
            if part == parts - 1:
                for copy in then:
                    copy.start()
            group[0].wait_recv()
            group[4].start()
            group[3].wait_recv()
            group[5].start()
        for group in groups:
            for at in (1, 2, 4, 5):
                group[at].wait_recv()
        shares = sum(groups, [])
    else:
        make_ready(0, rows)
        shares = [send(k - 1, shared, every.at[pl.ds(k * rows, rows), :], k, gather) for k in range(1, size)]
        for copy in [*shares, *then]:
            copy.start()
        for copy in shares:
            copy.wait_recv()
    own.wait()
    if chips and not last:
        came_home(0, rows)
    if last:
        for copy in small[size - 1 + len(met) :]:
            copy.wait()
        outs[0][...] = gain_rows[:, pl.ds(pl.multiple_of(c * own_width, own_width), own_width)]
        for mask in met:
            outs[0][...] += own_got[mask - 1]
    for copy in copies + shares + crossing[1:] + sum([group[1:] for group in going_home], []):
        copy.wait_send()


def exchange(name, number, a, w, finish, ins, outs, offset=0, chips=0, last=False):
    size = lax.axis_size("tensor")
    rows, width, depth = a.shape[0] // size, w.shape[0], a.shape[1]
    tile = min(512, width)
    parts = 2 if last and size == 4 else 1
    links = 6 * parts if size == 4 else size - 1
    whole = pl.BlockSpec(memory_space=pltpu.VMEM)
    anywhere = pl.BlockSpec(memory_space=pl.ANY)
    dma = pltpu.SemaphoreType.DMA
    gain_scratch = []
    if last:
        own, head_width = outs[0][0][1], outs[1][0][1]
        ranks = 2 * chips
        gain_scratch = [
            pltpu.VMEM((rows, width), BF),
            pltpu.VMEM((8, width), F32),
            pltpu.VMEM((8, head_width), F32),
            pltpu.VMEM((size - 1, 8, width), F32),
            pltpu.VMEM((ranks - 1, 8, head_width), F32),
            pltpu.VMEM((ranks - 1, 8, own), F32),
            dma((size - 1 + 2 * (ranks - 1),)),
            dma((size - 1 + 2 * (ranks - 1),)),
        ]
    return pl.pallas_call(
        functools.partial(exchange_kernel, size, width, depth, offset, tile, finish, chips, last, len(ins), len(outs)),
        in_specs=[anywhere, anywhere] + [anywhere if chips and not last and i == 0 else whole for i in range(len(ins))],
        out_specs=[anywhere] + [whole] * len(outs),
        out_shape=[jax.ShapeDtypeStruct((size * rows, width), BF)] + [jax.ShapeDtypeStruct(*out) for out in outs],
        scratch_shapes=[
            pltpu.VMEM((size * rows, depth), BF),
            pltpu.VMEM((width, depth), BF),
            pltpu.VMEM((size - 1, rows, width), BF),
            pltpu.VMEM((size - 1, rows, width), BF),
            pltpu.VMEM((rows, width), F32),
            pltpu.VMEM((rows, width), BF),
            dma((size,)),
            dma((width // tile,)),
            dma((links,)),
            dma((links,)),
            dma((links,)),
            dma((links,)),
            dma,
        ]
        + [dma((chips * parts,))] * (4 if chips else 0)
        + gain_scratch,
        compiler_params=pltpu.CompilerParams(vmem_limit_bytes=VMEM_LIMIT, collective_id=number, has_side_effects=True),
        cost_estimate=pl.CostEstimate(flops=2 * size * rows * width * depth, bytes_accessed=240_000_000, transcendentals=0),
        name=name,
    )(a, w, *ins)


def add_rows(ref, values):
    ref[...] += values[:8] + values[8:]


def finish_attended(at, attended, ins, outs):
    tokens, gain = ins
    outs[0][at, :] = attended
    hidden = tokens[at, :].astype(F32) + attended * norm_factor(attended) * gain[...]
    outs[1][at, :] = hidden
    return hidden


def finish_fed(at, fed, ins, outs):
    hidden, gain = ins[1:]
    factor = norm_factor(fed)
    outs[1][at, :] = (hidden[at, :] + fed * factor * gain[...]).astype(BF)
    grad, gain_rows = norm_back(fed, factor, gain[...], outs[0][at, :].astype(F32))
    add_rows(outs[3], gain_rows)
    return grad


def finish_hidden_grad(at, summed, ins, outs):
    attended, cotangent, gain = ins
    hidden_grad = cotangent[at, :].astype(F32) + summed
    outs[0][at, :] = hidden_grad
    values = attended[at, :]
    grad, gain_rows = norm_back(values, norm_factor(values), gain[...], hidden_grad)
    add_rows(outs[1], gain_rows)
    return grad


def turn(values, cosine, sine):
    heads = [values[:, i : i + HD] for i in range(0, values.shape[1], HD)]
    return jnp.concatenate([head * cosine + pltpu.roll(head, HD // 2, 1) * sine for head in heads], axis=1)


def turn_kernel(core_ref, raw_ref, column_ref, gain_ref, cosine_ref, sine_ref, keep_ref, send_ref):
    width = gain_ref.shape[1]
    half = width // 2
    cosine, sine = cosine_ref[...], sine_ref[...]
    first = core_ref[0] == 0
    for i in range(3):
        values = raw_ref[:, i * width : (i + 1) * width]
        if i < 2:
            values = turn(values * column_ref[:, i : i + 1] * gain_ref[i : i + 1, :], cosine, sine)
        low, high = values[:, :half].astype(BF), values[:, half:].astype(BF)
        keep_ref[i] = jnp.where(first, low, high)
        send_ref[i] = jnp.where(first, high, low)


def head_grads(core_ref, own_ref, other_ref, i):
    first = core_ref[0] == 0
    own, other = own_ref[i], other_ref[i]
    return jnp.concatenate([jnp.where(first, own, other), jnp.where(first, other, own)], axis=1).astype(F32)


def inner_kernel(core_ref, own_ref, other_ref, raw_ref, column_ref, gain_ref, cosine_ref, sine_ref, inner_ref, gains_ref):
    width = gain_ref.shape[1]
    cosine, sine = cosine_ref[...], -sine_ref[...]

    @pl.when(pl.program_id(0) == 0)
    def _():
        gains_ref[...] = jnp.zeros_like(gains_ref)

    for i in range(2):
        flat = turn(head_grads(core_ref, own_ref, other_ref, i), cosine, sine) * raw_ref[:, i * width : (i + 1) * width]
        inner_ref[i] = lax.dot_general(
            jnp.ones((8, width), F32),
            flat * gain_ref[i : i + 1, :],
            (((1,), (1,)), ((), ())),
            precision=lax.Precision.HIGHEST,
            preferred_element_type=F32,
        )
        flat = flat * column_ref[:, i : i + 1]
        gains_ref[i] += jnp.sum(flat.reshape(-1, 8, width), axis=0)


def raw_grad_kernel(core_ref, own_ref, other_ref, raw_ref, column_ref, gain_ref, cosine_ref, sine_ref, out_ref):
    width = gain_ref.shape[1]
    cosine, sine = cosine_ref[...], -sine_ref[...]
    for i in range(3):
        values = head_grads(core_ref, own_ref, other_ref, i)
        if i < 2:
            values = turn(values, cosine, sine) * column_ref[:, i : i + 1] * gain_ref[i : i + 1, :]
            values = values - raw_ref[:, i * width : (i + 1) * width] * column_ref[:, i + 2 : i + 3]
        out_ref[:, i * width : (i + 1) * width] = values.astype(BF)


def by_rows(kernel, name, core, ins, outs, rows=128):
    def spec(shape, dim):
        block = tuple(rows if i == dim else extent for i, extent in enumerate(shape))
        return pl.BlockSpec(block, lambda i, core: tuple(i if at == dim else 0 for at in range(len(shape))))

    count = next(out[0][dim] for *out, dim in outs if dim is not None)
    return pl.pallas_call(
        kernel,
        grid_spec=pltpu.PrefetchScalarGridSpec(
            num_scalar_prefetch=1,
            grid=(count // rows,),
            in_specs=[spec((array.shape[0], count, array.shape[2]) if dim == 1 else array.shape, dim) for array, dim in ins],
            out_specs=[spec(shape, dim) for shape, _, dim in outs],
        ),
        out_shape=[jax.ShapeDtypeStruct(shape, dtype) for shape, dtype, _ in outs],
        compiler_params=pltpu.CompilerParams(vmem_limit_bytes=VMEM_LIMIT),
        name=name,
    )(core[None].astype(jnp.int32), *[array for array, _ in ins])


def act_back_kernel(tile, grad_ref, w_ref, gate_up_ref, out_ref):
    hidden = w_ref.shape[1]

    def step(j, carry):
        at = pl.ds(pl.multiple_of(j * tile, tile), tile)
        up_at = pl.ds(pl.multiple_of(hidden + j * tile, tile), tile)
        act_grad = dot_nn(grad_ref[...], w_ref[:, at])
        gate, up = gate_up_ref[:, at], gate_up_ref[:, up_at]
        logistic = jax.nn.sigmoid(gate)
        silu = gate * logistic
        out_ref[:, at] = (act_grad * up * (logistic + silu * (1.0 - logistic))).astype(BF)
        out_ref[:, up_at] = (act_grad * silu).astype(BF)
        return carry

    lax.fori_loop(0, hidden // tile, step, 0)


def act_back(fed_low, w_down, gate_up):
    count, width = fed_low.shape
    hidden = w_down.shape[1]
    rows = 256
    return pl.pallas_call(
        functools.partial(act_back_kernel, 256),
        grid=(count // rows,),
        in_specs=[
            pl.BlockSpec((rows, width), lambda i: (i, 0)),
            pl.BlockSpec((width, hidden), lambda i: (0, 0)),
            pl.BlockSpec((rows, 2 * hidden), lambda i: (i, 0)),
        ],
        out_specs=pl.BlockSpec((rows, 2 * hidden), lambda i: (i, 0)),
        out_shape=jax.ShapeDtypeStruct((count, 2 * hidden), BF),
        compiler_params=pltpu.CompilerParams(vmem_limit_bytes=VMEM_LIMIT),
        cost_estimate=pl.CostEstimate(flops=2 * count * width * hidden, bytes_accessed=40_000_000, transcendentals=count * hidden),
        name="act_back",
    )(fed_low, w_down, gate_up)


def rank_products_kernel(tile, count, core_ref, *refs):
    out_ref = refs[-1]
    base = 0
    for left_ref, right_ref in zip(refs[:count], refs[count : 2 * count]):
        left = left_ref[...].astype(F32).T.astype(BF)
        for at in range(0, right_ref.shape[1], tile):
            part = dot_nn(left, right_ref[:, at : at + tile])
            if len(refs) > 2 * count + 1:
                part = part + refs[2 * count][:, base + at : base + at + tile].astype(F32)
            out_ref[:, base + at : base + at + tile] = part.astype(BF)
        base += right_ref.shape[1]


def rank_products(core, pairs, own, added=None):
    lefts, rights = [left for left, _ in pairs], [right for _, right in pairs]
    count, width = lefts[0].shape
    chips = width // (2 * own)
    across = sum(right.shape[1] for right in rights)
    block = pl.BlockSpec((own, across), lambda j, core: (j, 0))
    return pl.pallas_call(
        functools.partial(rank_products_kernel, min(512, *[right.shape[1] for right in rights]), len(pairs)),
        grid_spec=pltpu.PrefetchScalarGridSpec(
            num_scalar_prefetch=1,
            grid=(chips,),
            in_specs=[pl.BlockSpec((count, own), lambda j, core: (0, 2 * j + core[0]))] * len(pairs)
            + [pl.BlockSpec(right.shape, lambda j, core: (0, 0)) for right in rights]
            + [block] * (added is not None),
            out_specs=block,
        ),
        out_shape=jax.ShapeDtypeStruct((chips * own, across), BF),
        compiler_params=pltpu.CompilerParams(vmem_limit_bytes=VMEM_LIMIT),
        cost_estimate=pl.CostEstimate(flops=count * width * across, bytes_accessed=30_000_000, transcendentals=0),
        name="rank_products",
    )(core[None].astype(jnp.int32), *lefts, *rights, *([] if added is None else [added]))


def columns_of(*values):
    stacked = jnp.stack(values, axis=1)
    return jnp.pad(stacked, ((0, 0), (0, 8 - len(values))))


def in_order(at_ref, source, target, piece):
    def step(p, carry):
        start = pl.multiple_of(at_ref[p], piece)
        target[pl.ds(pl.multiple_of(p * piece, piece), piece), :] = source[pl.ds(start, piece), :]
        return carry

    lax.fori_loop(0, target.shape[0] // piece, step, 0)


def out_of_order(at_ref, source, target, piece):
    def step(p, carry):
        start = pl.multiple_of(at_ref[p], piece)
        target[pl.ds(start, piece), :] = source[pl.ds(pl.multiple_of(p * piece, piece), piece), :].astype(target.dtype)
        return carry

    lax.fori_loop(0, source.shape[0] // piece, step, 0)


def causal(tile):
    key_at = lax.broadcasted_iota(jnp.int32, (tile, tile), 0)
    query_at = lax.broadcasted_iota(jnp.int32, (tile, tile), 1)
    return query_at >= key_at


def attend_kernel(piece, tile, at_ref, qkv_ref, out_ref, log_ref, query, key, value, value_t, mixed):
    for slot, held in enumerate((query, key, value)):
        in_order(at_ref, qkv_ref.at[slot], held, piece)
    value_t[...] = value[...].astype(F32).T.astype(BF)
    allowed = causal(tile)
    for i in range(query.shape[0] // tile):
        low, high = i * tile, (i + 1) * tile
        rows = query[low:high, :]
        near = jnp.where(allowed, dot_nt(key[low:high, :], rows) * HD ** (-0.5), -1e30)
        top = jnp.max(near, axis=0, keepdims=True)
        if i:
            far = dot_nt(key[0:low, :], rows) * HD ** (-0.5)
            top = jnp.maximum(top, jnp.max(far, axis=0, keepdims=True))
        near = jnp.exp(near - top)
        total = jnp.sum(near, axis=0, keepdims=True)
        summed = dot_nn(value_t[:, low:high], near.astype(BF))
        if i:
            far = jnp.exp(far - top)
            total = total + jnp.sum(far, axis=0, keepdims=True)
            summed = summed + dot_nn(value_t[:, 0:low], far.astype(BF))
        mixed[low:high, :] = (summed / total).T
        log_ref[0, :, low:high] = top + jnp.log(total)
    out_of_order(at_ref, mixed, out_ref, piece)


def attend(qkv, at, piece):
    rows, width = qkv.shape[1:]
    heads = width // HD
    return pl.pallas_call(
        functools.partial(attend_kernel, piece, 256),
        grid_spec=pltpu.PrefetchScalarGridSpec(
            num_scalar_prefetch=1,
            grid=(heads,),
            in_specs=[pl.BlockSpec((3, rows, HD), lambda h, at: (0, 0, h))],
            out_specs=[
                pl.BlockSpec((rows, HD), lambda h, at: (0, h)),
                pl.BlockSpec((1, 1, rows), lambda h, at: (h, 0, 0)),
            ],
            scratch_shapes=[pltpu.VMEM((rows, HD), BF)] * 3 + [pltpu.VMEM((HD, rows), BF), pltpu.VMEM((rows, HD), F32)],
        ),
        out_shape=[jax.ShapeDtypeStruct((rows, width), BF), jax.ShapeDtypeStruct((heads, 1, rows), F32)],
        compiler_params=pltpu.CompilerParams(vmem_limit_bytes=VMEM_LIMIT),
        cost_estimate=pl.CostEstimate(
            flops=2 * 2 * heads * rows * rows * HD, bytes_accessed=8 * rows * width, transcendentals=heads * rows * rows // 2
        ),
        name="attend",
    )(at, qkv)


def attend_back_kernel(
    piece, tile, at_ref, qkv_ref, out_ref, grad_ref, log_ref, dqkv_ref, query, key, value, key_t, grad, mixed, dquery, dkey, dvalue
):
    for slot, held in enumerate((query, key, value)):
        in_order(at_ref, qkv_ref.at[slot], held, piece)
    in_order(at_ref, grad_ref, grad, piece)
    in_order(at_ref, out_ref, mixed, piece)
    key_t[...] = key[...].astype(F32).T.astype(BF)
    allowed = causal(tile)
    dkey[...] = jnp.zeros_like(dkey)
    dvalue[...] = jnp.zeros_like(dvalue)
    scale = HD ** (-0.5)
    for i in range(query.shape[0] // tile):
        low, high = i * tile, (i + 1) * tile
        rows = query[low:high, :]
        rows_grad = grad[low:high, :]
        log = log_ref[0, :, low:high]
        spread = jnp.sum((rows_grad.astype(F32) * mixed[low:high, :].astype(F32)).T, axis=0, keepdims=True)
        dquery_t = None
        for start, stop, masked in ((0, low, False), (low, high, True)):
            if start == stop:
                continue
            scores = dot_nt(key[start:stop, :], rows) * scale
            if masked:
                scores = jnp.where(allowed, scores, -1e30)
            probs = jnp.exp(scores - log)
            probs_grad = dot_nt(value[start:stop, :], rows_grad)
            scores_grad = (probs * (probs_grad - spread)).astype(BF)
            dvalue[start:stop, :] += dot_nn(probs.astype(BF), rows_grad)
            dkey[start:stop, :] += dot_nn(scores_grad, rows)
            term = dot_nn(key_t[:, start:stop], scores_grad)
            dquery_t = term if dquery_t is None else dquery_t + term
        dquery[low:high, :] = dquery_t.T * scale
    dkey[...] = dkey[...] * scale
    for slot, held in enumerate((dquery, dkey, dvalue)):
        out_of_order(at_ref, held, dqkv_ref.at[slot], piece)


def attend_back(qkv, out, grad, log, at, piece):
    rows, width = qkv.shape[1:]
    heads = width // HD
    return pl.pallas_call(
        functools.partial(attend_back_kernel, piece, 256),
        grid_spec=pltpu.PrefetchScalarGridSpec(
            num_scalar_prefetch=1,
            grid=(heads,),
            in_specs=[
                pl.BlockSpec((3, rows, HD), lambda h, at: (0, 0, h)),
                pl.BlockSpec((rows, HD), lambda h, at: (0, h)),
                pl.BlockSpec((rows, HD), lambda h, at: (0, h)),
                pl.BlockSpec((1, 1, rows), lambda h, at: (h, 0, 0)),
            ],
            out_specs=pl.BlockSpec((3, rows, HD), lambda h, at: (0, 0, h)),
            scratch_shapes=[pltpu.VMEM((rows, HD), BF)] * 3
            + [pltpu.VMEM((HD, rows), BF)]
            + [pltpu.VMEM((rows, HD), BF)] * 2
            + [pltpu.VMEM((rows, HD), F32)] * 3,
        ),
        out_shape=jax.ShapeDtypeStruct((3, rows, width), BF),
        compiler_params=pltpu.CompilerParams(vmem_limit_bytes=VMEM_LIMIT),
        cost_estimate=pl.CostEstimate(
            flops=5 * heads * rows * rows * HD * 2, bytes_accessed=16 * rows * width, transcendentals=heads * rows * rows // 2
        ),
        name="attend_back",
    )(at, qkv, out, grad, log)


def local(
    tokens,
    block_order,
    query_weight,
    key_weight,
    value_weight,
    output_weight,
    gate_weight,
    up_weight,
    down_weight,
    query_gain,
    key_gain,
    attention_gain,
    forward_gain,
    cotangent,
):
    seqs, local_len, width = tokens.shape
    ranks = lax.axis_size("context")
    columns = lax.axis_size("tensor")
    full_len = local_len * ranks
    piece_len = full_len // block_order.shape[0]
    piece = local_len // columns
    shard_rows = seqs * piece
    count = shard_rows * columns
    context = lax.axis_index("context")
    t = lax.axis_index("tensor")
    s, core = context // 2, context % 2
    head_width = query_weight.shape[1]
    half_width = head_width // 2
    hidden_width = gate_weight.shape[1]

    def gather(values, axis):
        return lax.all_gather(values, "context", axis=axis, tiled=True)

    gain_columns = jnp.stack([attention_gain, forward_gain], axis=1)
    gain_columns = jnp.pad(gain_columns, ((0, 0), (0, HD - 2)))
    w_first = gather(jnp.concatenate([query_weight, key_weight, value_weight, output_weight.T, gain_columns], axis=1), 0)
    qkv_width = 3 * head_width
    gains = w_first[:, 4 * head_width :]
    gain_attn, gain_feed = gains[:, 0].astype(F32)[None], gains[:, 1].astype(F32)[None]
    w_gate_up = gather(jnp.concatenate([gate_weight, up_weight], axis=1), 0)
    w_down = gather(down_weight.T, 0)
    query_scaling = query_gain.astype(F32)
    key_scaling = key_gain.astype(F32)

    chips = s ^ jnp.arange(seqs, dtype=jnp.int32)
    shards = t ^ jnp.arange(columns, dtype=jnp.int32)
    starts = (2 * chips[None, :] + core) * local_len + shards[:, None] * piece
    stored = (starts[:, :, None] + jnp.arange(piece, dtype=jnp.int32)).reshape(count)
    block = stored // piece_len
    slots = jnp.arange(block_order.shape[0], dtype=jnp.int32)
    place = jnp.sum(jnp.where(block[:, None] == slots[None, :], block_order[None, :], 0), axis=1) * piece_len
    place = place + stored % piece_len
    freq = THETA ** (-jnp.arange(0, HD, 2, dtype=F32) / HD)
    angle = place.astype(F32)[:, None] * freq[None, :]
    cosine = jnp.concatenate([jnp.cos(angle), jnp.cos(angle)], axis=-1)
    sine = jnp.concatenate([-jnp.sin(angle), jnp.sin(angle)], axis=-1)
    per_block = piece_len // piece
    pieces = jnp.arange(full_len // piece, dtype=jnp.int32)
    hits = block_order[None, :] == (pieces // per_block)[:, None]
    block_at = jnp.sum(jnp.where(hits, slots[None, :], 0), axis=1)
    piece_at = block_at * per_block + pieces % per_block
    rank_of, shard_of = piece_at // columns, piece_at % columns
    at = (((rank_of % 2) ^ core) * columns + (shard_of ^ t)) * seqs + ((rank_of // 2) ^ s)
    at = (at * piece).astype(jnp.int32)

    row_shard = to_sequences(tokens, s, t)
    rows = jnp.concatenate(gather_rows(row_shard), axis=0)
    qkv_raw = dot_nn(rows, w_first[:, :qkv_width])
    query_raw = qkv_raw[:, :head_width]
    key_raw = qkv_raw[:, head_width : 2 * head_width]
    totals = sum_over_tensor(jnp.stack([jnp.sum(query_raw * query_raw, axis=1), jnp.sum(key_raw * key_raw, axis=1)]))
    factors = lax.rsqrt(totals / width + EPS)
    scaling = jnp.stack([query_gain, key_gain]).astype(F32)
    keep, send = by_rows(
        turn_kernel,
        "turn",
        core,
        [(qkv_raw, 0), (columns_of(*factors), 0), (scaling, None), (cosine, 0), (sine, 0)],
        [((3, count, half_width), BF, 1)] * 2,
    )
    qkv = jnp.concatenate([keep, swap(send, "context", 1)], axis=1)
    mixed_heads, log = attend(qkv, at, piece)

    def to_heads(values):
        keep = lax.dynamic_slice_in_dim(values, core * half_width, half_width, axis=1)
        send = lax.dynamic_slice_in_dim(values, (1 - core) * half_width, half_width, axis=1)
        return jnp.concatenate([keep, swap(send, "context", 1)], axis=0)

    def to_rows(values):
        own, other = values[:count], swap(values[count:], "context", 1)
        return jnp.concatenate([jnp.where(core == 0, own, other), jnp.where(core == 0, other, own)], axis=1)

    mixed_low = to_rows(mixed_heads)

    def chunk(values, k):
        return values[k * shard_rows : (k + 1) * shard_rows]

    order = list(range(columns))
    shard = (shard_rows, width)
    hidden_low, attended, hidden = exchange(
        "attended", 1, mixed_low, w_first, finish_attended, [row_shard, gain_attn], [(shard, F32), (shard, F32)], offset=qkv_width
    )
    gate_up = dot_nn(hidden_low, w_gate_up)
    gate, up = gate_up[:, :hidden_width], gate_up[:, hidden_width:]
    act_low = (gate * jax.nn.sigmoid(gate) * up).astype(BF)

    fed_low, upstream, _, output_pieces, feed_gain_rows = exchange(
        "fed",
        2,
        act_low,
        w_down,
        finish_fed,
        [cotangent, hidden, gain_feed],
        [(shard, BF), (shard, BF), ((seqs, piece, width), BF), ((8, width), F32)],
        chips=seqs,
    )

    own = width // ranks
    cores = [list(range(0, ranks, 2)), list(range(1, ranks, 2))]

    def product_sum(*pairs):
        other = swap(rank_products(1 - core, pairs, own), "context", 1)
        return rank_products(core, pairs, own, other)

    def scatter(values):
        return lax.psum_scatter(values, "context", scatter_dimension=0, axis_index_groups=cores, tiled=True)

    down_part = dot_tn(fed_low, act_low).astype(BF)
    down_summed = lax.psum_scatter(down_part, "context", scatter_dimension=0, tiled=True)
    output_rows = gather_rows(output_pieces)
    gate_up_low = act_back(after(fed_low, down_part), w_down, gate_up)
    gate_up_other = rank_products(1 - core, [(after(hidden_low, gate_up_low, *output_rows[:3]), gate_up_low)], own)
    gate_up_other = swap(gate_up_other, "context", 1)
    layer_output = in_place(jnp.stack(output_rows), s, t, BF)
    gate_up_part = rank_products(core, [(after(hidden_low, layer_output), gate_up_low)], own, gate_up_other)
    gate_up_summed = scatter(gate_up_part)
    gate_up_low = after(gate_up_low, gate_up_part)
    attended_low, hidden_grad, attn_gain_rows = exchange(
        "hidden_grad",
        3,
        gate_up_low,
        w_gate_up,
        finish_hidden_grad,
        [attended, upstream, gain_attn],
        [(shard, F32), ((8, width), F32)],
    )
    mixed_grad = dot_nn(attended_low, w_first[:, qkv_width : 4 * head_width]).astype(BF)
    dqkv = attend_back(qkv, mixed_heads, to_heads(mixed_grad), log, at, piece)
    dqkv_other = swap(dqkv[:, count:], "context", 1)
    inner, head_gain_rows = by_rows(
        inner_kernel,
        "inner",
        core,
        [(dqkv, 1), (dqkv_other, 1), (qkv_raw, 0), (columns_of(*factors), 0), (scaling, None), (cosine, 0), (sine, 0)],
        [((2, 8, count), F32, 2), ((2, 8, head_width), F32, None)],
    )
    inner = sum_over_tensor(inner[:, 0])
    (qkv_low,) = by_rows(
        raw_grad_kernel,
        "raw_grad",
        core,
        [
            (dqkv, 1),
            (dqkv_other, 1),
            (qkv_raw, 0),
            (columns_of(*factors, *(inner * factors**3 / width)), 0),
            (scaling, None),
            (cosine, 0),
            (sine, 0),
        ],
        [((count, 3 * head_width), BF, 0)],
    )
    qkv_part = product_sum((rows, qkv_low), (attended_low, mixed_low))
    qkv_out_summed = scatter(after(qkv_part, gate_up_summed, down_summed))
    every, width_gains, head_gains = exchange(
        "tokens_grad",
        4,
        after(qkv_low, qkv_part),
        w_first,
        None,
        [hidden_grad, attn_gain_rows, feed_gain_rows, head_gain_rows.reshape(16, head_width)],
        [((8, own), F32), ((8, head_width), F32)],
        chips=seqs,
        last=True,
    )
    tokens_grad = in_place(every.reshape(columns, seqs, piece, width), s, t, F32)

    down_summed, gate_up_summed, qkv_out_summed = (
        values.astype(F32) for values in (down_summed, gate_up_summed, qkv_out_summed)
    )
    return (
        layer_output,
        tokens_grad,
        qkv_out_summed[:, :head_width],
        qkv_out_summed[:, head_width : 2 * head_width],
        qkv_out_summed[:, 2 * head_width : 3 * head_width],
        qkv_out_summed[:, 3 * head_width :].T,
        gate_up_summed[:, :hidden_width],
        gate_up_summed[:, hidden_width:],
        down_summed.T,
        head_gains[0],
        head_gains[1],
        width_gains[0],
        width_gains[1],
    )


def solution(mesh):
    return jax.shard_map(
        local,
        mesh=mesh,
        in_specs=(
            P(None, "context", None),
            P(),
            P("context", "tensor"),
            P("context", "tensor"),
            P("context", "tensor"),
            P("tensor", "context"),
            P("context", "tensor"),
            P("context", "tensor"),
            P("tensor", "context"),
            P("tensor"),
            P("tensor"),
            P("context"),
            P("context"),
            P(None, "context", None),
        ),
        out_specs=(
            P(None, "context", None),
            P(None, "context", None),
            P("context", "tensor"),
            P("context", "tensor"),
            P("context", "tensor"),
            P("tensor", "context"),
            P("context", "tensor"),
            P("context", "tensor"),
            P("tensor", "context"),
            P("tensor"),
            P("tensor"),
            P("context"),
            P("context"),
        ),
        check_vma=False,
    )
```

```python
import functools

import jax
import jax.numpy as jnp
from jax import lax
from jax.experimental import pallas as pl
from jax.experimental.pallas import tpu as pltpu
from jax.sharding import PartitionSpec as P

HD = 128
EPS = 1e-06
THETA = 500000.0
BF = jnp.bfloat16
F32 = jnp.float32
VMEM_LIMIT = 60 * 1024 * 1024
MESH = pl.DeviceIdType.MESH


def dot_nn(left, right):
    return jnp.dot(left, right, preferred_element_type=F32)


def dot_nt(left, right):
    return lax.dot_general(left, right, (((1,), (1,)), ((), ())), preferred_element_type=F32)


def dot_tn(left, right):
    return lax.dot_general(left, right, (((0,), (0,)), ((), ())), preferred_element_type=F32)


def after(values, *others):
    return lax.optimization_barrier((values, *others))[0]


def swap(values, axis, mask):
    size = lax.axis_size(axis)
    return lax.ppermute(values, axis, [(i, i ^ mask) for i in range(size)])


def gather_rows(shard):
    return [shard] + [swap(shard, "tensor", k) for k in range(1, lax.axis_size("tensor"))]


def scatter_rows(parts):
    total = parts[0]
    for k in range(1, len(parts)):
        total = total + swap(parts[k].astype(BF), "tensor", k).astype(F32)
    return total


def sum_over_tensor(values):
    size = lax.axis_size("tensor")
    chunks = values.reshape(values.shape[0], size, -1)
    total = chunks
    for m in range(1, size):
        other = swap(chunks, "tensor", m)
        total = total + jnp.stack([other[:, m ^ k] for k in range(size)], axis=1)
    return total.reshape(values.shape)


def to_sequences(values, s, t):
    seqs, local_len, width = values.shape
    size = lax.axis_size("tensor")
    mine = lax.dynamic_index_in_dim(values.reshape(seqs, size, local_len // size, width), t, 1, keepdims=False)
    pieces = []
    for j in range(seqs):
        piece = lax.dynamic_index_in_dim(mine, s ^ j, 0, keepdims=False)
        pieces.append(piece if j == 0 else swap(piece, "context", 2 * j))
    return jnp.concatenate(pieces, axis=0)


def place_kernel(at_ref, in_ref, out_ref):
    for a in range(out_ref.shape[0]):
        out_ref[a, 0] = in_ref[0, a ^ at_ref[0]].astype(out_ref.dtype)


def to_ranks(shard, seqs):
    pieces = shard.reshape(seqs, -1, shard.shape[1])
    return jnp.stack([pieces[0]] + [swap(pieces[j], "context", 2 * j) for j in range(1, seqs)], axis=0)


def in_place(every, s, t, dtype):
    size, seqs, piece, width = every.shape
    full = pl.pallas_call(
        place_kernel,
        grid_spec=pltpu.PrefetchScalarGridSpec(
            num_scalar_prefetch=1,
            grid=(size,),
            in_specs=[pl.BlockSpec((1, seqs, piece, width), lambda b, at: (b ^ at[1], 0, 0, 0))],
            out_specs=pl.BlockSpec((seqs, 1, piece, width), lambda b, at: (0, b, 0, 0)),
        ),
        out_shape=jax.ShapeDtypeStruct((seqs, size, piece, width), dtype),
        name="place_rows",
    )(jnp.stack([s, t]).astype(jnp.int32), every)
    return full.reshape(seqs, size * piece, width)


def norm_factor(values):
    return lax.rsqrt(jnp.mean(values * values, axis=-1, keepdims=True) + EPS)


def norm_back(values, factor, gain, grad):
    scaled = grad * gain
    inner = jnp.mean(values * scaled, axis=-1, keepdims=True)
    return factor * scaled - values * (factor**3 * inner), grad * values * factor


def flip(index, mask):
    bit = 1
    result = index
    while bit <= mask:
        if mask & bit:
            result = result + bit - 2 * bit * ((index // bit) % 2)
        bit *= 2
    return result


def exchange_kernel(size, width, depth, offset, tile, finish, chips, last, n_in, n_out, a_ref, w_ref, *refs):
    ins, rest = refs[:n_in], refs[n_in:]
    every, outs, rest = rest[0], rest[1 : 1 + n_out], rest[1 + n_out :]
    a_buf, w_buf, sent, got, total, mine, a_sem, w_sem, sent_sem, got_sem, out_sem, in_sem, own_sem = rest[:13]
    t = lax.axis_index("tensor")
    c = lax.axis_index("context")
    rows = total.shape[0]
    half = rows // 2

    def a_copy(k):
        at = pl.ds(k * rows, rows)
        return pltpu.make_async_copy(a_ref.at[at, :], a_buf.at[at, :], a_sem.at[k])

    def w_copy(j):
        at = pl.ds(pl.multiple_of(j * tile, tile), tile)
        return pltpu.make_async_copy(w_ref.at[at, pl.ds(offset, depth)], w_buf.at[at, :], w_sem.at[j])

    order = [3, 1, 2, 0] if size == 4 else [*range(1, size), 0]
    tiles = width // tile
    parts = 2 if last and size == 4 else 1
    across = width // parts
    a_copy(order[0]).start()
    for j in range(tiles):
        w_copy(j).start()
    for k in order[1:]:
        a_copy(k).start()
    barrier = pltpu.get_barrier_semaphore()
    for k in range(1, size):
        pl.semaphore_signal(barrier, inc=1, device_id={"tensor": flip(t, k)}, device_id_type=MESH)

    met = range(1, 2 * chips) if last else range(2, 2 * chips, 2)
    for mask in met:
        pl.semaphore_signal(barrier, inc=1, device_id={"context": flip(c, mask)}, device_id_type=MESH)
    for out in outs:
        if out.shape[0] == 8:
            out[...] = jnp.zeros_like(out)

    def cross(j, source, target, sems, base=0):
        if j == 0:
            return pltpu.make_async_copy(source, target, sems[0].at[base])
        return pltpu.make_async_remote_copy(
            src_ref=source,
            dst_ref=target,
            send_sem=sems[0].at[base + j],
            recv_sem=sems[1].at[base + j],
            device_id={"context": flip(c, 2 * j)},
            device_id_type=MESH,
        )

    def send(slot, source, target, partner, sems):
        return pltpu.make_async_remote_copy(
            src_ref=source,
            dst_ref=target,
            send_sem=sems[0].at[slot],
            recv_sem=sems[1].at[slot],
            device_id={"tensor": flip(t, partner)},
            device_id_type=MESH,
        )

    def product(k, first=False, part=0):
        if part == 0:
            a_copy(k).wait()

        def step(j, carry):
            if first:
                w_copy(j).wait()
            at = pl.ds(pl.multiple_of(j * tile, tile), tile)
            value = dot_nt(a_buf[k * rows : (k + 1) * rows, :], w_buf[at, :])
            if k:
                sent[k - 1, :, at] = value.astype(BF)
            else:
                total[:, at] = value
            return carry

        lax.fori_loop(part * tiles // parts, (part + 1) * tiles // parts, step, 0)

    def add(slot, other, first, columns):
        def step(i, carry):
            at = pl.ds(pl.multiple_of(first + i * 16, 16), 16)
            sent[slot, at, columns] = (sent[slot, at, columns].astype(F32) + got[other, at, columns].astype(F32)).astype(BF)
            return carry

        lax.fori_loop(0, half // 16, step, 0)

    def columns_of_part(part):
        return pl.ds(part * across, across)

    low, high = pl.ds(0, half), pl.ds(half, half)
    sums = (sent_sem, got_sem)
    product(order[0], first=True)
    pl.semaphore_wait(barrier, size - 1 + len(met))
    piece = rows // max(1, chips)
    crossing = []
    small = []
    if last:
        gain_rows, head_rows, gain_got, head_got, own_got, small_sent, small_got = rest[18:]
        attn_rows, feed_rows, two_heads = ins[1:]
        gain_rows[...] = jnp.zeros_like(gain_rows)
        head_rows[...] = jnp.zeros_like(head_rows)
        for i, part in enumerate((attn_rows, feed_rows)):
            gain_rows[i : i + 1, :] = jnp.sum(part[...], axis=0, keepdims=True)
            head_rows[i : i + 1, :] = jnp.sum(two_heads[8 * i : 8 * i + 8, :], axis=0, keepdims=True)
        own_width = outs[0].shape[1]

        def tell(source, target, device):
            copy = pltpu.make_async_remote_copy(
                src_ref=source,
                dst_ref=target,
                send_sem=small_sent.at[len(small)],
                recv_sem=small_got.at[len(small)],
                device_id=device,
                device_id_type=MESH,
            )
            copy.start()
            small.append(copy)

        for k in range(1, size):
            tell(gain_rows, gain_got.at[k - 1], {"tensor": flip(t, k)})
        for mask in met:
            tell(head_rows, head_got.at[mask - 1], {"context": flip(c, mask)})
    if chips and not last:
        source, target = ins[0], outs[0]
        for j in range(chips):
            crossing.append(
                cross(
                    j,
                    source.at[flip(c // 2, j), pl.ds(pl.multiple_of(t * piece, piece), piece), :],
                    target.at[pl.ds(j * piece, piece), :],
                    rest[13:15],
                )
            )
            crossing[-1].start()

    def home(part):
        at = columns_of_part(part)
        return [
            cross(j, mine.at[pl.ds(j * piece, piece), at], rest[17].at[pl.ds(j * piece, piece), at], rest[15:17], part * chips)
            for j in range(chips)
        ]

    def finish_last(part, group):
        at = columns_of_part(part)
        for copy in group[2:] if size == 4 else group:
            copy.wait_recv()

        def step(i, carry):
            row = pl.ds(pl.multiple_of(i * 16, 16), 16)
            summed = ins[0][row, at] + total[row, at]
            for other in range(2 if size == 4 else size - 1):
                summed = summed + got[other, row, at].astype(F32)
            mine[row, at] = summed.astype(BF)
            return carry

        lax.fori_loop(0, rows // 16, step, 0)
        for copy in home(part):
            copy.start()

    def sums_of(part):
        at = columns_of_part(part)
        return [
            send(6 * part + 0, sent.at[2, low, at], got.at[2, low, at], 1, sums),
            send(6 * part + 1, sent.at[2, high, at], got.at[2, high, at], 2, sums),
            send(6 * part + 2, sent.at[0, low, at], got.at[0, low, at], 1, sums),
            send(6 * part + 3, sent.at[1, high, at], got.at[1, high, at], 2, sums),
            send(6 * part + 4, sent.at[1, low, at], got.at[1, low, at], 2, sums),
            send(6 * part + 5, sent.at[0, high, at], got.at[0, high, at], 1, sums),
        ]

    if size == 4:
        groups = [sums_of(part) for part in range(parts)]
        copies = sum(groups, [])
        copies[0].start()
        copies[1].start()
        product(1)
        copies[2].start()
        product(2)
        copies[3].start()
        for part in range(1, parts):
            product(3, first=True, part=part)
            product(1, part=part)
            product(2, part=part)
        for part, group in enumerate(groups):
            at = columns_of_part(part)
            group[0].wait_recv()
            add(1, 2, 0, at)
            group[4].start()
            group[1].wait_recv()
            add(0, 2, half, at)
            group[5].start()
            for copy in groups[part + 1][:4] if part + 1 < parts else []:
                copy.start()
            product(0, part=part)
            if part + 1 < parts:
                finish_last(part, group)
        if not last:
            for copy in copies[2:]:
                copy.wait_recv()
        used = 2
    else:
        copies = [send(k - 1, sent.at[k - 1], got.at[k - 1], k, sums) for k in range(1, size)]
        copies[0].start()
        for k in range(2, size):
            product(k)
            copies[k - 1].start()
        product(0)
        groups = [copies]
        if not last:
            for copy in copies:
                copy.wait_recv()
        used = size - 1
    if last:
        finish_last(parts - 1, groups[-1])
    if chips and not last:
        crossing[0].wait()
        for copy in crossing[1:]:
            copy.wait_recv()

    def finish_rows(first, count, part=0):
        def step(i, carry):
            at = pl.ds(pl.multiple_of(first + i * 16, 16), 16)
            summed = total[at, :]
            for other in range(used):
                summed = summed + got[other, at, :].astype(F32)
            mine[at, :] = finish(at, summed, ins, outs).astype(BF)
            return carry

        lax.fori_loop(0, count // 16, step, 0)

    gather = (out_sem, in_sem)
    shared = rest[17] if last else mine
    own = pltpu.make_async_copy(shared, every.at[pl.ds(0, rows), :], own_sem)
    if last:
        going_home = [home(part) for part in range(parts)]
    else:
        going_home = [[cross(j, outs[1].at[pl.ds(j * piece, piece), :], outs[2].at[j], rest[15:17]) for j in range(chips)]]
    if last:
        for copy in small:
            copy.wait()
        for k in range(1, size):
            gain_rows[...] += gain_got[k - 1]
        outs[1][...] = head_rows[...]
        for mask in met:
            outs[1][...] += head_got[mask - 1]
        for mask in met:
            at = pl.ds(pl.multiple_of(flip(c, mask) * own_width, own_width), own_width)
            tell(gain_rows.at[:, at], own_got.at[mask - 1], {"context": flip(c, mask)})

    def came_home(first, count, part=0):
        for j in range(first // piece, (first + count) // piece):
            if j == 0:
                going_home[part][j].wait()
            else:
                going_home[part][j].wait_recv()

    make_ready = came_home if last else finish_rows
    then = [own] if last else [own, *going_home[0]]
    if size == 4:

        def chunk(k, side, part):
            return every.at[pl.ds(k * rows + side * half, half), columns_of_part(part)]

        def share(k, side, part):
            source = shared.at[pl.ds(side * half, half), columns_of_part(part)]
            return send(6 * part + 2 * k + side, source, chunk(k + 1, side, part), k + 1, gather)

        groups = []
        for part in range(parts):
            shares = [share(k, side, part) for k in (0, 1) for side in (0, 1)]
            passed = [
                send(6 * part + 4, chunk(1, 0, part), chunk(3, 0, part), 2, gather),
                send(6 * part + 5, chunk(2, 1, part), chunk(3, 1, part), 1, gather),
            ]
            groups.append(shares + passed)
        for part, group in enumerate(groups):
            make_ready(0, half, part)
            group[0].start()
            group[2].start()
            make_ready(half, half, part)
            group[3].start()
            group[1].start()
            if part == parts - 1:
                for copy in then:
                    copy.start()
            group[0].wait_recv()
            group[4].start()
            group[3].wait_recv()
            group[5].start()
        for group in groups:
            for at in (1, 2, 4, 5):
                group[at].wait_recv()
        shares = sum(groups, [])
    else:
        make_ready(0, rows)
        shares = [send(k - 1, shared, every.at[pl.ds(k * rows, rows), :], k, gather) for k in range(1, size)]
        for copy in [*shares, *then]:
            copy.start()
        for copy in shares:
            copy.wait_recv()
    own.wait()
    if chips and not last:
        came_home(0, rows)
    if last:
        for copy in small[size - 1 + len(met) :]:
            copy.wait()
        outs[0][...] = gain_rows[:, pl.ds(pl.multiple_of(c * own_width, own_width), own_width)]
        for mask in met:
            outs[0][...] += own_got[mask - 1]
    for copy in copies + shares + crossing[1:] + sum([group[1:] for group in going_home], []):
        copy.wait_send()


def exchange(name, number, a, w, finish, ins, outs, offset=0, chips=0, last=False):
    size = lax.axis_size("tensor")
    rows, width, depth = a.shape[0] // size, w.shape[0], a.shape[1]
    tile = min(512, width)
    parts = 2 if last and size == 4 else 1
    links = 6 * parts if size == 4 else size - 1
    whole = pl.BlockSpec(memory_space=pltpu.VMEM)
    anywhere = pl.BlockSpec(memory_space=pl.ANY)
    dma = pltpu.SemaphoreType.DMA
    gain_scratch = []
    if last:
        own, head_width = outs[0][0][1], outs[1][0][1]
        ranks = 2 * chips
        gain_scratch = [
            pltpu.VMEM((rows, width), BF),
            pltpu.VMEM((8, width), F32),
            pltpu.VMEM((8, head_width), F32),
            pltpu.VMEM((size - 1, 8, width), F32),
            pltpu.VMEM((ranks - 1, 8, head_width), F32),
            pltpu.VMEM((ranks - 1, 8, own), F32),
            dma((size - 1 + 2 * (ranks - 1),)),
            dma((size - 1 + 2 * (ranks - 1),)),
        ]
    return pl.pallas_call(
        functools.partial(exchange_kernel, size, width, depth, offset, tile, finish, chips, last, len(ins), len(outs)),
        in_specs=[anywhere, anywhere] + [anywhere if chips and not last and i == 0 else whole for i in range(len(ins))],
        out_specs=[anywhere] + [whole] * len(outs),
        out_shape=[jax.ShapeDtypeStruct((size * rows, width), BF)] + [jax.ShapeDtypeStruct(*out) for out in outs],
        scratch_shapes=[
            pltpu.VMEM((size * rows, depth), BF),
            pltpu.VMEM((width, depth), BF),
            pltpu.VMEM((size - 1, rows, width), BF),
            pltpu.VMEM((size - 1, rows, width), BF),
            pltpu.VMEM((rows, width), F32),
            pltpu.VMEM((rows, width), BF),
            dma((size,)),
            dma((width // tile,)),
            dma((links,)),
            dma((links,)),
            dma((links,)),
            dma((links,)),
            dma,
        ]
        + [dma((chips * parts,))] * (4 if chips else 0)
        + gain_scratch,
        compiler_params=pltpu.CompilerParams(vmem_limit_bytes=VMEM_LIMIT, collective_id=number, has_side_effects=True),
        cost_estimate=pl.CostEstimate(flops=2 * size * rows * width * depth, bytes_accessed=240_000_000, transcendentals=0),
        name=name,
    )(a, w, *ins)


def add_rows(ref, values):
    ref[...] += values[:8] + values[8:]


def finish_attended(at, attended, ins, outs):
    tokens, gain = ins
    outs[0][at, :] = attended
    hidden = tokens[at, :].astype(F32) + attended * norm_factor(attended) * gain[...]
    outs[1][at, :] = hidden
    return hidden


def finish_fed(at, fed, ins, outs):
    hidden, gain = ins[1:]
    factor = norm_factor(fed)
    outs[1][at, :] = (hidden[at, :] + fed * factor * gain[...]).astype(BF)
    grad, gain_rows = norm_back(fed, factor, gain[...], outs[0][at, :].astype(F32))
    add_rows(outs[3], gain_rows)
    return grad


def finish_hidden_grad(at, summed, ins, outs):
    attended, cotangent, gain = ins
    hidden_grad = cotangent[at, :].astype(F32) + summed
    outs[0][at, :] = hidden_grad
    values = attended[at, :]
    grad, gain_rows = norm_back(values, norm_factor(values), gain[...], hidden_grad)
    add_rows(outs[1], gain_rows)
    return grad


def remote(source, target, sems, slot, device):
    return pltpu.make_async_remote_copy(
        src_ref=source,
        dst_ref=target,
        send_sem=sems[0].at[slot],
        recv_sem=sems[1].at[slot],
        device_id=device,
        device_id_type=MESH,
    )


def meet(t, c, size, masks):
    barrier = pltpu.get_barrier_semaphore()
    for k in range(1, size):
        pl.semaphore_signal(barrier, inc=1, device_id={"tensor": flip(t, k)}, device_id_type=MESH)
    for mask in masks:
        pl.semaphore_signal(barrier, inc=1, device_id={"context": flip(c, mask)}, device_id_type=MESH)
    return lambda: pl.semaphore_wait(barrier, size - 1 + len(masks))


class Line:
    def __init__(self, chips, own, buf, up_sems, down_sems, core_sems):
        self.chips, self.own, self.buf = chips, own, buf
        self.sems, self.core_sems = {1: up_sems, -1: down_sems}, core_sems
        self.c = lax.axis_index("context")
        self.s, self.core = self.c // 2, self.c % 2

    def rows(self, chip):
        return pl.ds(pl.multiple_of((2 * chip + self.core) * self.own, self.own), self.own)

    def hop(self, k, way, chip):
        part = self.buf.at[self.rows(chip), :]
        return remote(part, part, self.sems[way], k, {"context": self.c + 2 * way})

    def cross(self, k, way, chip):
        part = self.buf.at[self.rows(chip), :]
        return remote(part, part, self.core_sems, 0 if k < 0 else 1 + 2 * k + (way < 0), {"context": flip(self.c, 1)})

    def sends(self, k, way):
        if way > 0:
            return (self.s >= k) & (self.s < self.chips - 1)
        return (self.s + k < self.chips) & (self.s > 0)

    def gets(self, k, way):
        return self.s >= k + 1 if way > 0 else self.s + k + 1 < self.chips

    def each(self, test, k, act):
        for way in (1, -1):
            pl.when(test(k, way))(functools.partial(act, k, way))

    def start(self, k):
        self.each(self.sends, k, lambda k, way: self.hop(k, way, self.s - way * k).start())

    def begin(self):
        self.start(0)
        self.cross(-1, 1, self.s).start()

    def advance(self, k):
        def got(k, way):
            chip = self.s - way * (k + 1)
            self.hop(k, way, chip).wait_recv()
            self.cross(k, way, chip).start()

        self.each(self.gets, k, got)
        if k + 1 < self.chips - 1:
            self.start(k + 1)

    def other_core(self, k):
        if k < 0:
            self.cross(-1, 1, self.s).wait_recv()
        else:
            self.each(self.gets, k, lambda k, way: self.cross(k, way, self.s - way * (k + 1)).wait_recv())

    def end(self):
        self.cross(-1, 1, self.s).wait_send()
        for k in range(self.chips - 1):
            self.each(self.sends, k, lambda k, way: self.hop(k, way, self.s - way * k).wait_send())
            self.each(self.gets, k, lambda k, way: self.cross(k, way, self.s - way * (k + 1)).wait_send())


def line_sems(chips):
    dma = pltpu.SemaphoreType.DMA
    return [dma((chips - 1,))] * 4 + [dma((2 * chips - 1,))] * 2


class Sums:
    def __init__(self, size, t, sent, got, columns, sems, base):
        rows = sent.shape[1]
        low, high = pl.ds(0, rows // 2), pl.ds(rows // 2, rows // 2)
        self.size, self.sent, self.got, self.columns, self.half = size, sent, got, columns, rows // 2

        def send(slot, of, to, at, partner):
            return remote(sent.at[of, at, columns], got.at[to, at, columns], sems, base + slot, {"tensor": flip(t, partner)})

        if size == 4:
            self.copies = [
                send(0, 2, 2, low, 1),
                send(1, 2, 2, high, 2),
                send(2, 0, 0, low, 1),
                send(3, 1, 1, high, 2),
                send(4, 1, 1, low, 2),
                send(5, 0, 0, high, 1),
            ]
            self.after_product = {3: self.copies[:2], 1: self.copies[2:3], 2: self.copies[3:4]}
        else:
            self.copies = [send(k - 1, k - 1, k - 1, pl.ds(0, rows), k) for k in range(1, size)]
            self.after_product = {k: self.copies[k - 1 : k] for k in range(1, size)}

    def pass_on(self):
        if self.size != 4:
            return
        for copy, slot, first, then in ((0, 1, 0, 4), (1, 0, self.half, 5)):
            self.copies[copy].wait_recv()

            def step(i, carry):
                at = pl.ds(pl.multiple_of(first + i * 16, 16), 16)
                summed = self.sent[slot, at, self.columns].astype(F32) + self.got[2, at, self.columns].astype(F32)
                self.sent[slot, at, self.columns] = summed.astype(BF)
                return carry

            lax.fori_loop(0, self.half // 16, step, 0)
            self.copies[then].start()

    def wait(self):
        for copy in self.copies[2:] if self.size == 4 else self.copies:
            copy.wait_recv()


class Gather:
    def __init__(self, size, t, shared, every, sems, own_sem):
        rows = shared.shape[0]
        half = rows // 2
        self.size = size
        self.own = pltpu.make_async_copy(shared, every.at[pl.ds(0, rows), :], own_sem)

        def chunk(k, side):
            return every.at[pl.ds(k * rows + side * half, half), :]

        def send(slot, source, target, partner):
            return remote(source, target, sems, slot, {"tensor": flip(t, partner)})

        if size == 4:
            self.copies = [send(2 * k + side, shared.at[pl.ds(side * half, half), :], chunk(k + 1, side), k + 1) for k in (0, 1) for side in (0, 1)]
            self.copies += [send(4, chunk(1, 0), chunk(3, 0), 2), send(5, chunk(2, 1), chunk(3, 1), 1)]
            self.ready = (self.copies[0:3:2], self.copies[3:0:-2])
        else:
            self.copies = [send(k - 1, shared, every.at[pl.ds(k * rows, rows), :], k) for k in range(1, size)]
            self.ready = ((), self.copies)

    def start(self, side):
        for copy in self.ready[side]:
            copy.start()
        if side:
            self.own.start()

    def pass_on(self):
        if self.size == 4:
            self.copies[0].wait_recv()
            self.copies[4].start()
            self.copies[3].wait_recv()
            self.copies[5].start()

    def wait(self):
        for at, copy in enumerate(self.copies):
            if self.size != 4 or at not in (0, 3):
                copy.wait_recv()
        self.own.wait()

    def end(self):
        for copy in self.copies:
            copy.wait_send()


def links_of(size):
    return 6 if size == 4 else size - 1


def feed_kernel(size, chips, tile, *refs):
    h_ref, gate_up_w_ref, down_ref, cotangent_ref, residual_ref, gain_ref = refs[:6]
    every, slopes_ref, act_ref, down_all_ref, upstream, output, pieces, gain_rows = refs[6:14]
    h_buf, w_buf, act, down, sent, got, total, mine, stage = refs[14:23]
    h_sem, w_sem, stage_sem, keep_sem, own_sem = refs[23:28]
    line_refs, sums, gather, coming, going = refs[28:34], refs[34:36], refs[36:38], refs[38:40], refs[40:42]
    t, c = lax.axis_index("tensor"), lax.axis_index("context")
    s = c // 2
    rows, width = total.shape
    hidden = act.shape[1]
    own = down_ref.shape[0]
    piece = rows // chips
    tiles = hidden // tile
    order = [3, 1, 2, 0] if size == 4 else [*range(1, size), 0]
    line = Line(chips, own, down, line_refs[0:2], line_refs[2:4], line_refs[4:6])

    def h_copy(k):
        at = pl.ds(k * rows, rows)
        return pltpu.make_async_copy(h_ref.at[at, :], h_buf.at[at, :], h_sem.at[k])

    def w_copy(j, i):
        at = pl.ds(pl.multiple_of(i * hidden + j * tile, tile), tile)
        return pltpu.make_async_copy(gate_up_w_ref.at[:, at], w_buf.at[:, at], w_sem.at[j, i])

    own_rows = line.rows(s)
    own_down = pltpu.make_async_copy(down_ref, down.at[own_rows, :], keep_sem.at[0])
    own_down.start()
    wait_others = meet(t, c, size, [1, *range(2, 2 * chips, 2)])
    h_copy(order[0]).start()
    for j in range(tiles):
        for i in range(2):
            w_copy(j, i).start()
    for k in order[1:]:
        h_copy(k).start()
    gain_rows[...] = jnp.zeros_like(gain_rows)
    own_down.wait()
    wait_others()
    line.begin()

    def stage_copy(slot, i, k, j):
        at = pl.ds(pl.multiple_of(i * hidden + j * tile, tile), tile)
        return pltpu.make_async_copy(stage.at[slot, i], slopes_ref.at[pl.ds(k * rows, rows), at], stage_sem.at[slot, i])

    for n, k in enumerate(order):
        h_copy(k).wait()
        chunk = pl.ds(k * rows, rows)

        def step(j, carry):
            slot = (n * tiles + j) % 2
            if n == 0:
                for i in range(2):
                    w_copy(j, i).wait()

            @pl.when(n * tiles + j >= 2)
            def _():
                for i in range(2):
                    stage_copy(slot, i, k, j).wait()

            gate, up = [
                dot_nn(h_buf[chunk, :], w_buf[:, pl.ds(pl.multiple_of(i * hidden + j * tile, tile), tile)]) for i in range(2)
            ]
            logistic = jax.nn.sigmoid(gate)
            silu = gate * logistic
            act[chunk, pl.ds(pl.multiple_of(j * tile, tile), tile)] = (silu * up).astype(BF)
            stage[slot, 0] = (up * (logistic + silu * (1.0 - logistic))).astype(BF)
            stage[slot, 1] = silu.astype(BF)
            for i in range(2):
                stage_copy(slot, i, k, j).start()
            return carry

        lax.fori_loop(0, tiles, step, 0)
    for slot in range(2):
        for i in range(2):
            stage_copy(slot, i, 0, 0).wait()
    act_out = pltpu.make_async_copy(act, act_ref, keep_sem.at[1])
    act_out.start()

    rounds = []

    def fed_round(i):
        at = pl.ds(pl.multiple_of(flip(s, i) * 2 * own, 2 * own), 2 * own)
        group = Sums(size, t, sent, got, at, sums, links_of(size) * i)
        for k in order:
            value = dot_nt(act[k * rows : (k + 1) * rows, :], down[at, :])
            if k:
                sent[k - 1, :, at] = value.astype(BF)
                for copy in group.after_product[k]:
                    copy.start()
            else:
                total[:, at] = value
        rounds.append(group)

    line.advance(0)
    line.other_core(-1)
    fed_round(0)
    line.other_core(0)
    fed_round(1)
    rounds[0].pass_on()
    rounds[1].pass_on()
    for k in range(1, chips - 1):
        line.advance(k)
        line.other_core(k)
        fed_round(k + 1)
        if k + 1 == chips - 1:
            arrivals = [
                (cotangent_ref.at[flip(s, j), pl.ds(pl.multiple_of(t * piece, piece), piece), :], upstream.at[pl.ds(j * piece, piece), :])
                for j in range(chips)
            ]
            first = pltpu.make_async_copy(*arrivals[0], coming[0].at[0])
            others = [remote(*arrivals[j], coming, j, {"context": flip(c, 2 * j)}) for j in range(1, chips)]
            for copy in [first, *others]:
                copy.start()
        rounds[k + 1].pass_on()
    down_out = pltpu.make_async_copy(down, down_all_ref, keep_sem.at[2])
    down_out.start()
    for group in rounds:
        group.wait()
    first.wait()
    for copy in others:
        copy.wait_recv()

    used = 2 if size == 4 else size - 1

    def finish_rows(side):
        def step(i, carry):
            at = pl.ds(pl.multiple_of(side * (rows // 2) + i * 16, 16), 16)
            fed = total[at, :]
            for other in range(used):
                fed = fed + got[other, at, :].astype(F32)
            factor = norm_factor(fed)
            output[at, :] = (residual_ref[at, :] + fed * factor * gain_ref[...]).astype(BF)
            grad, gains = norm_back(fed, factor, gain_ref[...], upstream[at, :].astype(F32))
            gain_rows[...] += gains[:8] + gains[8:]
            mine[at, :] = grad.astype(BF)
            return carry

        lax.fori_loop(0, rows // 32, step, 0)

    share = Gather(size, t, mine, every, gather, own_sem)
    finish_rows(0)
    share.start(0)
    finish_rows(1)
    share.start(1)
    kept = pltpu.make_async_copy(output.at[pl.ds(0, piece), :], pieces.at[0], going[0].at[0])
    gone = [
        remote(output.at[pl.ds(j * piece, piece), :], pieces.at[j], going, j, {"context": flip(c, 2 * j)})
        for j in range(1, chips)
    ]
    for copy in [kept, *gone]:
        copy.start()
    share.pass_on()
    share.wait()
    kept.wait()
    for copy in gone:
        copy.wait_recv()
    act_out.wait()
    down_out.wait()
    line.end()
    share.end()
    for copy in [*sum([group.copies for group in rounds], []), *others, *gone]:
        copy.wait_send()


def feed(hidden_low, gate_up_weight, down_shard, cotangent, residual, gain, chips):
    size = lax.axis_size("tensor")
    count, width = hidden_low.shape
    rows = count // size
    own, hidden = down_shard.shape
    ranks = 2 * chips
    tile = min(512, hidden)
    links = links_of(size)
    dma = pltpu.SemaphoreType.DMA
    anywhere, whole = pl.BlockSpec(memory_space=pl.ANY), pl.BlockSpec(memory_space=pltpu.VMEM)
    shape = jax.ShapeDtypeStruct
    return pl.pallas_call(
        functools.partial(feed_kernel, size, chips, tile),
        in_specs=[anywhere] * 4 + [whole] * 2,
        out_specs=[anywhere] * 4 + [whole] * 4,
        out_shape=[
            shape((count, width), BF),
            shape((count, 2 * hidden), BF),
            shape((count, hidden), BF),
            shape((ranks * own, hidden), BF),
            shape((rows, width), BF),
            shape((rows, width), BF),
            shape((chips, rows // chips, width), BF),
            shape((8, width), F32),
        ],
        scratch_shapes=[
            pltpu.VMEM((count, width), BF),
            pltpu.VMEM((width, 2 * hidden), BF),
            pltpu.VMEM((count, hidden), BF),
            pltpu.VMEM((ranks * own, hidden), BF),
            pltpu.VMEM((size - 1, rows, width), BF),
            pltpu.VMEM((size - 1, rows, width), BF),
            pltpu.VMEM((rows, width), F32),
            pltpu.VMEM((rows, width), BF),
            pltpu.VMEM((2, 2, rows, tile), BF),
            dma((size,)),
            dma((hidden // tile, 2)),
            dma((2, 2)),
            dma((3,)),
            dma,
        ]
        + line_sems(chips)
        + [dma((links * chips,))] * 2
        + [dma((links,))] * 2
        + [dma((chips,))] * 4,
        compiler_params=pltpu.CompilerParams(vmem_limit_bytes=VMEM_LIMIT, collective_id=2, has_side_effects=True),
        cost_estimate=pl.CostEstimate(flops=6 * count * width * hidden, bytes_accessed=400_000_000, transcendentals=count * hidden),
        name="feed",
    )(hidden_low, gate_up_weight, down_shard, cotangent, residual, gain)


def turn(values, cosine, sine):
    heads = [values[:, i : i + HD] for i in range(0, values.shape[1], HD)]
    return jnp.concatenate([head * cosine + pltpu.roll(head, HD // 2, 1) * sine for head in heads], axis=1)


def turn_kernel(core_ref, raw_ref, column_ref, gain_ref, cosine_ref, sine_ref, keep_ref, send_ref):
    width = gain_ref.shape[1]
    half = width // 2
    cosine, sine = cosine_ref[...], sine_ref[...]
    first = core_ref[0] == 0
    for i in range(3):
        values = raw_ref[:, i * width : (i + 1) * width]
        if i < 2:
            values = turn(values * column_ref[:, i : i + 1] * gain_ref[i : i + 1, :], cosine, sine)
        low, high = values[:, :half].astype(BF), values[:, half:].astype(BF)
        keep_ref[i] = jnp.where(first, low, high)
        send_ref[i] = jnp.where(first, high, low)


def head_grads(core_ref, own_ref, other_ref, i):
    first = core_ref[0] == 0
    own, other = own_ref[i], other_ref[i]
    return jnp.concatenate([jnp.where(first, own, other), jnp.where(first, other, own)], axis=1).astype(F32)


def inner_kernel(core_ref, own_ref, other_ref, raw_ref, column_ref, gain_ref, cosine_ref, sine_ref, inner_ref, gains_ref):
    width = gain_ref.shape[1]
    cosine, sine = cosine_ref[...], -sine_ref[...]

    @pl.when(pl.program_id(0) == 0)
    def _():
        gains_ref[...] = jnp.zeros_like(gains_ref)

    for i in range(2):
        flat = turn(head_grads(core_ref, own_ref, other_ref, i), cosine, sine) * raw_ref[:, i * width : (i + 1) * width]
        inner_ref[i] = lax.dot_general(
            jnp.ones((8, width), F32),
            flat * gain_ref[i : i + 1, :],
            (((1,), (1,)), ((), ())),
            precision=lax.Precision.HIGHEST,
            preferred_element_type=F32,
        )
        flat = flat * column_ref[:, i : i + 1]
        gains_ref[i] += jnp.sum(flat.reshape(-1, 8, width), axis=0)


def raw_grad_kernel(core_ref, own_ref, other_ref, raw_ref, column_ref, gain_ref, cosine_ref, sine_ref, out_ref):
    width = gain_ref.shape[1]
    cosine, sine = cosine_ref[...], -sine_ref[...]
    for i in range(3):
        values = head_grads(core_ref, own_ref, other_ref, i)
        if i < 2:
            values = turn(values, cosine, sine) * column_ref[:, i : i + 1] * gain_ref[i : i + 1, :]
            values = values - raw_ref[:, i * width : (i + 1) * width] * column_ref[:, i + 2 : i + 3]
        out_ref[:, i * width : (i + 1) * width] = values.astype(BF)


def by_rows(kernel, name, core, ins, outs, rows=256):
    def spec(shape, dim):
        block = tuple(rows if i == dim else extent for i, extent in enumerate(shape))
        return pl.BlockSpec(block, lambda i, core: tuple(i if at == dim else 0 for at in range(len(shape))))

    count = next(out[0][dim] for *out, dim in outs if dim is not None)
    return pl.pallas_call(
        kernel,
        grid_spec=pltpu.PrefetchScalarGridSpec(
            num_scalar_prefetch=1,
            grid=(count // rows,),
            in_specs=[spec((array.shape[0], count, array.shape[2]) if dim == 1 else array.shape, dim) for array, dim in ins],
            out_specs=[spec(shape, dim) for shape, _, dim in outs],
        ),
        out_shape=[jax.ShapeDtypeStruct(shape, dtype) for shape, dtype, _ in outs],
        compiler_params=pltpu.CompilerParams(vmem_limit_bytes=VMEM_LIMIT),
        name=name,
    )(core[None].astype(jnp.int32), *[array for array, _ in ins])


def act_back_kernel(tile, grad_ref, w_ref, slopes_ref, out_ref):
    hidden = w_ref.shape[1]
    for j in range(0, hidden, tile):
        act_grad = dot_nn(grad_ref[...], w_ref[:, j : j + tile])
        for at in (j, hidden + j):
            out_ref[:, at : at + tile] = (act_grad * slopes_ref[:, at : at + tile].astype(F32)).astype(BF)


def act_back(fed_low, w_down, slopes):
    count, width = fed_low.shape
    hidden = w_down.shape[1]
    rows = 256
    return pl.pallas_call(
        functools.partial(act_back_kernel, 512),
        grid=(count // rows,),
        in_specs=[
            pl.BlockSpec((rows, width), lambda i: (i, 0)),
            pl.BlockSpec((width, hidden), lambda i: (0, 0)),
            pl.BlockSpec((rows, 2 * hidden), lambda i: (i, 0)),
        ],
        out_specs=pl.BlockSpec((rows, 2 * hidden), lambda i: (i, 0)),
        out_shape=jax.ShapeDtypeStruct((count, 2 * hidden), BF),
        compiler_params=pltpu.CompilerParams(vmem_limit_bytes=VMEM_LIMIT),
        cost_estimate=pl.CostEstimate(flops=2 * count * width * hidden, bytes_accessed=40_000_000, transcendentals=count * hidden),
        name="act_back",
    )(fed_low, w_down, slopes)


def rank_sums_kernel(chips, tile, count, *refs):
    lefts, rights, out_ref = refs[:count], refs[count : 2 * count], refs[2 * count]
    refs = refs[2 * count + 1 :]
    left_bufs, right_bufs = refs[:count], refs[count : 2 * count]
    passed, got, out, left_sem, right_sem, out_sem, sent_sem, got_sem = refs[2 * count :]
    c = lax.axis_index("context")
    core = c % 2
    own = out.shape[1]
    blocks = [(j, core_at) for core_at in (1, 0) for j in range(chips)]

    def left_copy(i, j, core_at):
        rank = 2 * j + (core if core_at == 0 else 1 - core)
        at = pl.ds(pl.multiple_of(rank * own, own), own)
        block = left_bufs[i].at[core_at * chips + j]
        return pltpu.make_async_copy(lefts[i].at[:, at], block, left_sem.at[i, core_at * chips + j])

    tiles = [right.shape[1] // tile for right in rights]

    def right_copy(i, n):
        at = pl.ds(pl.multiple_of(n * tile, tile), tile)
        return pltpu.make_async_copy(rights[i].at[:, at], right_bufs[i].at[:, at], right_sem.at[i, n])

    barrier = pltpu.get_barrier_semaphore()
    pl.semaphore_signal(barrier, inc=1, device_id={"context": flip(c, 1)}, device_id_type=MESH)
    for i in range(count):
        left_copy(i, *blocks[0]).start()
        for n in range(tiles[i]):
            right_copy(i, n).start()
        for block in blocks[1:]:
            left_copy(i, *block).start()
    pl.semaphore_wait(barrier, 1)
    sends = [remote(passed.at[j], got.at[j], (sent_sem, got_sem), j, {"context": flip(c, 1)}) for j in range(chips)]
    writes = [pltpu.make_async_copy(out.at[j], out_ref.at[pl.ds(j * own, own), :], out_sem.at[j]) for j in range(chips)]
    for at, (j, core_at) in enumerate(blocks):
        base = 0
        if core_at == 0:
            sends[j].wait_recv()
        for i in range(count):
            left_copy(i, j, core_at).wait()
            left = left_bufs[i][core_at * chips + j].astype(F32).T.astype(BF)

            def step(n, carry):
                if at == 0:
                    right_copy(i, n).wait()
                part = dot_nn(left, right_bufs[i][:, pl.ds(pl.multiple_of(n * tile, tile), tile)])
                to = pl.ds(pl.multiple_of(base + n * tile, tile), tile)
                if core_at:
                    passed[j, :, to] = part.astype(BF)
                else:
                    out[j, :, to] = (part + got[j, :, to].astype(F32)).astype(BF)
                return carry

            lax.fori_loop(0, tiles[i], step, 0)
            base += tiles[i] * tile
        (sends if core_at else writes)[j].start()
    for j in range(chips):
        sends[j].wait_send()
        writes[j].wait()


def rank_sums(number, pairs, own):
    lefts, rights = [left for left, _ in pairs], [right for _, right in pairs]
    count, width = lefts[0].shape
    chips = width // (2 * own)
    across = sum(right.shape[1] for right in rights)
    tile = min(512, *[right.shape[1] for right in rights])
    most = max(right.shape[1] for right in rights) // tile
    dma = pltpu.SemaphoreType.DMA
    return pl.pallas_call(
        functools.partial(rank_sums_kernel, chips, tile, len(pairs)),
        in_specs=[pl.BlockSpec(memory_space=pl.ANY)] * (2 * len(pairs)),
        out_specs=pl.BlockSpec(memory_space=pl.ANY),
        out_shape=jax.ShapeDtypeStruct((chips * own, across), BF),
        scratch_shapes=[pltpu.VMEM((2 * chips, count, own), BF)] * len(pairs)
        + [pltpu.VMEM(right.shape, BF) for right in rights]
        + [pltpu.VMEM((chips, own, across), BF)] * 3
        + [dma((len(pairs), 2 * chips)), dma((len(pairs), most)), dma((chips,)), dma((chips,)), dma((chips,))],
        compiler_params=pltpu.CompilerParams(vmem_limit_bytes=VMEM_LIMIT, collective_id=number, has_side_effects=True),
        cost_estimate=pl.CostEstimate(flops=2 * count * width * across, bytes_accessed=60_000_000, transcendentals=0),
        name="rank_sums",
    )(*lefts, *rights)


def columns_of(*values):
    stacked = jnp.stack(values, axis=1)
    return jnp.pad(stacked, ((0, 0), (0, 8 - len(values))))


def in_order(at_ref, source, target, piece, other=None):
    rows = source.shape[0]

    def step(p, carry):
        start = at_ref[p]
        at = pl.ds(pl.multiple_of(start % rows, piece), piece)
        values = source[at, :]
        if other is not None:
            values = jnp.where(start < rows, values, other[at, :])
        target[pl.ds(pl.multiple_of(p * piece, piece), piece), :] = values
        return carry

    lax.fori_loop(0, target.shape[0] // piece, step, 0)


def out_of_order(at_ref, source, target, piece):
    def step(p, carry):
        start = pl.multiple_of(at_ref[p], piece)
        target[pl.ds(start, piece), :] = source[pl.ds(pl.multiple_of(p * piece, piece), piece), :].astype(target.dtype)
        return carry

    lax.fori_loop(0, source.shape[0] // piece, step, 0)


def causal(tile):
    key_at = lax.broadcasted_iota(jnp.int32, (tile, tile), 0)
    query_at = lax.broadcasted_iota(jnp.int32, (tile, tile), 1)
    return query_at >= key_at


def attend_kernel(piece, tile, at_ref, own_ref, other_ref, out_ref, log_ref, query, key, value, value_t, mixed):
    for slot, held in enumerate((query, key, value)):
        in_order(at_ref, own_ref.at[slot], held, piece, other_ref.at[slot])
    value_t[...] = value[...].astype(F32).T.astype(BF)
    allowed = causal(tile)
    for i in range(query.shape[0] // tile):
        low, high = i * tile, (i + 1) * tile
        rows = query[low:high, :]
        near = jnp.where(allowed, dot_nt(key[low:high, :], rows) * HD ** (-0.5), -1e30)
        top = jnp.max(near, axis=0, keepdims=True)
        if i:
            far = dot_nt(key[0:low, :], rows) * HD ** (-0.5)
            top = jnp.maximum(top, jnp.max(far, axis=0, keepdims=True))
        near = jnp.exp(near - top)
        total = jnp.sum(near, axis=0, keepdims=True)
        summed = dot_nn(value_t[:, low:high], near.astype(BF))
        if i:
            far = jnp.exp(far - top)
            total = total + jnp.sum(far, axis=0, keepdims=True)
            summed = summed + dot_nn(value_t[:, 0:low], far.astype(BF))
        mixed[low:high, :] = (summed / total).T
        log_ref[0, :, low:high] = top + jnp.log(total)
    out_of_order(at_ref, mixed, out_ref, piece)


def attend(own, other, at, piece):
    half, width = own.shape[1:]
    rows = 2 * half
    heads = width // HD
    return pl.pallas_call(
        functools.partial(attend_kernel, piece, 256),
        grid_spec=pltpu.PrefetchScalarGridSpec(
            num_scalar_prefetch=1,
            grid=(heads,),
            in_specs=[pl.BlockSpec((3, half, HD), lambda h, at: (0, 0, h))] * 2,
            out_specs=[
                pl.BlockSpec((rows, HD), lambda h, at: (0, h)),
                pl.BlockSpec((1, 1, rows), lambda h, at: (h, 0, 0)),
            ],
            scratch_shapes=[pltpu.VMEM((rows, HD), BF)] * 3 + [pltpu.VMEM((HD, rows), BF), pltpu.VMEM((rows, HD), F32)],
        ),
        out_shape=[jax.ShapeDtypeStruct((rows, width), BF), jax.ShapeDtypeStruct((heads, 1, rows), F32)],
        compiler_params=pltpu.CompilerParams(vmem_limit_bytes=VMEM_LIMIT),
        cost_estimate=pl.CostEstimate(
            flops=2 * 2 * heads * rows * rows * HD, bytes_accessed=8 * rows * width, transcendentals=heads * rows * rows // 2
        ),
        name="attend",
    )(at, own, other)


def attend_back_kernel(
    piece, tile, at_ref, own_ref, other_ref, out_ref, grad_ref, log_ref, dqkv_ref, query, key, value, key_t, grad, mixed, dquery, dkey, dvalue
):
    for slot, held in enumerate((query, key, value)):
        in_order(at_ref, own_ref.at[slot], held, piece, other_ref.at[slot])
    in_order(at_ref, grad_ref, grad, piece)
    in_order(at_ref, out_ref, mixed, piece)
    key_t[...] = key[...].astype(F32).T.astype(BF)
    allowed = causal(tile)
    dkey[...] = jnp.zeros_like(dkey)
    dvalue[...] = jnp.zeros_like(dvalue)
    scale = HD ** (-0.5)
    for i in range(query.shape[0] // tile):
        low, high = i * tile, (i + 1) * tile
        rows = query[low:high, :]
        rows_grad = grad[low:high, :]
        log = log_ref[0, :, low:high]
        spread = jnp.sum((rows_grad.astype(F32) * mixed[low:high, :].astype(F32)).T, axis=0, keepdims=True)
        dquery_t = None
        for start, stop, masked in ((0, low, False), (low, high, True)):
            if start == stop:
                continue
            scores = dot_nt(key[start:stop, :], rows) * scale
            if masked:
                scores = jnp.where(allowed, scores, -1e30)
            probs = jnp.exp(scores - log)
            probs_grad = dot_nt(value[start:stop, :], rows_grad)
            scores_grad = (probs * (probs_grad - spread)).astype(BF)
            dvalue[start:stop, :] += dot_nn(probs.astype(BF), rows_grad)
            dkey[start:stop, :] += dot_nn(scores_grad, rows)
            term = dot_nn(key_t[:, start:stop], scores_grad)
            dquery_t = term if dquery_t is None else dquery_t + term
        dquery[low:high, :] = dquery_t.T * scale
    dkey[...] = dkey[...] * scale
    for slot, held in enumerate((dquery, dkey, dvalue)):
        out_of_order(at_ref, held, dqkv_ref.at[slot], piece)


def attend_back(own, other, out, grad, log, at, piece):
    half, width = own.shape[1:]
    rows = 2 * half
    heads = width // HD
    return pl.pallas_call(
        functools.partial(attend_back_kernel, piece, 256),
        grid_spec=pltpu.PrefetchScalarGridSpec(
            num_scalar_prefetch=1,
            grid=(heads,),
            in_specs=[
                pl.BlockSpec((3, half, HD), lambda h, at: (0, 0, h)),
                pl.BlockSpec((3, half, HD), lambda h, at: (0, 0, h)),
                pl.BlockSpec((rows, HD), lambda h, at: (0, h)),
                pl.BlockSpec((rows, HD), lambda h, at: (0, h)),
                pl.BlockSpec((1, 1, rows), lambda h, at: (h, 0, 0)),
            ],
            out_specs=pl.BlockSpec((3, rows, HD), lambda h, at: (0, 0, h)),
            scratch_shapes=[pltpu.VMEM((rows, HD), BF)] * 3
            + [pltpu.VMEM((HD, rows), BF)]
            + [pltpu.VMEM((rows, HD), BF)] * 2
            + [pltpu.VMEM((rows, HD), F32)] * 3,
        ),
        out_shape=jax.ShapeDtypeStruct((3, rows, width), BF),
        compiler_params=pltpu.CompilerParams(vmem_limit_bytes=VMEM_LIMIT),
        cost_estimate=pl.CostEstimate(
            flops=5 * heads * rows * rows * HD * 2, bytes_accessed=16 * rows * width, transcendentals=heads * rows * rows // 2
        ),
        name="attend_back",
    )(at, own, other, out, grad, log)


def local(
    tokens,
    block_order,
    query_weight,
    key_weight,
    value_weight,
    output_weight,
    gate_weight,
    up_weight,
    down_weight,
    query_gain,
    key_gain,
    attention_gain,
    forward_gain,
    cotangent,
):
    seqs, local_len, width = tokens.shape
    ranks = lax.axis_size("context")
    columns = lax.axis_size("tensor")
    full_len = local_len * ranks
    piece_len = full_len // block_order.shape[0]
    piece = local_len // columns
    shard_rows = seqs * piece
    count = shard_rows * columns
    context = lax.axis_index("context")
    t = lax.axis_index("tensor")
    s, core = context // 2, context % 2
    head_width = query_weight.shape[1]
    half_width = head_width // 2
    hidden_width = gate_weight.shape[1]

    def gather(values, axis):
        return lax.all_gather(values, "context", axis=axis, tiled=True)

    gain_columns = jnp.stack([attention_gain, forward_gain], axis=1)
    gain_columns = jnp.pad(gain_columns, ((0, 0), (0, HD - 2)))
    w_first = gather(jnp.concatenate([query_weight, key_weight, value_weight, output_weight.T, gain_columns], axis=1), 0)
    qkv_width = 3 * head_width
    gains = w_first[:, 4 * head_width :]
    gain_attn, gain_feed = gains[:, 0].astype(F32)[None], gains[:, 1].astype(F32)[None]
    w_gate_up = gather(jnp.concatenate([gate_weight, up_weight], axis=1), 0)
    query_scaling = query_gain.astype(F32)
    key_scaling = key_gain.astype(F32)

    chips = s ^ jnp.arange(seqs, dtype=jnp.int32)
    shards = t ^ jnp.arange(columns, dtype=jnp.int32)
    starts = (2 * chips[None, :] + core) * local_len + shards[:, None] * piece
    stored = (starts[:, :, None] + jnp.arange(piece, dtype=jnp.int32)).reshape(count)
    block = stored // piece_len
    slots = jnp.arange(block_order.shape[0], dtype=jnp.int32)
    place = jnp.sum(jnp.where(block[:, None] == slots[None, :], block_order[None, :], 0), axis=1) * piece_len
    place = place + stored % piece_len
    freq = THETA ** (-jnp.arange(0, HD, 2, dtype=F32) / HD)
    angle = place.astype(F32)[:, None] * freq[None, :]
    cosine = jnp.concatenate([jnp.cos(angle), jnp.cos(angle)], axis=-1)
    sine = jnp.concatenate([-jnp.sin(angle), jnp.sin(angle)], axis=-1)
    per_block = piece_len // piece
    pieces = jnp.arange(full_len // piece, dtype=jnp.int32)
    hits = block_order[None, :] == (pieces // per_block)[:, None]
    block_at = jnp.sum(jnp.where(hits, slots[None, :], 0), axis=1)
    piece_at = block_at * per_block + pieces % per_block
    rank_of, shard_of = piece_at // columns, piece_at % columns
    at = (((rank_of % 2) ^ core) * columns + (shard_of ^ t)) * seqs + ((rank_of // 2) ^ s)
    at = (at * piece).astype(jnp.int32)

    row_shard = to_sequences(tokens, s, t)
    rows = jnp.concatenate(gather_rows(row_shard), axis=0)
    qkv_raw = dot_nn(rows, w_first[:, :qkv_width])
    query_raw = qkv_raw[:, :head_width]
    key_raw = qkv_raw[:, head_width : 2 * head_width]
    totals = sum_over_tensor(jnp.stack([jnp.sum(query_raw * query_raw, axis=1), jnp.sum(key_raw * key_raw, axis=1)]))
    factors = lax.rsqrt(totals / width + EPS)
    scaling = jnp.stack([query_gain, key_gain]).astype(F32)
    keep, send = by_rows(
        turn_kernel,
        "turn",
        core,
        [(qkv_raw, 0), (columns_of(*factors), 0), (scaling, None), (cosine, 0), (sine, 0)],
        [((3, count, half_width), BF, 1)] * 2,
    )
    received = swap(send, "context", 1)
    mixed_heads, log = attend(keep, received, at, piece)

    def to_heads(values):
        keep = lax.dynamic_slice_in_dim(values, core * half_width, half_width, axis=1)
        send = lax.dynamic_slice_in_dim(values, (1 - core) * half_width, half_width, axis=1)
        return jnp.concatenate([keep, swap(send, "context", 1)], axis=0)

    def to_rows(values):
        own, other = values[:count], swap(values[count:], "context", 1)
        return jnp.concatenate([jnp.where(core == 0, own, other), jnp.where(core == 0, other, own)], axis=1)

    mixed_low = to_rows(mixed_heads)

    def chunk(values, k):
        return values[k * shard_rows : (k + 1) * shard_rows]

    order = list(range(columns))
    shard = (shard_rows, width)
    hidden_low, attended, hidden = exchange(
        "attended", 1, mixed_low, w_first, finish_attended, [row_shard, gain_attn], [(shard, F32), (shard, F32)], offset=qkv_width
    )

    fed_low, slopes, act_low, w_down, upstream, _, output_pieces, feed_gain_rows = feed(
        hidden_low, w_gate_up, down_weight.T, cotangent, hidden, gain_feed, seqs
    )

    own = width // ranks
    cores = [list(range(0, ranks, 2)), list(range(1, ranks, 2))]

    def scatter(values):
        return lax.psum_scatter(values, "context", scatter_dimension=0, axis_index_groups=cores, tiled=True)

    down_part = rank_sums(5, [(fed_low, act_low)], own)
    down_summed = scatter(down_part)
    gate_up_low = act_back(after(fed_low, down_part), w_down, slopes)
    output_rows = [output_pieces] + [swap(output_pieces, "tensor", k) for k in (order[1:3] if columns == 4 else order[1:])]
    gate_up_part = rank_sums(6, [(after(hidden_low, *output_rows), gate_up_low)], own)
    gate_up_summed = scatter(gate_up_part)
    if columns == 4:
        passed = [swap(output_rows[1][: seqs // 2], "tensor", 2), swap(output_rows[2][seqs // 2 :], "tensor", 1)]
        output_rows.append(jnp.concatenate(passed, axis=0))
    layer_output = in_place(jnp.stack(output_rows), s, t, BF)
    gate_up_low = after(gate_up_low, gate_up_part, layer_output)
    attended_low, hidden_grad, attn_gain_rows = exchange(
        "hidden_grad",
        3,
        gate_up_low,
        w_gate_up,
        finish_hidden_grad,
        [attended, upstream, gain_attn],
        [(shard, F32), ((8, width), F32)],
    )
    mixed_grad = dot_nn(attended_low, w_first[:, qkv_width : 4 * head_width]).astype(BF)
    dqkv = attend_back(keep, received, mixed_heads, to_heads(mixed_grad), log, at, piece)
    dqkv_other = swap(dqkv[:, count:], "context", 1)
    inner, head_gain_rows = by_rows(
        inner_kernel,
        "inner",
        core,
        [(dqkv, 1), (dqkv_other, 1), (qkv_raw, 0), (columns_of(*factors), 0), (scaling, None), (cosine, 0), (sine, 0)],
        [((2, 8, count), F32, 2), ((2, 8, head_width), F32, None)],
    )
    inner = sum_over_tensor(inner[:, 0])
    (qkv_low,) = by_rows(
        raw_grad_kernel,
        "raw_grad",
        core,
        [
            (dqkv, 1),
            (dqkv_other, 1),
            (qkv_raw, 0),
            (columns_of(*factors, *(inner * factors**3 / width)), 0),
            (scaling, None),
            (cosine, 0),
            (sine, 0),
        ],
        [((count, 3 * head_width), BF, 0)],
    )
    qkv_part = rank_sums(7, [(rows, qkv_low), (attended_low, mixed_low)], own)
    qkv_out_summed = scatter(after(qkv_part, gate_up_summed, down_summed))
    down_grad = down_summed.astype(F32).T
    every, width_gains, head_gains = exchange(
        "tokens_grad",
        4,
        after(qkv_low, qkv_part),
        w_first,
        None,
        [hidden_grad, attn_gain_rows, feed_gain_rows, head_gain_rows.reshape(16, head_width)],
        [((8, own), F32), ((8, head_width), F32)],
        chips=seqs,
        last=True,
    )
    tokens_grad = in_place(every.reshape(columns, seqs, piece, width), s, t, F32)

    gate_up_summed, qkv_out_summed = gate_up_summed.astype(F32), qkv_out_summed.astype(F32)
    return (
        layer_output,
        tokens_grad,
        qkv_out_summed[:, :head_width],
        qkv_out_summed[:, head_width : 2 * head_width],
        qkv_out_summed[:, 2 * head_width : 3 * head_width],
        qkv_out_summed[:, 3 * head_width :].T,
        gate_up_summed[:, :hidden_width],
        gate_up_summed[:, hidden_width:],
        down_grad,
        head_gains[0],
        head_gains[1],
        width_gains[0],
        width_gains[1],
    )


def solution(mesh):
    return jax.shard_map(
        local,
        mesh=mesh,
        in_specs=(
            P(None, "context", None),
            P(),
            P("context", "tensor"),
            P("context", "tensor"),
            P("context", "tensor"),
            P("tensor", "context"),
            P("context", "tensor"),
            P("context", "tensor"),
            P("tensor", "context"),
            P("tensor"),
            P("tensor"),
            P("context"),
            P("context"),
            P(None, "context", None),
        ),
        out_specs=(
            P(None, "context", None),
            P(None, "context", None),
            P("context", "tensor"),
            P("context", "tensor"),
            P("context", "tensor"),
            P("tensor", "context"),
            P("context", "tensor"),
            P("context", "tensor"),
            P("tensor", "context"),
            P("tensor"),
            P("tensor"),
            P("context"),
            P("context"),
        ),
        check_vma=False,
    )
```

```python
import functools

import jax
import jax.numpy as jnp
from jax import lax
from jax.experimental import pallas as pl
from jax.experimental.pallas import tpu as pltpu
from jax.sharding import PartitionSpec as P

HD = 128
EPS = 1e-06
THETA = 500000.0
BF = jnp.bfloat16
F32 = jnp.float32
VMEM_LIMIT = 60 * 1024 * 1024
MESH = pl.DeviceIdType.MESH


def dot_nn(left, right):
    return jnp.dot(left, right, preferred_element_type=F32)


def dot_nt(left, right):
    return lax.dot_general(left, right, (((1,), (1,)), ((), ())), preferred_element_type=F32)


def after(values, *others):
    return lax.optimization_barrier((values, *others))[0]


def swap(values, axis, mask):
    size = lax.axis_size(axis)
    return lax.ppermute(values, axis, [(i, i ^ mask) for i in range(size)])


def sum_over_tensor(values):
    size = lax.axis_size("tensor")
    chunks = values.reshape(values.shape[0], size, -1)
    total = chunks
    for m in range(1, size):
        other = swap(chunks, "tensor", m)
        total = total + jnp.stack([other[:, m ^ k] for k in range(size)], axis=1)
    return total.reshape(values.shape)


def place_kernel(at_ref, *refs):
    out_ref = refs[-1]
    for a in range(out_ref.shape[0]):
        at, base, values = a ^ at_ref[0], 0, None
        for ref in refs[:-1]:
            count = ref.shape[1]
            part = ref[0, jnp.clip(at - base, 0, count - 1)]
            values = part if values is None else jnp.where(at >= base, part, values)
            base += count
        out_ref[a, 0] = values.astype(out_ref.dtype)


def in_place(parts, s, t, dtype):
    size, _, piece, width = parts[0].shape
    seqs = sum(part.shape[1] for part in parts)
    full = pl.pallas_call(
        place_kernel,
        grid_spec=pltpu.PrefetchScalarGridSpec(
            num_scalar_prefetch=1,
            grid=(size,),
            in_specs=[pl.BlockSpec((1, *part.shape[1:]), lambda b, at: (b ^ at[1], 0, 0, 0)) for part in parts],
            out_specs=pl.BlockSpec((seqs, 1, piece, width), lambda b, at: (0, b, 0, 0)),
        ),
        out_shape=jax.ShapeDtypeStruct((seqs, size, piece, width), dtype),
        name="place_rows",
    )(jnp.stack([s, t]).astype(jnp.int32), *parts)
    return full.reshape(seqs, size * piece, width)


def norm_factor(values):
    return lax.rsqrt(jnp.mean(values * values, axis=-1, keepdims=True) + EPS)


def norm_back(values, factor, gain, grad):
    scaled = grad * gain
    inner = jnp.mean(values * scaled, axis=-1, keepdims=True)
    return factor * scaled - values * (factor**3 * inner), grad * values * factor


def flip(index, mask):
    bit = 1
    result = index
    while bit <= mask:
        if mask & bit:
            result = result + bit - 2 * bit * ((index // bit) % 2)
        bit *= 2
    return result


def exchange_kernel(size, width, depth, offset, tile, finish, chips, last, n_in, n_out, a_ref, w_ref, *refs):
    ins, rest = refs[:n_in], refs[n_in:]
    every, outs, rest = rest[0], rest[1 : 1 + n_out], rest[1 + n_out :]
    a_buf, w_buf, sent, got, total, mine, a_sem, w_sem, sent_sem, got_sem, out_sem, in_sem, own_sem = rest[:13]
    t = lax.axis_index("tensor")
    c = lax.axis_index("context")
    rows = total.shape[0]
    half = rows // 2

    def a_copy(k):
        at = pl.ds(k * rows, rows)
        return pltpu.make_async_copy(a_ref.at[at, :], a_buf.at[at, :], a_sem.at[k])

    def w_copy(j):
        at = pl.ds(pl.multiple_of(j * tile, tile), tile)
        return pltpu.make_async_copy(w_ref.at[at, pl.ds(offset, depth)], w_buf.at[at, :], w_sem.at[j])

    order = [3, 1, 2, 0] if size == 4 else [*range(1, size), 0]
    tiles = width // tile
    parts = tiles if size == 4 else 1
    across = width // parts
    a_copy(order[0]).start()
    for j in range(tiles):
        w_copy(j).start()
    for k in order[1:]:
        a_copy(k).start()
    barrier = pltpu.get_barrier_semaphore()
    for k in range(1, size):
        pl.semaphore_signal(barrier, inc=1, device_id={"tensor": flip(t, k)}, device_id_type=MESH)

    met = range(1, 2 * chips) if last else range(2, 2 * chips, 2)
    for mask in met:
        pl.semaphore_signal(barrier, inc=1, device_id={"context": flip(c, mask)}, device_id_type=MESH)
    for out in outs:
        if out.shape[0] == 8:
            out[...] = jnp.zeros_like(out)

    def cross(j, source, target, sems, base=0):
        if j == 0:
            return pltpu.make_async_copy(source, target, sems[0].at[base])
        return pltpu.make_async_remote_copy(
            src_ref=source,
            dst_ref=target,
            send_sem=sems[0].at[base + j],
            recv_sem=sems[1].at[base + j],
            device_id={"context": flip(c, 2 * j)},
            device_id_type=MESH,
        )

    def send(slot, source, target, partner, sems):
        return pltpu.make_async_remote_copy(
            src_ref=source,
            dst_ref=target,
            send_sem=sems[0].at[slot],
            recv_sem=sems[1].at[slot],
            device_id={"tensor": flip(t, partner)},
            device_id_type=MESH,
        )

    def product(k, first=False, part=0):
        if part == 0:
            a_copy(k).wait()

        def step(j, carry):
            if first:
                w_copy(j).wait()
            at = pl.ds(pl.multiple_of(j * tile, tile), tile)
            value = dot_nt(a_buf[k * rows : (k + 1) * rows, :], w_buf[at, :])
            if k:
                sent[k - 1, :, at] = value.astype(BF)
            else:
                total[:, at] = value
            return carry

        lax.fori_loop(part * tiles // parts, (part + 1) * tiles // parts, step, 0)

    def add(slot, other, first, columns):
        def step(i, carry):
            at = pl.ds(pl.multiple_of(first + i * 16, 16), 16)
            sent[slot, at, columns] = (sent[slot, at, columns].astype(F32) + got[other, at, columns].astype(F32)).astype(BF)
            return carry

        lax.fori_loop(0, half // 16, step, 0)

    def columns_of_part(part):
        return pl.ds(part * across, across)

    low, high = pl.ds(0, half), pl.ds(half, half)
    sums = (sent_sem, got_sem)
    product(order[0], first=True)
    pl.semaphore_wait(barrier, size - 1 + len(met))
    piece = rows // max(1, chips)
    crossing = []
    small = []
    if last:
        gain_rows, head_rows, gain_got, head_got, own_got, small_sent, small_got = rest[18:]
        attn_rows, feed_rows, two_heads = ins[1:]
        gain_rows[...] = jnp.zeros_like(gain_rows)
        head_rows[...] = jnp.zeros_like(head_rows)
        for i, part in enumerate((attn_rows, feed_rows)):
            gain_rows[i : i + 1, :] = jnp.sum(part[...], axis=0, keepdims=True)
            head_rows[i : i + 1, :] = jnp.sum(two_heads[8 * i : 8 * i + 8, :], axis=0, keepdims=True)
        own_width = outs[0].shape[1]

        def tell(source, target, device):
            copy = pltpu.make_async_remote_copy(
                src_ref=source,
                dst_ref=target,
                send_sem=small_sent.at[len(small)],
                recv_sem=small_got.at[len(small)],
                device_id=device,
                device_id_type=MESH,
            )
            copy.start()
            small.append(copy)

        for k in range(1, size):
            tell(gain_rows, gain_got.at[k - 1], {"tensor": flip(t, k)})
        for mask in met:
            tell(head_rows, head_got.at[mask - 1], {"context": flip(c, mask)})
    if chips and not last:
        source, target = ins[0], outs[0]
        for j in range(chips):
            crossing.append(
                cross(
                    j,
                    source.at[flip(c // 2, j), pl.ds(pl.multiple_of(t * piece, piece), piece), :],
                    target.at[pl.ds(j * piece, piece), :],
                    rest[13:15],
                )
            )
            crossing[-1].start()

    def home(part):
        at = columns_of_part(part)
        return [
            cross(j, mine.at[pl.ds(j * piece, piece), at], rest[17].at[pl.ds(j * piece, piece), at], rest[15:17], part * chips)
            for j in range(chips)
        ]

    def finish_last(part, group):
        at = columns_of_part(part)
        for copy in group[2:] if size == 4 else group:
            copy.wait_recv()

        def step(i, carry):
            row = pl.ds(pl.multiple_of(i * 16, 16), 16)
            summed = ins[0][row, at] + total[row, at]
            for other in range(2 if size == 4 else size - 1):
                summed = summed + got[other, row, at].astype(F32)
            mine[row, at] = summed.astype(BF)
            return carry

        lax.fori_loop(0, rows // 16, step, 0)
        for copy in home(part):
            copy.start()

    def sums_of(part):
        at = columns_of_part(part)
        return [
            send(6 * part + 0, sent.at[2, low, at], got.at[2, low, at], 1, sums),
            send(6 * part + 1, sent.at[2, high, at], got.at[2, high, at], 2, sums),
            send(6 * part + 2, sent.at[0, low, at], got.at[0, low, at], 1, sums),
            send(6 * part + 3, sent.at[1, high, at], got.at[1, high, at], 2, sums),
            send(6 * part + 4, sent.at[1, low, at], got.at[1, low, at], 2, sums),
            send(6 * part + 5, sent.at[0, high, at], got.at[0, high, at], 1, sums),
        ]

    if size == 4:
        groups = [sums_of(part) for part in range(parts)]
        copies = sum(groups, [])
        for part, group in enumerate(groups):
            for k, ready in ((3, group[:2]), (1, group[2:3]), (2, group[3:4])):
                if k != 3 or part:
                    product(k, first=k == 3, part=part)
                for copy in [] if last and part else ready:
                    copy.start()
        for part, group in enumerate(groups):
            at = columns_of_part(part)
            group[0].wait_recv()
            add(1, 2, 0, at)
            group[4].start()
            group[1].wait_recv()
            add(0, 2, half, at)
            group[5].start()
            for copy in groups[part + 1][:4] if last and part + 1 < parts else []:
                copy.start()
            product(0, part=part)
            if last and part + 1 < parts:
                finish_last(part, group)
        for group in [] if last else groups:
            for copy in group[2:]:
                copy.wait_recv()
        used = 2
    else:
        copies = [send(k - 1, sent.at[k - 1], got.at[k - 1], k, sums) for k in range(1, size)]
        copies[0].start()
        for k in range(2, size):
            product(k)
            copies[k - 1].start()
        product(0)
        groups = [copies]
        if not last:
            for copy in copies:
                copy.wait_recv()
        used = size - 1
    if last:
        finish_last(parts - 1, groups[-1])
    if chips and not last:
        crossing[0].wait()
        for copy in crossing[1:]:
            copy.wait_recv()

    def finish_rows(first, count, part=0):
        def step(i, carry):
            at = pl.ds(pl.multiple_of(first + i * 16, 16), 16)
            summed = total[at, :]
            for other in range(used):
                summed = summed + got[other, at, :].astype(F32)
            mine[at, :] = finish(at, summed, ins, outs).astype(BF)
            return carry

        lax.fori_loop(0, count // 16, step, 0)

    gather = (out_sem, in_sem)
    shared = rest[17] if last else mine
    own = pltpu.make_async_copy(shared, every.at[pl.ds(0, rows), :], own_sem)
    if last:
        going_home = [home(part) for part in range(parts)]
    else:
        going_home = [[cross(j, outs[1].at[pl.ds(j * piece, piece), :], outs[2].at[j], rest[15:17]) for j in range(chips)]]
    if last:
        for copy in small:
            copy.wait()
        for k in range(1, size):
            gain_rows[...] += gain_got[k - 1]
        outs[1][...] = head_rows[...]
        for mask in met:
            outs[1][...] += head_got[mask - 1]
        for mask in met:
            at = pl.ds(pl.multiple_of(flip(c, mask) * own_width, own_width), own_width)
            tell(gain_rows.at[:, at], own_got.at[mask - 1], {"context": flip(c, mask)})

    def came_home(first, count, part=0):
        for j in range(first // piece, (first + count) // piece):
            if j == 0:
                going_home[part][j].wait()
            else:
                going_home[part][j].wait_recv()

    out_parts = parts if last else 1
    make_ready = came_home if last else finish_rows
    then = [own] if last else [own, *going_home[0]]
    if size == 4:

        def out_columns(part):
            return pl.ds(part * (width // out_parts), width // out_parts)

        def chunk(k, side, part):
            return every.at[pl.ds(k * rows + side * half, half), out_columns(part)]

        def share(k, side, part):
            source = shared.at[pl.ds(side * half, half), out_columns(part)]
            return send(6 * part + 2 * k + side, source, chunk(k + 1, side, part), k + 1, gather)

        groups = []
        for part in range(out_parts):
            shares = [share(k, side, part) for k in (0, 1) for side in (0, 1)]
            passed = [
                send(6 * part + 4, chunk(1, 0, part), chunk(3, 0, part), 2, gather),
                send(6 * part + 5, chunk(2, 1, part), chunk(3, 1, part), 1, gather),
            ]
            groups.append(shares + passed)
        for part, group in enumerate(groups):
            make_ready(0, half, part)
            group[0].start()
            group[2].start()
            make_ready(half, half, part)
            group[3].start()
            group[1].start()
            if part == out_parts - 1:
                for copy in then:
                    copy.start()
            group[0].wait_recv()
            group[4].start()
            group[3].wait_recv()
            group[5].start()
        for group in groups:
            for at in (1, 2, 4, 5):
                group[at].wait_recv()
        shares = sum(groups, [])
    else:
        make_ready(0, rows)
        shares = [send(k - 1, shared, every.at[pl.ds(k * rows, rows), :], k, gather) for k in range(1, size)]
        for copy in [*shares, *then]:
            copy.start()
        for copy in shares:
            copy.wait_recv()
    own.wait()
    if chips and not last:
        came_home(0, rows)
    if last:
        for copy in small[size - 1 + len(met) :]:
            copy.wait()
        outs[0][...] = gain_rows[:, pl.ds(pl.multiple_of(c * own_width, own_width), own_width)]
        for mask in met:
            outs[0][...] += own_got[mask - 1]
    for copy in copies + shares + crossing[1:] + sum([group[1:] for group in going_home], []):
        copy.wait_send()


def exchange(name, number, a, w, finish, ins, outs, offset=0, chips=0, last=False):
    size = lax.axis_size("tensor")
    rows, width, depth = a.shape[0] // size, w.shape[0], a.shape[1]
    tile = min(512, width)
    parts = width // tile if size == 4 else 1
    links = 6 * parts if size == 4 else size - 1
    whole = pl.BlockSpec(memory_space=pltpu.VMEM)
    anywhere = pl.BlockSpec(memory_space=pl.ANY)
    dma = pltpu.SemaphoreType.DMA
    gain_scratch = []
    if last:
        own, head_width = outs[0][0][1], outs[1][0][1]
        ranks = 2 * chips
        gain_scratch = [
            pltpu.VMEM((rows, width), BF),
            pltpu.VMEM((8, width), F32),
            pltpu.VMEM((8, head_width), F32),
            pltpu.VMEM((size - 1, 8, width), F32),
            pltpu.VMEM((ranks - 1, 8, head_width), F32),
            pltpu.VMEM((ranks - 1, 8, own), F32),
            dma((size - 1 + 2 * (ranks - 1),)),
            dma((size - 1 + 2 * (ranks - 1),)),
        ]
    return pl.pallas_call(
        functools.partial(exchange_kernel, size, width, depth, offset, tile, finish, chips, last, len(ins), len(outs)),
        in_specs=[anywhere, anywhere] + [anywhere if chips and not last and i == 0 else whole for i in range(len(ins))],
        out_specs=[anywhere] + [whole] * len(outs),
        out_shape=[jax.ShapeDtypeStruct((size * rows, width), BF)] + [jax.ShapeDtypeStruct(*out) for out in outs],
        scratch_shapes=[
            pltpu.VMEM((size * rows, depth), BF),
            pltpu.VMEM((width, depth), BF),
            pltpu.VMEM((size - 1, rows, width), BF),
            pltpu.VMEM((size - 1, rows, width), BF),
            pltpu.VMEM((rows, width), F32),
            pltpu.VMEM((rows, width), BF),
            dma((size,)),
            dma((width // tile,)),
            dma((links,)),
            dma((links,)),
            dma((links,)),
            dma((links,)),
            dma,
        ]
        + [dma((chips * parts,))] * (4 if chips else 0)
        + gain_scratch,
        compiler_params=pltpu.CompilerParams(vmem_limit_bytes=VMEM_LIMIT, collective_id=number, has_side_effects=True),
        cost_estimate=pl.CostEstimate(flops=2 * size * rows * width * depth, bytes_accessed=240_000_000, transcendentals=0),
        name=name,
    )(a, w, *ins)


def add_rows(ref, values):
    ref[...] += values[:8] + values[8:]


def finish_attended(at, attended, ins, outs):
    tokens, gain = ins
    outs[0][at, :] = attended
    hidden = tokens[at, :].astype(F32) + attended * norm_factor(attended) * gain[...]
    outs[1][at, :] = hidden
    return hidden


def finish_hidden_grad(at, summed, ins, outs):
    attended, cotangent, gain = ins
    hidden_grad = cotangent[at, :].astype(F32) + summed
    outs[0][at, :] = hidden_grad
    values = attended[at, :]
    grad, gain_rows = norm_back(values, norm_factor(values), gain[...], hidden_grad)
    add_rows(outs[1], gain_rows)
    return grad


def remote(source, target, sems, slot, device):
    return pltpu.make_async_remote_copy(
        src_ref=source,
        dst_ref=target,
        send_sem=sems[0].at[slot],
        recv_sem=sems[1].at[slot],
        device_id=device,
        device_id_type=MESH,
    )


def meet(t, c, size, masks):
    barrier = pltpu.get_barrier_semaphore()
    for k in range(1, size):
        pl.semaphore_signal(barrier, inc=1, device_id={"tensor": flip(t, k)}, device_id_type=MESH)
    for mask in masks:
        pl.semaphore_signal(barrier, inc=1, device_id={"context": flip(c, mask)}, device_id_type=MESH)
    return lambda: pl.semaphore_wait(barrier, size - 1 + len(masks))


class Line:
    def __init__(self, chips, own, buf, up_sems, down_sems, core_sems):
        self.chips, self.own, self.buf = chips, own, buf
        self.sems, self.core_sems = {1: up_sems, -1: down_sems}, core_sems
        self.c = lax.axis_index("context")
        self.s, self.core = self.c // 2, self.c % 2

    def rows(self, chip):
        return pl.ds(pl.multiple_of((2 * chip + self.core) * self.own, self.own), self.own)

    def hop(self, k, way, chip):
        part = self.buf.at[self.rows(chip), :]
        return remote(part, part, self.sems[way], k, {"context": self.c + 2 * way})

    def cross(self, k, way, chip):
        part = self.buf.at[self.rows(chip), :]
        return remote(part, part, self.core_sems, 0 if k < 0 else 1 + 2 * k + (way < 0), {"context": flip(self.c, 1)})

    def sends(self, k, way):
        if way > 0:
            return (self.s >= k) & (self.s < self.chips - 1)
        return (self.s + k < self.chips) & (self.s > 0)

    def gets(self, k, way):
        return self.s >= k + 1 if way > 0 else self.s + k + 1 < self.chips

    def each(self, test, k, act):
        for way in (1, -1):
            pl.when(test(k, way))(functools.partial(act, k, way))

    def start(self, k):
        self.each(self.sends, k, lambda k, way: self.hop(k, way, self.s - way * k).start())

    def begin(self):
        self.start(0)
        self.cross(-1, 1, self.s).start()

    def advance(self, k):
        def got(k, way):
            chip = self.s - way * (k + 1)
            self.hop(k, way, chip).wait_recv()
            self.cross(k, way, chip).start()

        self.each(self.gets, k, got)
        if k + 1 < self.chips - 1:
            self.start(k + 1)

    def other_core(self, k):
        if k < 0:
            self.cross(-1, 1, self.s).wait_recv()
        else:
            self.each(self.gets, k, lambda k, way: self.cross(k, way, self.s - way * (k + 1)).wait_recv())

    def end(self):
        self.cross(-1, 1, self.s).wait_send()
        for k in range(self.chips - 1):
            self.each(self.sends, k, lambda k, way: self.hop(k, way, self.s - way * k).wait_send())
            self.each(self.gets, k, lambda k, way: self.cross(k, way, self.s - way * (k + 1)).wait_send())


def line_sems(chips):
    dma = pltpu.SemaphoreType.DMA
    return [dma((chips - 1,))] * 4 + [dma((2 * chips - 1,))] * 2


class Sums:
    def __init__(self, size, t, sent, got, columns, sems, base):
        rows = sent.shape[1]
        low, high = pl.ds(0, rows // 2), pl.ds(rows // 2, rows // 2)
        self.size, self.sent, self.got, self.columns, self.half = size, sent, got, columns, rows // 2

        def send(slot, of, to, at, partner):
            return remote(sent.at[of, at, columns], got.at[to, at, columns], sems, base + slot, {"tensor": flip(t, partner)})

        if size == 4:
            self.copies = [
                send(0, 2, 2, low, 1),
                send(1, 2, 2, high, 2),
                send(2, 0, 0, low, 1),
                send(3, 1, 1, high, 2),
                send(4, 1, 1, low, 2),
                send(5, 0, 0, high, 1),
            ]
            self.after_product = {3: self.copies[:2], 1: self.copies[2:3], 2: self.copies[3:4]}
        else:
            self.copies = [send(k - 1, k - 1, k - 1, pl.ds(0, rows), k) for k in range(1, size)]
            self.after_product = {k: self.copies[k - 1 : k] for k in range(1, size)}

    def pass_on(self):
        if self.size != 4:
            return
        for copy, slot, first, then in ((0, 1, 0, 4), (1, 0, self.half, 5)):
            self.copies[copy].wait_recv()

            def step(i, carry):
                at = pl.ds(pl.multiple_of(first + i * 16, 16), 16)
                summed = self.sent[slot, at, self.columns].astype(F32) + self.got[2, at, self.columns].astype(F32)
                self.sent[slot, at, self.columns] = summed.astype(BF)
                return carry

            lax.fori_loop(0, self.half // 16, step, 0)
            self.copies[then].start()

    def wait(self):
        for copy in self.copies[2:] if self.size == 4 else self.copies:
            copy.wait_recv()


class Gather:
    def __init__(self, size, t, shared, every, sems, own_sem):
        rows = every.shape[0] // size
        half = rows // 2
        self.size = size
        self.own = pltpu.make_async_copy(shared, every.at[pl.ds(0, rows), :], own_sem)

        def chunk(k, side):
            return every.at[pl.ds(k * rows + side * half, half), :]

        def send(slot, source, target, partner):
            return remote(source, target, sems, slot, {"tensor": flip(t, partner)})

        if size == 4:
            self.copies = [send(2 * k + side, shared.at[pl.ds(side * half, half), :], chunk(k + 1, side), k + 1) for k in (0, 1) for side in (0, 1)]
            self.copies += [send(4, chunk(1, 0), chunk(3, 0), 2), send(5, chunk(2, 1), chunk(3, 1), 1)]
            self.ready = (self.copies[0:3:2], self.copies[3:0:-2])
        else:
            self.copies = [send(k - 1, shared, every.at[pl.ds(k * rows, rows), :], k) for k in range(1, size)]
            self.ready = ((), self.copies)

    def start(self, side):
        for copy in self.ready[side]:
            copy.start()
        if side:
            self.own.start()

    def pass_on(self):
        if self.size == 4:
            self.copies[0].wait_recv()
            self.copies[4].start()
            self.copies[3].wait_recv()
            self.copies[5].start()

    def wait(self):
        for at, copy in enumerate(self.copies):
            if self.size != 4 or at not in (0, 3):
                copy.wait_recv()
        self.own.wait()

    def end(self):
        for copy in self.copies:
            copy.wait_send()


def links_of(size):
    return 6 if size == 4 else size - 1


def start_kernel(size, chips, offsets, n_pair, *refs):
    tokens_ref, firsts, pair, refs = refs[0], refs[1 : 1 + len(offsets)], refs[1 + len(offsets) :][:n_pair], refs[1 + len(offsets) + n_pair :]
    every, whole, both, shard = refs[:4]
    line_refs, gather, coming, own_sem, keep_sem = refs[4:10], refs[10:12], refs[12:14], refs[14], refs[15]
    t, c = lax.axis_index("tensor"), lax.axis_index("context")
    s = c // 2
    rows = shard.shape[0]
    piece = rows // chips
    own = firsts[0].shape[0]
    line = Line(chips, own, whole, line_refs[0:2], line_refs[2:4], line_refs[4:6])
    wait_others = meet(t, c, size, [1, *range(2, 2 * chips, 2)])
    kept = [
        pltpu.make_async_copy(first, whole.at[line.rows(s), pl.ds(offset, first.shape[1])], keep_sem.at[i])
        for i, (first, offset) in enumerate(zip(firsts, offsets))
    ]
    across = pair[0].shape[1]
    kept += [
        pltpu.make_async_copy(part, both.at[:, pl.ds(i * across, across)], keep_sem.at[len(offsets) + i]) for i, part in enumerate(pair)
    ]
    for copy in kept:
        copy.start()
    arrivals = [
        (tokens_ref.at[flip(s, j), pl.ds(pl.multiple_of(t * piece, piece), piece), :], shard.at[pl.ds(j * piece, piece), :])
        for j in range(chips)
    ]
    first = pltpu.make_async_copy(*arrivals[0], coming[0].at[0])
    others = [remote(*arrivals[j], coming, j, {"context": flip(c, 2 * j)}) for j in range(1, chips)]
    wait_others()
    for copy in [first, *others]:
        copy.start()
    for copy in kept:
        copy.wait()
    line.begin()
    first.wait()
    for copy in others:
        copy.wait_recv()
    share = Gather(size, t, shard, every, gather, own_sem)
    share.start(0)
    share.start(1)
    line.advance(0)
    share.pass_on()
    for k in range(1, chips - 1):
        line.advance(k)
    share.wait()
    for k in range(-1, chips - 1):
        line.other_core(k)
    line.end()
    share.end()
    for copy in others:
        copy.wait_send()


def start(tokens, firsts, pair, chips):
    size = lax.axis_size("tensor")
    seqs, local_len, width = tokens.shape
    rows = seqs * local_len // size
    own = firsts[0].shape[0]
    offsets, across = [], 0
    for first in firsts:
        offsets.append(across)
        across += first.shape[1]
    dma = pltpu.SemaphoreType.DMA
    anywhere = pl.BlockSpec(memory_space=pl.ANY)
    shape = jax.ShapeDtypeStruct
    return pl.pallas_call(
        functools.partial(start_kernel, size, chips, offsets, len(pair)),
        in_specs=[anywhere] * (1 + len(firsts) + len(pair)),
        out_specs=[anywhere] + [pl.BlockSpec(memory_space=pltpu.VMEM)] * 3,
        out_shape=[
            shape((size * rows, width), BF),
            shape((2 * chips * own, across), BF),
            shape((own, sum(part.shape[1] for part in pair)), BF),
            shape((rows, width), BF),
        ],
        scratch_shapes=line_sems(chips)
        + [dma((links_of(size),))] * 2
        + [dma((chips,))] * 2
        + [dma, dma((len(firsts) + len(pair),))],
        compiler_params=pltpu.CompilerParams(vmem_limit_bytes=VMEM_LIMIT, collective_id=8, has_side_effects=True),
        cost_estimate=pl.CostEstimate(flops=0, bytes_accessed=300_000_000, transcendentals=0),
        name="start",
    )(tokens, *firsts, *pair)


def feed_kernel(size, chips, tile, *refs):
    h_ref, gate_up_w_ref, down_ref, cotangent_ref, residual_ref, gain_ref = refs[:6]
    every, slopes_ref, act_ref, down_all_ref, upstream, output, pieces, gain_rows = refs[6:14]
    h_buf, w_buf, act, down, sent, got, total, mine, stage = refs[14:23]
    h_sem, w_sem, stage_sem, keep_sem, own_sem = refs[23:28]
    line_refs, sums, gather, coming, going = refs[28:34], refs[34:36], refs[36:38], refs[38:40], refs[40:42]
    t, c = lax.axis_index("tensor"), lax.axis_index("context")
    s = c // 2
    rows, width = total.shape
    hidden = act.shape[1]
    own = down_ref.shape[0]
    piece = rows // chips
    tiles = hidden // tile
    order = [3, 1, 2, 0] if size == 4 else [*range(1, size), 0]
    line = Line(chips, own, down, line_refs[0:2], line_refs[2:4], line_refs[4:6])

    def h_copy(k):
        at = pl.ds(k * rows, rows)
        return pltpu.make_async_copy(h_ref.at[at, :], h_buf.at[at, :], h_sem.at[k])

    def w_copy(j, i):
        at = pl.ds(pl.multiple_of(i * hidden + j * tile, tile), tile)
        return pltpu.make_async_copy(gate_up_w_ref.at[:, at], w_buf.at[:, at], w_sem.at[j, i])

    own_rows = line.rows(s)
    own_down = pltpu.make_async_copy(down_ref, down.at[own_rows, :], keep_sem.at[0])
    own_down.start()
    wait_others = meet(t, c, size, [1, *range(2, 2 * chips, 2)])
    h_copy(order[0]).start()
    for j in range(tiles):
        for i in range(2):
            w_copy(j, i).start()
    for k in order[1:]:
        h_copy(k).start()
    gain_rows[...] = jnp.zeros_like(gain_rows)
    own_down.wait()
    wait_others()
    line.begin()

    def stage_copy(slot, i, k, j):
        at = pl.ds(pl.multiple_of(i * hidden + j * tile, tile), tile)
        return pltpu.make_async_copy(stage.at[slot, i], slopes_ref.at[pl.ds(k * rows, rows), at], stage_sem.at[slot, i])

    for n, k in enumerate(order):
        h_copy(k).wait()
        chunk = pl.ds(k * rows, rows)

        def step(j, carry):
            slot = (n * tiles + j) % 2
            if n == 0:
                for i in range(2):
                    w_copy(j, i).wait()

            @pl.when(n * tiles + j >= 2)
            def _():
                for i in range(2):
                    stage_copy(slot, i, k, j).wait()

            gate, up = [
                dot_nn(h_buf[chunk, :], w_buf[:, pl.ds(pl.multiple_of(i * hidden + j * tile, tile), tile)]) for i in range(2)
            ]
            logistic = jax.nn.sigmoid(gate)
            silu = gate * logistic
            act[chunk, pl.ds(pl.multiple_of(j * tile, tile), tile)] = (silu * up).astype(BF)
            stage[slot, 0] = (up * (logistic + silu * (1.0 - logistic))).astype(BF)
            stage[slot, 1] = silu.astype(BF)
            for i in range(2):
                stage_copy(slot, i, k, j).start()
            return carry

        lax.fori_loop(0, tiles, step, 0)
    for slot in range(2):
        for i in range(2):
            stage_copy(slot, i, 0, 0).wait()
    act_out = pltpu.make_async_copy(act, act_ref, keep_sem.at[1])
    act_out.start()

    rounds = []

    def fed_round(i):
        at = pl.ds(pl.multiple_of(flip(s, i) * 2 * own, 2 * own), 2 * own)
        group = Sums(size, t, sent, got, at, sums, links_of(size) * i)
        for k in order:
            value = dot_nt(act[k * rows : (k + 1) * rows, :], down[at, :])
            if k:
                sent[k - 1, :, at] = value.astype(BF)
                for copy in group.after_product[k]:
                    copy.start()
            else:
                total[:, at] = value
        rounds.append(group)

    line.advance(0)
    line.other_core(-1)
    fed_round(0)
    line.other_core(0)
    fed_round(1)
    rounds[0].pass_on()
    rounds[1].pass_on()
    for k in range(1, chips - 1):
        line.advance(k)
        line.other_core(k)
        fed_round(k + 1)
        if k + 1 == chips - 1:
            arrivals = [
                (cotangent_ref.at[flip(s, j), pl.ds(pl.multiple_of(t * piece, piece), piece), :], upstream.at[pl.ds(j * piece, piece), :])
                for j in range(chips)
            ]
            first = pltpu.make_async_copy(*arrivals[0], coming[0].at[0])
            others = [remote(*arrivals[j], coming, j, {"context": flip(c, 2 * j)}) for j in range(1, chips)]
            for copy in [first, *others]:
                copy.start()
        rounds[k + 1].pass_on()
    down_out = pltpu.make_async_copy(down, down_all_ref, keep_sem.at[2])
    down_out.start()
    for group in rounds:
        group.wait()
    first.wait()
    for copy in others:
        copy.wait_recv()

    used = 2 if size == 4 else size - 1

    def finish_rows(side):
        def step(i, carry):
            at = pl.ds(pl.multiple_of(side * (rows // 2) + i * 16, 16), 16)
            fed = total[at, :]
            for other in range(used):
                fed = fed + got[other, at, :].astype(F32)
            factor = norm_factor(fed)
            output[at, :] = (residual_ref[at, :] + fed * factor * gain_ref[...]).astype(BF)
            grad, gains = norm_back(fed, factor, gain_ref[...], upstream[at, :].astype(F32))
            gain_rows[...] += gains[:8] + gains[8:]
            mine[at, :] = grad.astype(BF)
            return carry

        lax.fori_loop(0, rows // 32, step, 0)

    share = Gather(size, t, mine, every, gather, own_sem)
    finish_rows(0)
    share.start(0)
    finish_rows(1)
    share.start(1)
    kept = pltpu.make_async_copy(output.at[pl.ds(0, piece), :], pieces.at[0], going[0].at[0])
    gone = [
        remote(output.at[pl.ds(j * piece, piece), :], pieces.at[j], going, j, {"context": flip(c, 2 * j)})
        for j in range(1, chips)
    ]
    for copy in [kept, *gone]:
        copy.start()
    share.pass_on()
    share.wait()
    kept.wait()
    for copy in gone:
        copy.wait_recv()
    act_out.wait()
    down_out.wait()
    line.end()
    share.end()
    for copy in [*sum([group.copies for group in rounds], []), *others, *gone]:
        copy.wait_send()


def feed(hidden_low, gate_up_weight, down_shard, cotangent, residual, gain, chips):
    size = lax.axis_size("tensor")
    count, width = hidden_low.shape
    rows = count // size
    own, hidden = down_shard.shape
    ranks = 2 * chips
    tile = min(512, hidden)
    links = links_of(size)
    dma = pltpu.SemaphoreType.DMA
    anywhere, whole = pl.BlockSpec(memory_space=pl.ANY), pl.BlockSpec(memory_space=pltpu.VMEM)
    shape = jax.ShapeDtypeStruct
    return pl.pallas_call(
        functools.partial(feed_kernel, size, chips, tile),
        in_specs=[anywhere] * 4 + [whole] * 2,
        out_specs=[anywhere] * 4 + [whole] * 4,
        out_shape=[
            shape((count, width), BF),
            shape((count, 2 * hidden), BF),
            shape((count, hidden), BF),
            shape((ranks * own, hidden), BF),
            shape((rows, width), BF),
            shape((rows, width), BF),
            shape((chips, rows // chips, width), BF),
            shape((8, width), F32),
        ],
        scratch_shapes=[
            pltpu.VMEM((count, width), BF),
            pltpu.VMEM((width, 2 * hidden), BF),
            pltpu.VMEM((count, hidden), BF),
            pltpu.VMEM((ranks * own, hidden), BF),
            pltpu.VMEM((size - 1, rows, width), BF),
            pltpu.VMEM((size - 1, rows, width), BF),
            pltpu.VMEM((rows, width), F32),
            pltpu.VMEM((rows, width), BF),
            pltpu.VMEM((2, 2, rows, tile), BF),
            dma((size,)),
            dma((hidden // tile, 2)),
            dma((2, 2)),
            dma((3,)),
            dma,
        ]
        + line_sems(chips)
        + [dma((links * chips,))] * 2
        + [dma((links,))] * 2
        + [dma((chips,))] * 4,
        compiler_params=pltpu.CompilerParams(vmem_limit_bytes=VMEM_LIMIT, collective_id=2, has_side_effects=True),
        cost_estimate=pl.CostEstimate(flops=6 * count * width * hidden, bytes_accessed=400_000_000, transcendentals=count * hidden),
        name="feed",
    )(hidden_low, gate_up_weight, down_shard, cotangent, residual, gain)


def turn(values, cosine, sine):
    heads = [values[:, i : i + HD] for i in range(0, values.shape[1], HD)]
    return jnp.concatenate([head * cosine + pltpu.roll(head, HD // 2, 1) * sine for head in heads], axis=1)


def turn_kernel(core_ref, raw_ref, column_ref, gain_ref, cosine_ref, sine_ref, keep_ref, send_ref):
    width = gain_ref.shape[1]
    half = width // 2
    cosine, sine = cosine_ref[...], sine_ref[...]
    first = core_ref[0] == 0
    for i in range(3):
        values = raw_ref[:, i * width : (i + 1) * width]
        if i < 2:
            values = turn(values * column_ref[:, i : i + 1] * gain_ref[i : i + 1, :], cosine, sine)
        low, high = values[:, :half].astype(BF), values[:, half:].astype(BF)
        keep_ref[i] = jnp.where(first, low, high)
        send_ref[i] = jnp.where(first, high, low)


def head_grads(core_ref, own_ref, other_ref, i):
    first = core_ref[0] == 0
    own, other = own_ref[i], other_ref[i]
    return jnp.concatenate([jnp.where(first, own, other), jnp.where(first, other, own)], axis=1).astype(F32)


def inner_kernel(core_ref, own_ref, other_ref, raw_ref, column_ref, gain_ref, cosine_ref, sine_ref, inner_ref, gains_ref):
    width = gain_ref.shape[1]
    cosine, sine = cosine_ref[...], -sine_ref[...]

    @pl.when(pl.program_id(0) == 0)
    def _():
        gains_ref[...] = jnp.zeros_like(gains_ref)

    for i in range(2):
        flat = turn(head_grads(core_ref, own_ref, other_ref, i), cosine, sine) * raw_ref[:, i * width : (i + 1) * width]
        inner_ref[i] = lax.dot_general(
            jnp.ones((8, width), F32),
            flat * gain_ref[i : i + 1, :],
            (((1,), (1,)), ((), ())),
            precision=lax.Precision.HIGHEST,
            preferred_element_type=F32,
        )
        flat = flat * column_ref[:, i : i + 1]
        gains_ref[i] += jnp.sum(flat.reshape(-1, 8, width), axis=0)


def raw_grad_kernel(core_ref, own_ref, other_ref, raw_ref, column_ref, gain_ref, cosine_ref, sine_ref, out_ref):
    width = gain_ref.shape[1]
    cosine, sine = cosine_ref[...], -sine_ref[...]
    for i in range(3):
        values = head_grads(core_ref, own_ref, other_ref, i)
        if i < 2:
            values = turn(values, cosine, sine) * column_ref[:, i : i + 1] * gain_ref[i : i + 1, :]
            values = values - raw_ref[:, i * width : (i + 1) * width] * column_ref[:, i + 2 : i + 3]
        out_ref[:, i * width : (i + 1) * width] = values.astype(BF)


def by_rows(kernel, name, core, ins, outs, rows=256):
    def spec(shape, dim):
        block = tuple(rows if i == dim else extent for i, extent in enumerate(shape))
        return pl.BlockSpec(block, lambda i, core: tuple(i if at == dim else 0 for at in range(len(shape))))

    count = next(out[0][dim] for *out, dim in outs if dim is not None)
    return pl.pallas_call(
        kernel,
        grid_spec=pltpu.PrefetchScalarGridSpec(
            num_scalar_prefetch=1,
            grid=(count // rows,),
            in_specs=[spec((array.shape[0], count, array.shape[2]) if dim == 1 else array.shape, dim) for array, dim in ins],
            out_specs=[spec(shape, dim) for shape, _, dim in outs],
        ),
        out_shape=[jax.ShapeDtypeStruct(shape, dtype) for shape, dtype, _ in outs],
        compiler_params=pltpu.CompilerParams(vmem_limit_bytes=VMEM_LIMIT),
        name=name,
    )(core[None].astype(jnp.int32), *[array for array, _ in ins])


def act_back_kernel(tile, grad_ref, w_ref, slopes_ref, out_ref):
    hidden = w_ref.shape[1]
    for j in range(0, hidden, tile):
        act_grad = dot_nn(grad_ref[...], w_ref[:, j : j + tile])
        for at in (j, hidden + j):
            out_ref[:, at : at + tile] = (act_grad * slopes_ref[:, at : at + tile].astype(F32)).astype(BF)


def act_back(fed_low, w_down, slopes):
    count, width = fed_low.shape
    hidden = w_down.shape[1]
    rows = 256
    return pl.pallas_call(
        functools.partial(act_back_kernel, 512),
        grid=(count // rows,),
        in_specs=[
            pl.BlockSpec((rows, width), lambda i: (i, 0)),
            pl.BlockSpec((width, hidden), lambda i: (0, 0)),
            pl.BlockSpec((rows, 2 * hidden), lambda i: (i, 0)),
        ],
        out_specs=pl.BlockSpec((rows, 2 * hidden), lambda i: (i, 0)),
        out_shape=jax.ShapeDtypeStruct((count, 2 * hidden), BF),
        compiler_params=pltpu.CompilerParams(vmem_limit_bytes=VMEM_LIMIT),
        cost_estimate=pl.CostEstimate(flops=2 * count * width * hidden, bytes_accessed=40_000_000, transcendentals=count * hidden),
        name="act_back",
    )(fed_low, w_down, slopes)


def rank_sums_kernel(chips, size, tile, count, carries, *refs):
    lefts, rights, refs = refs[:count], refs[count : 2 * count], refs[2 * count :]
    if carries:
        carried_ref, out_ref, every_ref, *refs = refs
    else:
        out_ref, *refs = refs
    left_bufs, right_bufs = refs[:count], refs[count : 2 * count]
    passed, got, out, left_sem, right_sem, out_sem, sent_sem, got_sem = refs[2 * count : 2 * count + 8]
    t, c = lax.axis_index("tensor"), lax.axis_index("context")
    core = c % 2
    own = out.shape[1]
    blocks = [(j, core_at) for core_at in (1, 0) for j in range(chips)]

    def left_copy(i, j, core_at):
        rank = 2 * j + (core if core_at == 0 else 1 - core)
        at = pl.ds(pl.multiple_of(rank * own, own), own)
        block = left_bufs[i].at[core_at * chips + j]
        return pltpu.make_async_copy(lefts[i].at[:, at], block, left_sem.at[i, core_at * chips + j])

    tiles = [right.shape[1] // tile for right in rights]

    def right_copy(i, n):
        at = pl.ds(pl.multiple_of(n * tile, tile), tile)
        return pltpu.make_async_copy(rights[i].at[:, at], right_bufs[i].at[:, at], right_sem.at[i, n])

    wait_others = meet(t, c, size if carries else 1, [1])
    for i in range(count):
        left_copy(i, *blocks[0]).start()
        for n in range(tiles[i]):
            right_copy(i, n).start()
        for block in blocks[1:]:
            left_copy(i, *block).start()
    wait_others()
    if carries:
        sent_out, got_out, own_sem = refs[2 * count + 8 :]
        part = carried_ref.at[pl.ds(carries[0], carries[1]), :]
        share = Gather(size, t, part, every_ref, (sent_out, got_out), own_sem)
        share.start(0)
        share.start(1)
    sends = [remote(passed.at[j], got.at[j], (sent_sem, got_sem), j, {"context": flip(c, 1)}) for j in range(chips)]
    writes = [pltpu.make_async_copy(out.at[j], out_ref.at[pl.ds(j * own, own), :], out_sem.at[j]) for j in range(chips)]
    for at, (j, core_at) in enumerate(blocks):
        base = 0
        if core_at == 0:
            sends[j].wait_recv()
        for i in range(count):
            left_copy(i, j, core_at).wait()
            left = left_bufs[i][core_at * chips + j].astype(F32).T.astype(BF)

            def step(n, carry):
                if at == 0:
                    right_copy(i, n).wait()
                part = dot_nn(left, right_bufs[i][:, pl.ds(pl.multiple_of(n * tile, tile), tile)])
                to = pl.ds(pl.multiple_of(base + n * tile, tile), tile)
                if core_at:
                    passed[j, :, to] = part.astype(BF)
                else:
                    out[j, :, to] = (part + got[j, :, to].astype(F32)).astype(BF)
                return carry

            lax.fori_loop(0, tiles[i], step, 0)
            base += tiles[i] * tile
        (sends if core_at else writes)[j].start()
        if carries and at == len(blocks) - 3:
            share.pass_on()
    for j in range(chips):
        sends[j].wait_send()
        writes[j].wait()
    if carries:
        share.wait()
        share.end()


def rank_sums(number, pairs, own, carried=None):
    size = lax.axis_size("tensor")
    lefts, rights = [left for left, _ in pairs], [right for _, right in pairs]
    count, width = lefts[0].shape
    chips = width // (2 * own)
    across = sum(right.shape[1] for right in rights)
    tile = min(512, *[right.shape[1] for right in rights])
    most = max(right.shape[1] for right in rights) // tile
    more = [] if carried is None else [carried[0]]
    dma = pltpu.SemaphoreType.DMA
    return pl.pallas_call(
        functools.partial(rank_sums_kernel, chips, size, tile, len(pairs), carried and carried[1:]),
        in_specs=[pl.BlockSpec(memory_space=pl.ANY)] * (2 * len(pairs) + len(more)),
        out_specs=[pl.BlockSpec(memory_space=pl.ANY)] * (1 + len(more)),
        out_shape=[jax.ShapeDtypeStruct((chips * own, across), BF)]
        + [jax.ShapeDtypeStruct((size * carried[2], rows.shape[1]), BF) for rows in more],
        scratch_shapes=[pltpu.VMEM((2 * chips, count, own), BF)] * len(pairs)
        + [pltpu.VMEM(right.shape, BF) for right in rights]
        + [pltpu.VMEM((chips, own, across), BF)] * 3
        + [dma((len(pairs), 2 * chips)), dma((len(pairs), most)), dma((chips,)), dma((chips,)), dma((chips,))]
        + [dma((links_of(size),)), dma((links_of(size),)), dma] * len(more),
        compiler_params=pltpu.CompilerParams(vmem_limit_bytes=VMEM_LIMIT, collective_id=number, has_side_effects=True),
        cost_estimate=pl.CostEstimate(flops=2 * count * width * across, bytes_accessed=60_000_000, transcendentals=0),
        name="rank_sums",
    )(*lefts, *rights, *more)


def columns_of(*values):
    stacked = jnp.stack(values, axis=1)
    return jnp.pad(stacked, ((0, 0), (0, 8 - len(values))))


def in_order(at_ref, source, target, piece, other=None):
    rows = source.shape[0]

    def step(p, carry):
        start = at_ref[p]
        at = pl.ds(pl.multiple_of(start % rows, piece), piece)
        values = source[at, :]
        if other is not None:
            values = jnp.where(start < rows, values, other[at, :])
        target[pl.ds(pl.multiple_of(p * piece, piece), piece), :] = values
        return carry

    lax.fori_loop(0, target.shape[0] // piece, step, 0)


def out_of_order(at_ref, source, target, piece):
    def step(p, carry):
        start = pl.multiple_of(at_ref[p], piece)
        target[pl.ds(start, piece), :] = source[pl.ds(pl.multiple_of(p * piece, piece), piece), :].astype(target.dtype)
        return carry

    lax.fori_loop(0, source.shape[0] // piece, step, 0)


def causal(tile):
    key_at = lax.broadcasted_iota(jnp.int32, (tile, tile), 0)
    query_at = lax.broadcasted_iota(jnp.int32, (tile, tile), 1)
    return query_at >= key_at


def attend_kernel(piece, tile, at_ref, own_ref, other_ref, out_ref, log_ref, query, key, value, value_t, mixed):
    for slot, held in enumerate((query, key, value)):
        in_order(at_ref, own_ref.at[slot], held, piece, other_ref.at[slot])
    value_t[...] = value[...].astype(F32).T.astype(BF)
    allowed = causal(tile)
    for i in range(query.shape[0] // tile):
        low, high = i * tile, (i + 1) * tile
        rows = query[low:high, :]
        near = jnp.where(allowed, dot_nt(key[low:high, :], rows) * HD ** (-0.5), -1e30)
        top = jnp.max(near, axis=0, keepdims=True)
        if i:
            far = dot_nt(key[0:low, :], rows) * HD ** (-0.5)
            top = jnp.maximum(top, jnp.max(far, axis=0, keepdims=True))
        near = jnp.exp(near - top)
        total = jnp.sum(near, axis=0, keepdims=True)
        summed = dot_nn(value_t[:, low:high], near.astype(BF))
        if i:
            far = jnp.exp(far - top)
            total = total + jnp.sum(far, axis=0, keepdims=True)
            summed = summed + dot_nn(value_t[:, 0:low], far.astype(BF))
        mixed[low:high, :] = (summed / total).T
        log_ref[0, :, low:high] = top + jnp.log(total)
    out_of_order(at_ref, mixed, out_ref, piece)


def attend(own, other, at, piece):
    half, width = own.shape[1:]
    rows = 2 * half
    heads = width // HD
    return pl.pallas_call(
        functools.partial(attend_kernel, piece, 256),
        grid_spec=pltpu.PrefetchScalarGridSpec(
            num_scalar_prefetch=1,
            grid=(heads,),
            in_specs=[pl.BlockSpec((3, half, HD), lambda h, at: (0, 0, h))] * 2,
            out_specs=[
                pl.BlockSpec((rows, HD), lambda h, at: (0, h)),
                pl.BlockSpec((1, 1, rows), lambda h, at: (h, 0, 0)),
            ],
            scratch_shapes=[pltpu.VMEM((rows, HD), BF)] * 3 + [pltpu.VMEM((HD, rows), BF), pltpu.VMEM((rows, HD), F32)],
        ),
        out_shape=[jax.ShapeDtypeStruct((rows, width), BF), jax.ShapeDtypeStruct((heads, 1, rows), F32)],
        compiler_params=pltpu.CompilerParams(vmem_limit_bytes=VMEM_LIMIT),
        cost_estimate=pl.CostEstimate(
            flops=2 * 2 * heads * rows * rows * HD, bytes_accessed=8 * rows * width, transcendentals=heads * rows * rows // 2
        ),
        name="attend",
    )(at, own, other)


def attend_back_kernel(
    piece, tile, at_ref, own_ref, other_ref, out_ref, grad_ref, log_ref, dqkv_ref, query, key, value, key_t, grad, mixed, dquery, dkey, dvalue
):
    for slot, held in enumerate((query, key, value)):
        in_order(at_ref, own_ref.at[slot], held, piece, other_ref.at[slot])
    in_order(at_ref, grad_ref, grad, piece)
    in_order(at_ref, out_ref, mixed, piece)
    key_t[...] = key[...].astype(F32).T.astype(BF)
    allowed = causal(tile)
    dkey[...] = jnp.zeros_like(dkey)
    dvalue[...] = jnp.zeros_like(dvalue)
    scale = HD ** (-0.5)
    for i in range(query.shape[0] // tile):
        low, high = i * tile, (i + 1) * tile
        rows = query[low:high, :]
        rows_grad = grad[low:high, :]
        log = log_ref[0, :, low:high]
        spread = jnp.sum((rows_grad.astype(F32) * mixed[low:high, :].astype(F32)).T, axis=0, keepdims=True)
        dquery_t = None
        for start, stop, masked in ((0, low, False), (low, high, True)):
            if start == stop:
                continue
            scores = dot_nt(key[start:stop, :], rows) * scale
            if masked:
                scores = jnp.where(allowed, scores, -1e30)
            probs = jnp.exp(scores - log)
            probs_grad = dot_nt(value[start:stop, :], rows_grad)
            scores_grad = (probs * (probs_grad - spread)).astype(BF)
            dvalue[start:stop, :] += dot_nn(probs.astype(BF), rows_grad)
            dkey[start:stop, :] += dot_nn(scores_grad, rows)
            term = dot_nn(key_t[:, start:stop], scores_grad)
            dquery_t = term if dquery_t is None else dquery_t + term
        dquery[low:high, :] = dquery_t.T * scale
    dkey[...] = dkey[...] * scale
    for slot, held in enumerate((dquery, dkey, dvalue)):
        out_of_order(at_ref, held, dqkv_ref.at[slot], piece)


def attend_back(own, other, out, grad, log, at, piece):
    half, width = own.shape[1:]
    rows = 2 * half
    heads = width // HD
    return pl.pallas_call(
        functools.partial(attend_back_kernel, piece, 256),
        grid_spec=pltpu.PrefetchScalarGridSpec(
            num_scalar_prefetch=1,
            grid=(heads,),
            in_specs=[
                pl.BlockSpec((3, half, HD), lambda h, at: (0, 0, h)),
                pl.BlockSpec((3, half, HD), lambda h, at: (0, 0, h)),
                pl.BlockSpec((rows, HD), lambda h, at: (0, h)),
                pl.BlockSpec((rows, HD), lambda h, at: (0, h)),
                pl.BlockSpec((1, 1, rows), lambda h, at: (h, 0, 0)),
            ],
            out_specs=pl.BlockSpec((3, rows, HD), lambda h, at: (0, 0, h)),
            scratch_shapes=[pltpu.VMEM((rows, HD), BF)] * 3
            + [pltpu.VMEM((HD, rows), BF)]
            + [pltpu.VMEM((rows, HD), BF)] * 2
            + [pltpu.VMEM((rows, HD), F32)] * 3,
        ),
        out_shape=jax.ShapeDtypeStruct((3, rows, width), BF),
        compiler_params=pltpu.CompilerParams(vmem_limit_bytes=VMEM_LIMIT),
        cost_estimate=pl.CostEstimate(
            flops=5 * heads * rows * rows * HD * 2, bytes_accessed=16 * rows * width, transcendentals=heads * rows * rows // 2
        ),
        name="attend_back",
    )(at, own, other, out, grad, log)


def local(
    tokens,
    block_order,
    query_weight,
    key_weight,
    value_weight,
    output_weight,
    gate_weight,
    up_weight,
    down_weight,
    query_gain,
    key_gain,
    attention_gain,
    forward_gain,
    cotangent,
):
    seqs, local_len, width = tokens.shape
    ranks = lax.axis_size("context")
    columns = lax.axis_size("tensor")
    full_len = local_len * ranks
    piece_len = full_len // block_order.shape[0]
    piece = local_len // columns
    shard_rows = seqs * piece
    count = shard_rows * columns
    context = lax.axis_index("context")
    t = lax.axis_index("tensor")
    s, core = context // 2, context % 2
    head_width = query_weight.shape[1]
    half_width = head_width // 2
    hidden_width = gate_weight.shape[1]

    gain_columns = jnp.stack([attention_gain, forward_gain], axis=1)
    gain_columns = jnp.pad(gain_columns, ((0, 0), (0, HD - 2)))
    firsts = [query_weight, key_weight, value_weight, output_weight.T, gain_columns]
    rows, w_first, gate_up_shard, row_shard = start(tokens, firsts, [gate_weight, up_weight], seqs)
    qkv_width = 3 * head_width
    gains = w_first[:, 4 * head_width :]
    gain_attn, gain_feed = gains[:, 0].astype(F32)[None], gains[:, 1].astype(F32)[None]
    w_gate_up = lax.all_gather(gate_up_shard, "context", axis=0, tiled=True)

    chips = s ^ jnp.arange(seqs, dtype=jnp.int32)
    shards = t ^ jnp.arange(columns, dtype=jnp.int32)
    starts = (2 * chips[None, :] + core) * local_len + shards[:, None] * piece
    stored = (starts[:, :, None] + jnp.arange(piece, dtype=jnp.int32)).reshape(count)
    block = stored // piece_len
    slots = jnp.arange(block_order.shape[0], dtype=jnp.int32)
    place = jnp.sum(jnp.where(block[:, None] == slots[None, :], block_order[None, :], 0), axis=1) * piece_len
    place = place + stored % piece_len
    freq = THETA ** (-jnp.arange(0, HD, 2, dtype=F32) / HD)
    angle = place.astype(F32)[:, None] * freq[None, :]
    cosine = jnp.concatenate([jnp.cos(angle), jnp.cos(angle)], axis=-1)
    sine = jnp.concatenate([-jnp.sin(angle), jnp.sin(angle)], axis=-1)
    per_block = piece_len // piece
    pieces = jnp.arange(full_len // piece, dtype=jnp.int32)
    hits = block_order[None, :] == (pieces // per_block)[:, None]
    block_at = jnp.sum(jnp.where(hits, slots[None, :], 0), axis=1)
    piece_at = block_at * per_block + pieces % per_block
    rank_of, shard_of = piece_at // columns, piece_at % columns
    at = (((rank_of % 2) ^ core) * columns + (shard_of ^ t)) * seqs + ((rank_of // 2) ^ s)
    at = (at * piece).astype(jnp.int32)

    qkv_raw = dot_nn(rows, w_first[:, :qkv_width])
    query_raw = qkv_raw[:, :head_width]
    key_raw = qkv_raw[:, head_width : 2 * head_width]
    totals = sum_over_tensor(jnp.stack([jnp.sum(query_raw * query_raw, axis=1), jnp.sum(key_raw * key_raw, axis=1)]))
    factors = lax.rsqrt(totals / width + EPS)
    scaling = jnp.stack([query_gain, key_gain]).astype(F32)
    keep, send = by_rows(
        turn_kernel,
        "turn",
        core,
        [(qkv_raw, 0), (columns_of(*factors), 0), (scaling, None), (cosine, 0), (sine, 0)],
        [((3, count, half_width), BF, 1)] * 2,
    )
    received = swap(send, "context", 1)
    mixed_heads, log = attend(keep, received, at, piece)

    def to_heads(values):
        keep = lax.dynamic_slice_in_dim(values, core * half_width, half_width, axis=1)
        send = lax.dynamic_slice_in_dim(values, (1 - core) * half_width, half_width, axis=1)
        return jnp.concatenate([keep, swap(send, "context", 1)], axis=0)

    def to_rows(values):
        own, other = values[:count], swap(values[count:], "context", 1)
        return jnp.concatenate([jnp.where(core == 0, own, other), jnp.where(core == 0, other, own)], axis=1)

    mixed_low = to_rows(mixed_heads)

    def chunk(values, k):
        return values[k * shard_rows : (k + 1) * shard_rows]

    order = list(range(columns))
    shard = (shard_rows, width)
    hidden_low, attended, hidden = exchange(
        "attended", 1, mixed_low, w_first, finish_attended, [row_shard, gain_attn], [(shard, F32), (shard, F32)], offset=qkv_width
    )

    fed_low, slopes, act_low, w_down, upstream, _, output_pieces, feed_gain_rows = feed(
        hidden_low, w_gate_up, down_weight.T, cotangent, hidden, gain_feed, seqs
    )

    own = width // ranks
    cores = [list(range(0, ranks, 2)), list(range(1, ranks, 2))]

    def scatter(values):
        return lax.psum_scatter(values, "context", scatter_dimension=0, axis_index_groups=cores, tiled=True)

    output_pieces = output_pieces.reshape(shard)
    split = seqs // 4 * piece
    down_part, first_rows = rank_sums(5, [(fed_low, act_low)], own, (output_pieces, 0, split))
    down_summed = scatter(down_part)
    down_grad = down_summed.astype(F32).T
    gate_up_low = act_back(after(fed_low, down_part), w_down, slopes)
    gate_up_part, other_rows = rank_sums(6, [(hidden_low, gate_up_low)], own, (output_pieces, split, shard_rows - split))
    layer_output = in_place([values.reshape(columns, -1, piece, width) for values in (first_rows, other_rows)], s, t, BF)
    gate_up_summed = scatter(gate_up_part)
    gate_up_low = after(gate_up_low, gate_up_part)
    attended_low, hidden_grad, attn_gain_rows = exchange(
        "hidden_grad",
        3,
        gate_up_low,
        w_gate_up,
        finish_hidden_grad,
        [attended, upstream, gain_attn],
        [(shard, F32), ((8, width), F32)],
    )
    attended_low = after(attended_low, layer_output)
    mixed_grad = dot_nn(attended_low, w_first[:, qkv_width : 4 * head_width]).astype(BF)
    dqkv = attend_back(keep, received, mixed_heads, to_heads(mixed_grad), log, at, piece)
    dqkv_other = swap(dqkv[:, count:], "context", 1)
    inner, head_gain_rows = by_rows(
        inner_kernel,
        "inner",
        core,
        [(dqkv, 1), (dqkv_other, 1), (qkv_raw, 0), (columns_of(*factors), 0), (scaling, None), (cosine, 0), (sine, 0)],
        [((2, 8, count), F32, 2), ((2, 8, head_width), F32, None)],
    )
    inner = sum_over_tensor(inner[:, 0])
    (qkv_low,) = by_rows(
        raw_grad_kernel,
        "raw_grad",
        core,
        [
            (dqkv, 1),
            (dqkv_other, 1),
            (qkv_raw, 0),
            (after(columns_of(*factors, *(inner * factors**3 / width)), down_grad), 0),
            (scaling, None),
            (cosine, 0),
            (sine, 0),
        ],
        [((count, 3 * head_width), BF, 0)],
    )
    (qkv_part,) = rank_sums(7, [(rows, qkv_low), (attended_low, mixed_low)], own)
    qkv_out_summed = scatter(after(qkv_part, gate_up_summed, down_summed))
    every, width_gains, head_gains = exchange(
        "tokens_grad",
        4,
        after(qkv_low, qkv_part),
        w_first,
        None,
        [hidden_grad, attn_gain_rows, feed_gain_rows, head_gain_rows.reshape(16, head_width)],
        [((8, own), F32), ((8, head_width), F32)],
        chips=seqs,
        last=True,
    )
    tokens_grad = in_place([every.reshape(columns, seqs, piece, width)], s, t, F32)

    gate_up_summed, qkv_out_summed = gate_up_summed.astype(F32), qkv_out_summed.astype(F32)
    return (
        layer_output,
        tokens_grad,
        qkv_out_summed[:, :head_width],
        qkv_out_summed[:, head_width : 2 * head_width],
        qkv_out_summed[:, 2 * head_width : 3 * head_width],
        qkv_out_summed[:, 3 * head_width :].T,
        gate_up_summed[:, :hidden_width],
        gate_up_summed[:, hidden_width:],
        down_grad,
        head_gains[0],
        head_gains[1],
        width_gains[0],
        width_gains[1],
    )


def solution(mesh):
    return jax.shard_map(
        local,
        mesh=mesh,
        in_specs=(
            P(None, "context", None),
            P(),
            P("context", "tensor"),
            P("context", "tensor"),
            P("context", "tensor"),
            P("tensor", "context"),
            P("context", "tensor"),
            P("context", "tensor"),
            P("tensor", "context"),
            P("tensor"),
            P("tensor"),
            P("context"),
            P("context"),
            P(None, "context", None),
        ),
        out_specs=(
            P(None, "context", None),
            P(None, "context", None),
            P("context", "tensor"),
            P("context", "tensor"),
            P("context", "tensor"),
            P("tensor", "context"),
            P("context", "tensor"),
            P("context", "tensor"),
            P("tensor", "context"),
            P("tensor"),
            P("tensor"),
            P("context"),
            P("context"),
        ),
        check_vma=False,
    )
```

```python
import functools

import jax
import jax.numpy as jnp
from jax import lax
from jax.experimental import pallas as pl
from jax.experimental.pallas import tpu as pltpu
from jax.sharding import PartitionSpec as P

HD = 128
EPS = 1e-06
THETA = 500000.0
BF = jnp.bfloat16
F32 = jnp.float32
VMEM_LIMIT = 60 * 1024 * 1024
MESH = pl.DeviceIdType.MESH


def dot_nn(left, right):
    return jnp.dot(left, right, preferred_element_type=F32)


def dot_nt(left, right):
    return lax.dot_general(left, right, (((1,), (1,)), ((), ())), preferred_element_type=F32)


def after(values, *others):
    return lax.optimization_barrier((values, *others))[0]


def swap(values, axis, mask):
    size = lax.axis_size(axis)
    return lax.ppermute(values, axis, [(i, i ^ mask) for i in range(size)])


def sum_over_tensor(values):
    size = lax.axis_size("tensor")
    chunks = values.reshape(values.shape[0], size, -1)
    total = chunks
    for m in range(1, size):
        other = swap(chunks, "tensor", m)
        total = total + jnp.stack([other[:, m ^ k] for k in range(size)], axis=1)
    return total.reshape(values.shape)


def place_kernel(at_ref, *refs):
    out_ref = refs[-1]
    for a in range(out_ref.shape[0]):
        at, base, values = a ^ at_ref[0], 0, None
        for ref in refs[:-1]:
            count = ref.shape[1]
            part = ref[0, jnp.clip(at - base, 0, count - 1)]
            values = part if values is None else jnp.where(at >= base, part, values)
            base += count
        out_ref[a, 0] = values.astype(out_ref.dtype)


def in_place(parts, s, t, dtype):
    size, _, piece, width = parts[0].shape
    seqs = sum(part.shape[1] for part in parts)
    full = pl.pallas_call(
        place_kernel,
        grid_spec=pltpu.PrefetchScalarGridSpec(
            num_scalar_prefetch=1,
            grid=(size,),
            in_specs=[pl.BlockSpec((1, *part.shape[1:]), lambda b, at: (b ^ at[1], 0, 0, 0)) for part in parts],
            out_specs=pl.BlockSpec((seqs, 1, piece, width), lambda b, at: (0, b, 0, 0)),
        ),
        out_shape=jax.ShapeDtypeStruct((seqs, size, piece, width), dtype),
        name="place_rows",
    )(jnp.stack([s, t]).astype(jnp.int32), *parts)
    return full.reshape(seqs, size * piece, width)


def norm_factor(values):
    return lax.rsqrt(jnp.mean(values * values, axis=-1, keepdims=True) + EPS)


def norm_back(values, factor, gain, grad):
    scaled = grad * gain
    inner = jnp.mean(values * scaled, axis=-1, keepdims=True)
    return factor * scaled - values * (factor**3 * inner), grad * values * factor


def flip(index, mask):
    bit = 1
    result = index
    while bit <= mask:
        if mask & bit:
            result = result + bit - 2 * bit * ((index // bit) % 2)
        bit *= 2
    return result


def exchange_kernel(size, width, depth, offset, tile, finish, chips, last, n_in, n_out, a_ref, w_ref, *refs):
    ins, rest = refs[:n_in], refs[n_in:]
    every, outs, rest = rest[0], rest[1 : 1 + n_out], rest[1 + n_out :]
    a_buf, w_buf, sent, got, total, mine, a_sem, w_sem, sent_sem, got_sem, out_sem, in_sem, own_sem = rest[:13]
    t = lax.axis_index("tensor")
    c = lax.axis_index("context")
    rows = total.shape[0]
    half = rows // 2

    def a_copy(k):
        at = pl.ds(k * rows, rows)
        return pltpu.make_async_copy(a_ref.at[at, :], a_buf.at[at, :], a_sem.at[k])

    def w_copy(j):
        at = pl.ds(pl.multiple_of(j * tile, tile), tile)
        return pltpu.make_async_copy(w_ref.at[at, pl.ds(offset, depth)], w_buf.at[at, :], w_sem.at[j])

    order = [3, 1, 2, 0] if size == 4 else [*range(1, size), 0]
    tiles = width // tile
    parts = tiles if size == 4 else 1
    across = width // parts
    a_copy(order[0]).start()
    for j in range(tiles):
        w_copy(j).start()
    for k in order[1:]:
        a_copy(k).start()
    barrier = pltpu.get_barrier_semaphore()
    for k in range(1, size):
        pl.semaphore_signal(barrier, inc=1, device_id={"tensor": flip(t, k)}, device_id_type=MESH)

    met = range(1, 2 * chips) if last else range(2, 2 * chips, 2)
    for mask in met:
        pl.semaphore_signal(barrier, inc=1, device_id={"context": flip(c, mask)}, device_id_type=MESH)
    for out in outs:
        if out.shape[0] == 8:
            out[...] = jnp.zeros_like(out)

    def cross(j, source, target, sems, base=0):
        if j == 0:
            return pltpu.make_async_copy(source, target, sems[0].at[base])
        return pltpu.make_async_remote_copy(
            src_ref=source,
            dst_ref=target,
            send_sem=sems[0].at[base + j],
            recv_sem=sems[1].at[base + j],
            device_id={"context": flip(c, 2 * j)},
            device_id_type=MESH,
        )

    def send(slot, source, target, partner, sems):
        return pltpu.make_async_remote_copy(
            src_ref=source,
            dst_ref=target,
            send_sem=sems[0].at[slot],
            recv_sem=sems[1].at[slot],
            device_id={"tensor": flip(t, partner)},
            device_id_type=MESH,
        )

    def product(k, first=False, part=0):
        if part == 0:
            a_copy(k).wait()

        def step(j, carry):
            if first:
                w_copy(j).wait()
            at = pl.ds(pl.multiple_of(j * tile, tile), tile)
            value = dot_nt(a_buf[k * rows : (k + 1) * rows, :], w_buf[at, :])
            if k:
                sent[k - 1, :, at] = value.astype(BF)
            else:
                total[:, at] = value
            return carry

        lax.fori_loop(part * tiles // parts, (part + 1) * tiles // parts, step, 0)

    def add(slot, other, first, columns):
        def step(i, carry):
            at = pl.ds(pl.multiple_of(first + i * 16, 16), 16)
            sent[slot, at, columns] = (sent[slot, at, columns].astype(F32) + got[other, at, columns].astype(F32)).astype(BF)
            return carry

        lax.fori_loop(0, half // 16, step, 0)

    def columns_of_part(part):
        return pl.ds(part * across, across)

    low, high = pl.ds(0, half), pl.ds(half, half)
    sums = (sent_sem, got_sem)
    product(order[0], first=True)
    pl.semaphore_wait(barrier, size - 1 + len(met))
    piece = rows // max(1, chips)
    crossing = []
    small = []
    if last:
        gain_rows, head_rows, gain_got, head_got, own_got, small_sent, small_got = rest[18:]
        attn_rows, feed_rows, two_heads = ins[1:]
        gain_rows[...] = jnp.zeros_like(gain_rows)
        head_rows[...] = jnp.zeros_like(head_rows)
        for i, part in enumerate((attn_rows, feed_rows)):
            gain_rows[i : i + 1, :] = jnp.sum(part[...], axis=0, keepdims=True)
            head_rows[i : i + 1, :] = jnp.sum(two_heads[8 * i : 8 * i + 8, :], axis=0, keepdims=True)
        own_width = outs[0].shape[1]

        def tell(source, target, device):
            copy = pltpu.make_async_remote_copy(
                src_ref=source,
                dst_ref=target,
                send_sem=small_sent.at[len(small)],
                recv_sem=small_got.at[len(small)],
                device_id=device,
                device_id_type=MESH,
            )
            copy.start()
            small.append(copy)

        for k in range(1, size):
            tell(gain_rows, gain_got.at[k - 1], {"tensor": flip(t, k)})
        for mask in met:
            tell(head_rows, head_got.at[mask - 1], {"context": flip(c, mask)})
    if chips and not last:
        source, target = ins[0], outs[0]
        for j in range(chips):
            crossing.append(
                cross(
                    j,
                    source.at[flip(c // 2, j), pl.ds(pl.multiple_of(t * piece, piece), piece), :],
                    target.at[pl.ds(j * piece, piece), :],
                    rest[13:15],
                )
            )
            crossing[-1].start()

    def home(part):
        at = columns_of_part(part)
        return [
            cross(j, mine.at[pl.ds(j * piece, piece), at], rest[17].at[pl.ds(j * piece, piece), at], rest[15:17], part * chips)
            for j in range(chips)
        ]

    def finish_last(part, group):
        at = columns_of_part(part)
        for copy in group[2:] if size == 4 else group:
            copy.wait_recv()

        def step(i, carry):
            row = pl.ds(pl.multiple_of(i * 16, 16), 16)
            summed = ins[0][row, at] + total[row, at]
            for other in range(2 if size == 4 else size - 1):
                summed = summed + got[other, row, at].astype(F32)
            mine[row, at] = summed.astype(BF)
            return carry

        lax.fori_loop(0, rows // 16, step, 0)
        for copy in home(part):
            copy.start()

    def sums_of(part):
        at = columns_of_part(part)
        return [
            send(6 * part + 0, sent.at[2, low, at], got.at[2, low, at], 1, sums),
            send(6 * part + 1, sent.at[2, high, at], got.at[2, high, at], 2, sums),
            send(6 * part + 2, sent.at[0, low, at], got.at[0, low, at], 1, sums),
            send(6 * part + 3, sent.at[1, high, at], got.at[1, high, at], 2, sums),
            send(6 * part + 4, sent.at[1, low, at], got.at[1, low, at], 2, sums),
            send(6 * part + 5, sent.at[0, high, at], got.at[0, high, at], 1, sums),
        ]

    if size == 4:
        groups = [sums_of(part) for part in range(parts)]
        copies = sum(groups, [])
        for part, group in enumerate(groups):
            for k, ready in ((3, group[:2]), (1, group[2:3]), (2, group[3:4])):
                if k != 3 or part:
                    product(k, first=k == 3, part=part)
                for copy in [] if last and part else ready:
                    copy.start()
        for part, group in enumerate(groups):
            at = columns_of_part(part)
            group[0].wait_recv()
            add(1, 2, 0, at)
            group[4].start()
            group[1].wait_recv()
            add(0, 2, half, at)
            group[5].start()
            for copy in groups[part + 1][:4] if last and part + 1 < parts else []:
                copy.start()
            product(0, part=part)
            if last and part + 1 < parts:
                finish_last(part, group)
        for group in [] if last else groups:
            for copy in group[2:]:
                copy.wait_recv()
        used = 2
    else:
        copies = [send(k - 1, sent.at[k - 1], got.at[k - 1], k, sums) for k in range(1, size)]
        copies[0].start()
        for k in range(2, size):
            product(k)
            copies[k - 1].start()
        product(0)
        groups = [copies]
        if not last:
            for copy in copies:
                copy.wait_recv()
        used = size - 1
    if last:
        finish_last(parts - 1, groups[-1])
    if chips and not last:
        crossing[0].wait()
        for copy in crossing[1:]:
            copy.wait_recv()

    def finish_rows(first, count, part=0):
        def step(i, carry):
            at = pl.ds(pl.multiple_of(first + i * 16, 16), 16)
            summed = total[at, :]
            for other in range(used):
                summed = summed + got[other, at, :].astype(F32)
            mine[at, :] = finish(at, summed, ins, outs).astype(BF)
            return carry

        lax.fori_loop(0, count // 16, step, 0)

    gather = (out_sem, in_sem)
    shared = rest[17] if last else mine
    own = pltpu.make_async_copy(shared, every.at[pl.ds(0, rows), :], own_sem)
    if last:
        going_home = [home(part) for part in range(parts)]
    else:
        going_home = [[cross(j, outs[1].at[pl.ds(j * piece, piece), :], outs[2].at[j], rest[15:17]) for j in range(chips)]]
    if last:
        for copy in small:
            copy.wait()
        for k in range(1, size):
            gain_rows[...] += gain_got[k - 1]
        outs[1][...] = head_rows[...]
        for mask in met:
            outs[1][...] += head_got[mask - 1]
        for mask in met:
            at = pl.ds(pl.multiple_of(flip(c, mask) * own_width, own_width), own_width)
            tell(gain_rows.at[:, at], own_got.at[mask - 1], {"context": flip(c, mask)})

    def came_home(first, count, part=0):
        for j in range(first // piece, (first + count) // piece):
            if j == 0:
                going_home[part][j].wait()
            else:
                going_home[part][j].wait_recv()

    out_parts = parts if last else 1
    make_ready = came_home if last else finish_rows
    then = [own] if last else [own, *going_home[0]]
    if size == 4:

        def out_columns(part):
            return pl.ds(part * (width // out_parts), width // out_parts)

        def chunk(k, side, part):
            return every.at[pl.ds(k * rows + side * half, half), out_columns(part)]

        def share(k, side, part):
            source = shared.at[pl.ds(side * half, half), out_columns(part)]
            return send(6 * part + 2 * k + side, source, chunk(k + 1, side, part), k + 1, gather)

        groups = []
        for part in range(out_parts):
            shares = [share(k, side, part) for k in (0, 1) for side in (0, 1)]
            passed = [
                send(6 * part + 4, chunk(1, 0, part), chunk(3, 0, part), 2, gather),
                send(6 * part + 5, chunk(2, 1, part), chunk(3, 1, part), 1, gather),
            ]
            groups.append(shares + passed)
        for part, group in enumerate(groups):
            make_ready(0, half, part)
            group[0].start()
            group[2].start()
            make_ready(half, half, part)
            group[3].start()
            group[1].start()
            if part == out_parts - 1:
                for copy in then:
                    copy.start()
            group[0].wait_recv()
            group[4].start()
            group[3].wait_recv()
            group[5].start()
        for group in groups:
            for at in (1, 2, 4, 5):
                group[at].wait_recv()
        shares = sum(groups, [])
    else:
        make_ready(0, rows)
        shares = [send(k - 1, shared, every.at[pl.ds(k * rows, rows), :], k, gather) for k in range(1, size)]
        for copy in [*shares, *then]:
            copy.start()
        for copy in shares:
            copy.wait_recv()
    own.wait()
    if chips and not last:
        came_home(0, rows)
    if last:
        for copy in small[size - 1 + len(met) :]:
            copy.wait()
        outs[0][...] = gain_rows[:, pl.ds(pl.multiple_of(c * own_width, own_width), own_width)]
        for mask in met:
            outs[0][...] += own_got[mask - 1]
    for copy in copies + shares + crossing[1:] + sum([group[1:] for group in going_home], []):
        copy.wait_send()


def exchange(name, number, a, w, finish, ins, outs, offset=0, chips=0, last=False):
    size = lax.axis_size("tensor")
    rows, width, depth = a.shape[0] // size, w.shape[0], a.shape[1]
    tile = min(512, width)
    parts = width // tile if size == 4 else 1
    links = 6 * parts if size == 4 else size - 1
    whole = pl.BlockSpec(memory_space=pltpu.VMEM)
    anywhere = pl.BlockSpec(memory_space=pl.ANY)
    dma = pltpu.SemaphoreType.DMA
    gain_scratch = []
    if last:
        own, head_width = outs[0][0][1], outs[1][0][1]
        ranks = 2 * chips
        gain_scratch = [
            pltpu.VMEM((rows, width), BF),
            pltpu.VMEM((8, width), F32),
            pltpu.VMEM((8, head_width), F32),
            pltpu.VMEM((size - 1, 8, width), F32),
            pltpu.VMEM((ranks - 1, 8, head_width), F32),
            pltpu.VMEM((ranks - 1, 8, own), F32),
            dma((size - 1 + 2 * (ranks - 1),)),
            dma((size - 1 + 2 * (ranks - 1),)),
        ]
    return pl.pallas_call(
        functools.partial(exchange_kernel, size, width, depth, offset, tile, finish, chips, last, len(ins), len(outs)),
        in_specs=[anywhere, anywhere] + [anywhere if chips and not last and i == 0 else whole for i in range(len(ins))],
        out_specs=[anywhere] + [whole] * len(outs),
        out_shape=[jax.ShapeDtypeStruct((size * rows, width), BF)] + [jax.ShapeDtypeStruct(*out) for out in outs],
        scratch_shapes=[
            pltpu.VMEM((size * rows, depth), BF),
            pltpu.VMEM((width, depth), BF),
            pltpu.VMEM((size - 1, rows, width), BF),
            pltpu.VMEM((size - 1, rows, width), BF),
            pltpu.VMEM((rows, width), F32),
            pltpu.VMEM((rows, width), BF),
            dma((size,)),
            dma((width // tile,)),
            dma((links,)),
            dma((links,)),
            dma((links,)),
            dma((links,)),
            dma,
        ]
        + [dma((chips * parts,))] * (4 if chips else 0)
        + gain_scratch,
        compiler_params=pltpu.CompilerParams(vmem_limit_bytes=VMEM_LIMIT, collective_id=number, has_side_effects=True),
        cost_estimate=pl.CostEstimate(flops=2 * size * rows * width * depth, bytes_accessed=240_000_000, transcendentals=0),
        name=name,
    )(a, w, *ins)


def add_rows(ref, values):
    ref[...] += values[:8] + values[8:]


def finish_attended(at, attended, ins, outs):
    tokens, gain = ins
    outs[0][at, :] = attended
    hidden = tokens[at, :].astype(F32) + attended * norm_factor(attended) * gain[...]
    outs[1][at, :] = hidden
    return hidden


def finish_hidden_grad(at, summed, ins, outs):
    attended, cotangent, gain = ins
    hidden_grad = cotangent[at, :].astype(F32) + summed
    outs[0][at, :] = hidden_grad
    values = attended[at, :]
    grad, gain_rows = norm_back(values, norm_factor(values), gain[...], hidden_grad)
    add_rows(outs[1], gain_rows)
    return grad


def remote(source, target, sems, slot, device):
    return pltpu.make_async_remote_copy(
        src_ref=source,
        dst_ref=target,
        send_sem=sems[0].at[slot],
        recv_sem=sems[1].at[slot],
        device_id=device,
        device_id_type=MESH,
    )


def meet(t, c, size, masks):
    barrier = pltpu.get_barrier_semaphore()
    for k in range(1, size):
        pl.semaphore_signal(barrier, inc=1, device_id={"tensor": flip(t, k)}, device_id_type=MESH)
    for mask in masks:
        pl.semaphore_signal(barrier, inc=1, device_id={"context": flip(c, mask)}, device_id_type=MESH)
    return lambda: pl.semaphore_wait(barrier, size - 1 + len(masks))


class Line:
    def __init__(self, chips, own, buf, up_sems, down_sems, core_sems):
        self.chips, self.own, self.buf = chips, own, buf
        self.sems, self.core_sems = {1: up_sems, -1: down_sems}, core_sems
        self.c = lax.axis_index("context")
        self.s, self.core = self.c // 2, self.c % 2

    def rows(self, chip, part=None):
        base = (2 * chip + self.core) * self.own
        if part is None:
            return pl.ds(pl.multiple_of(base, self.own), self.own)
        half = self.own // 2
        return pl.ds(pl.multiple_of(base + part * half, half), half)

    def hop(self, k, way, chip, part):
        ref = self.buf.at[self.rows(chip, part), :]
        return remote(ref, ref, self.sems[way], 2 * k + part, {"context": self.c + 2 * way})

    def cross(self, k, way, chip, part):
        ref = self.buf.at[self.rows(chip, part), :]
        slot = 0 if k < 0 else 1 + 2 * k + (way < 0)
        return remote(ref, ref, self.core_sems, 2 * slot + part, {"context": flip(self.c, 1)})

    def sends(self, k, way):
        if way > 0:
            return (self.s >= k) & (self.s < self.chips - 1)
        return (self.s + k < self.chips) & (self.s > 0)

    def gets(self, k, way):
        return self.s >= k + 1 if way > 0 else self.s + k + 1 < self.chips

    def each(self, test, k, act):
        for way in (1, -1):
            pl.when(test(k, way))(functools.partial(act, k, way))

    def start(self, k, part):
        self.each(self.sends, k, lambda k, way: self.hop(k, way, self.s - way * k, part).start())

    def begin(self):
        for part in range(2):
            self.start(0, part)
            self.cross(-1, 1, self.s, part).start()

    def advance(self, k, parts=(0, 1)):
        for part in parts:

            def got(k, way):
                chip = self.s - way * (k + 1)
                self.hop(k, way, chip, part).wait_recv()
                self.cross(k, way, chip, part).start()

            self.each(self.gets, k, got)
            if k + 1 < self.chips - 1:
                self.start(k + 1, part)

    def other_core(self, k):
        for part in range(2):
            if k < 0:
                self.cross(-1, 1, self.s, part).wait_recv()
            else:
                self.each(self.gets, k, lambda k, way: self.cross(k, way, self.s - way * (k + 1), part).wait_recv())

    def end(self):
        for part in range(2):
            self.cross(-1, 1, self.s, part).wait_send()
            for k in range(self.chips - 1):
                self.each(self.sends, k, lambda k, way: self.hop(k, way, self.s - way * k, part).wait_send())
                self.each(self.gets, k, lambda k, way: self.cross(k, way, self.s - way * (k + 1), part).wait_send())


def line_sems(chips):
    dma = pltpu.SemaphoreType.DMA
    return [dma((2 * (chips - 1),))] * 4 + [dma((2 * (2 * chips - 1),))] * 2


class Sums:
    def __init__(self, size, t, sent, got, columns, sems, base):
        rows = sent.shape[1]
        low, high = pl.ds(0, rows // 2), pl.ds(rows // 2, rows // 2)
        self.size, self.sent, self.got, self.columns, self.half = size, sent, got, columns, rows // 2

        def send(slot, of, to, at, partner):
            return remote(sent.at[of, at, columns], got.at[to, at, columns], sems, base + slot, {"tensor": flip(t, partner)})

        if size == 4:
            self.copies = [
                send(0, 2, 2, low, 1),
                send(1, 2, 2, high, 2),
                send(2, 0, 0, low, 1),
                send(3, 1, 1, high, 2),
                send(4, 1, 1, low, 2),
                send(5, 0, 0, high, 1),
            ]
            self.after_product = {3: self.copies[:2], 1: self.copies[2:3], 2: self.copies[3:4]}
        else:
            self.copies = [send(k - 1, k - 1, k - 1, pl.ds(0, rows), k) for k in range(1, size)]
            self.after_product = {k: self.copies[k - 1 : k] for k in range(1, size)}

    def pass_on(self):
        if self.size != 4:
            return
        for copy, slot, first, then in ((0, 1, 0, 4), (1, 0, self.half, 5)):
            self.copies[copy].wait_recv()

            def step(i, carry):
                at = pl.ds(pl.multiple_of(first + i * 16, 16), 16)
                summed = self.sent[slot, at, self.columns].astype(F32) + self.got[2, at, self.columns].astype(F32)
                self.sent[slot, at, self.columns] = summed.astype(BF)
                return carry

            lax.fori_loop(0, self.half // 16, step, 0)
            self.copies[then].start()

    def wait(self):
        for copy in self.copies[2:] if self.size == 4 else self.copies:
            copy.wait_recv()


class Gather:
    def __init__(self, size, t, shared, every, sems, own_sem):
        rows = every.shape[0] // size
        half = rows // 2
        self.size = size
        self.own = pltpu.make_async_copy(shared, every.at[pl.ds(0, rows), :], own_sem)

        def chunk(k, side):
            return every.at[pl.ds(k * rows + side * half, half), :]

        def send(slot, source, target, partner):
            return remote(source, target, sems, slot, {"tensor": flip(t, partner)})

        if size == 4:
            self.copies = [send(2 * k + side, shared.at[pl.ds(side * half, half), :], chunk(k + 1, side), k + 1) for k in (0, 1) for side in (0, 1)]
            self.copies += [send(4, chunk(1, 0), chunk(3, 0), 2), send(5, chunk(2, 1), chunk(3, 1), 1)]
            self.ready = (self.copies[0:3:2], self.copies[3:0:-2])
        else:
            self.copies = [send(k - 1, shared, every.at[pl.ds(k * rows, rows), :], k) for k in range(1, size)]
            self.ready = ((), self.copies)

    def start(self, side):
        for copy in self.ready[side]:
            copy.start()
        if side:
            self.own.start()

    def pass_on(self):
        if self.size == 4:
            self.copies[0].wait_recv()
            self.copies[4].start()
            self.copies[3].wait_recv()
            self.copies[5].start()

    def wait(self):
        for at, copy in enumerate(self.copies):
            if self.size != 4 or at not in (0, 3):
                copy.wait_recv()
        self.own.wait()

    def end(self):
        for copy in self.copies:
            copy.wait_send()


def links_of(size):
    return 6 if size == 4 else size - 1


def start_kernel(size, chips, offsets, n_pair, *refs):
    tokens_ref, firsts, refs = refs[0], refs[1 : 1 + len(offsets)], refs[1 + len(offsets) :]
    turned_ref, gains_ref, pair, refs = refs[0], refs[1], refs[2 : 2 + n_pair], refs[2 + n_pair :]
    every, out, both, shard = refs[:4]
    line_refs, gather, coming, own_sem, keep_sem, whole, turned, out_sem = refs[4:10], refs[10:12], refs[12:14], *refs[14:19]
    t, c = lax.axis_index("tensor"), lax.axis_index("context")
    s = c // 2
    rows = shard.shape[0]
    piece = rows // chips
    own = firsts[0].shape[0]
    line = Line(chips, own, whole, line_refs[0:2], line_refs[2:4], line_refs[4:6])
    wait_others = meet(t, c, size, [1, *range(2, 2 * chips, 2)])
    kept = [
        pltpu.make_async_copy(first, whole.at[line.rows(s), pl.ds(offset, first.shape[1])], keep_sem.at[i])
        for i, (first, offset) in enumerate(zip(firsts, offsets))
    ]
    across = pair[0].shape[1]
    kept += [
        pltpu.make_async_copy(part, both.at[:, pl.ds(i * across, across)], keep_sem.at[len(offsets) + i]) for i, part in enumerate(pair)
    ]
    turned_copy = pltpu.make_async_copy(turned_ref, turned, keep_sem.at[len(offsets) + n_pair])
    for copy in [turned_copy, *kept]:
        copy.start()
    after_firsts = sum(first.shape[1] for first in firsts)
    height = turned.shape[0]
    turned_copy.wait()
    whole[line.rows(s), after_firsts : after_firsts + height] = turned[...].astype(F32).T.astype(BF)
    gains = jnp.concatenate([gains_ref[...].astype(F32), jnp.zeros((HD - gains_ref.shape[0], own), F32)], axis=0)
    whole[line.rows(s), after_firsts + height :] = gains.T.astype(BF)
    arrivals = [
        (tokens_ref.at[flip(s, j), pl.ds(pl.multiple_of(t * piece, piece), piece), :], shard.at[pl.ds(j * piece, piece), :])
        for j in range(chips)
    ]
    first = pltpu.make_async_copy(*arrivals[0], coming[0].at[0])
    others = [remote(*arrivals[j], coming, j, {"context": flip(c, 2 * j)}) for j in range(1, chips)]
    wait_others()
    for copy in [first, *others]:
        copy.start()
    for copy in kept:
        copy.wait()
    line.begin()
    first.wait()
    for copy in others:
        copy.wait_recv()
    share = Gather(size, t, shard, every, gather, own_sem)
    share.start(0)
    share.start(1)

    def write(k, way, chip):
        at = pl.ds(pl.multiple_of(chip * 2 * own, 2 * own), 2 * own)
        return pltpu.make_async_copy(whole.at[at, :], out.at[at, :], out_sem.at[0 if k < 0 else 1 + 2 * k + (way < 0)])

    def keep(k):
        line.other_core(k)
        line.each(line.gets, k, lambda k, way: write(k, way, s - way * (k + 1)).start())

    line.advance(0)
    line.other_core(-1)
    write(-1, 1, s).start()
    share.pass_on()
    for k in range(1, chips - 1):
        line.advance(k)
        keep(k - 1)
    share.wait()
    keep(chips - 2)
    line.end()
    share.end()
    for copy in others:
        copy.wait_send()
    write(-1, 1, s).wait()
    for k in range(chips - 1):
        line.each(line.gets, k, lambda k, way: write(k, way, s - way * (k + 1)).wait())


def start(tokens, firsts, turned, gains, pair, chips):
    size = lax.axis_size("tensor")
    seqs, local_len, width = tokens.shape
    rows = seqs * local_len // size
    own = firsts[0].shape[0]
    offsets, across = [], 0
    for first in firsts:
        offsets.append(across)
        across += first.shape[1]
    across += turned.shape[0] + HD
    dma = pltpu.SemaphoreType.DMA
    anywhere, in_vmem = pl.BlockSpec(memory_space=pl.ANY), pl.BlockSpec(memory_space=pltpu.VMEM)
    shape = jax.ShapeDtypeStruct
    return pl.pallas_call(
        functools.partial(start_kernel, size, chips, offsets, len(pair)),
        in_specs=[anywhere] * (2 + len(firsts)) + [in_vmem] + [anywhere] * len(pair),
        out_specs=[anywhere] * 2 + [in_vmem] * 2,
        out_shape=[
            shape((size * rows, width), BF),
            shape((2 * chips * own, across), BF),
            shape((own, sum(part.shape[1] for part in pair)), BF),
            shape((rows, width), BF),
        ],
        scratch_shapes=line_sems(chips)
        + [dma((links_of(size),))] * 2
        + [dma((chips,))] * 2
        + [dma, dma((len(firsts) + len(pair) + 1,))]
        + [pltpu.VMEM((2 * chips * own, across), BF), pltpu.VMEM(turned.shape, BF), dma((2 * chips - 1,))],
        compiler_params=pltpu.CompilerParams(vmem_limit_bytes=VMEM_LIMIT, collective_id=8, has_side_effects=True),
        cost_estimate=pl.CostEstimate(flops=0, bytes_accessed=300_000_000, transcendentals=0),
        name="start",
    )(tokens, *firsts, turned, gains, *pair)


def feed_kernel(size, chips, tile, *refs):
    h_ref, gate_up_w_ref, down_ref, cotangent_ref, residual_ref, gain_ref = refs[:6]
    every, slopes_ref, act_ref, down_all_ref, upstream, output, pieces, gain_rows = refs[6:14]
    h_buf, w_buf, act, down, sent, got, total, mine, stage = refs[14:23]
    h_sem, w_sem, stage_sem, keep_sem, own_sem = refs[23:28]
    line_refs, sums, gather, coming, going = refs[28:34], refs[34:36], refs[36:38], refs[38:40], refs[40:42]
    t, c = lax.axis_index("tensor"), lax.axis_index("context")
    s = c // 2
    rows, width = total.shape
    hidden = act.shape[1]
    own = down_ref.shape[0]
    piece = rows // chips
    tiles = hidden // tile
    order = [3, 1, 2, 0] if size == 4 else [*range(1, size), 0]
    line = Line(chips, own, down, line_refs[0:2], line_refs[2:4], line_refs[4:6])

    def h_copy(k):
        at = pl.ds(k * rows, rows)
        return pltpu.make_async_copy(h_ref.at[at, :], h_buf.at[at, :], h_sem.at[k])

    def w_copy(j, i):
        at = pl.ds(pl.multiple_of(i * hidden + j * tile, tile), tile)
        return pltpu.make_async_copy(gate_up_w_ref.at[:, at], w_buf.at[:, at], w_sem.at[j, i])

    own_rows = line.rows(s)
    own_down = pltpu.make_async_copy(down_ref, down.at[own_rows, :], keep_sem.at[0])
    own_down.start()
    wait_others = meet(t, c, size, [1, *range(2, 2 * chips, 2)])
    h_copy(order[0]).start()
    for j in range(tiles):
        for i in range(2):
            w_copy(j, i).start()
    for k in order[1:]:
        h_copy(k).start()
    gain_rows[...] = jnp.zeros_like(gain_rows)
    own_down.wait()
    wait_others()
    line.begin()

    def stage_copy(slot, i, k, j):
        at = pl.ds(pl.multiple_of(i * hidden + j * tile, tile), tile)
        return pltpu.make_async_copy(stage.at[slot, i], slopes_ref.at[pl.ds(k * rows, rows), at], stage_sem.at[slot, i])

    for n, k in enumerate(order):
        h_copy(k).wait()
        chunk = pl.ds(k * rows, rows)

        def step(j, carry):
            slot = (n * tiles + j) % 2
            if n == 0:
                for i in range(2):
                    w_copy(j, i).wait()

            @pl.when(n * tiles + j >= 2)
            def _():
                for i in range(2):
                    stage_copy(slot, i, k, j).wait()

            gate, up = [
                dot_nn(h_buf[chunk, :], w_buf[:, pl.ds(pl.multiple_of(i * hidden + j * tile, tile), tile)]) for i in range(2)
            ]
            logistic = jax.nn.sigmoid(gate)
            silu = gate * logistic
            act[chunk, pl.ds(pl.multiple_of(j * tile, tile), tile)] = (silu * up).astype(BF)
            stage[slot, 0] = (up * (logistic + silu * (1.0 - logistic))).astype(BF)
            stage[slot, 1] = silu.astype(BF)
            for i in range(2):
                stage_copy(slot, i, k, j).start()
            return carry

        lax.fori_loop(0, tiles, step, 0)
        if n + 1 == size // 2:
            line.advance(0, (0,))
        if n + 1 == size * 3 // 4:
            line.advance(0, (1,))
    for slot in range(2):
        for i in range(2):
            stage_copy(slot, i, 0, 0).wait()
    act_out = pltpu.make_async_copy(act, act_ref, keep_sem.at[1])
    act_out.start()

    rounds = []

    def fed_round(i):
        at = pl.ds(pl.multiple_of(flip(s, i) * 2 * own, 2 * own), 2 * own)
        group = Sums(size, t, sent, got, at, sums, links_of(size) * i)
        for k in order:
            value = dot_nt(act[k * rows : (k + 1) * rows, :], down[at, :])
            if k:
                sent[k - 1, :, at] = value.astype(BF)
                for copy in group.after_product[k]:
                    copy.start()
            else:
                total[:, at] = value
        rounds.append(group)

    line.other_core(-1)
    fed_round(0)
    line.other_core(0)
    fed_round(1)
    rounds[0].pass_on()
    rounds[1].pass_on()
    for k in range(1, chips - 1):
        line.advance(k)
        line.other_core(k)
        fed_round(k + 1)
        if k + 1 == chips - 1:
            arrivals = [
                (cotangent_ref.at[flip(s, j), pl.ds(pl.multiple_of(t * piece, piece), piece), :], upstream.at[pl.ds(j * piece, piece), :])
                for j in range(chips)
            ]
            first = pltpu.make_async_copy(*arrivals[0], coming[0].at[0])
            others = [remote(*arrivals[j], coming, j, {"context": flip(c, 2 * j)}) for j in range(1, chips)]
            for copy in [first, *others]:
                copy.start()
        rounds[k + 1].pass_on()
    down_out = pltpu.make_async_copy(down, down_all_ref, keep_sem.at[2])
    down_out.start()
    for group in rounds:
        group.wait()
    first.wait()
    for copy in others:
        copy.wait_recv()

    used = 2 if size == 4 else size - 1

    def finish_rows(side):
        def step(i, carry):
            at = pl.ds(pl.multiple_of(side * (rows // 2) + i * 16, 16), 16)
            fed = total[at, :]
            for other in range(used):
                fed = fed + got[other, at, :].astype(F32)
            factor = norm_factor(fed)
            output[at, :] = (residual_ref[at, :] + fed * factor * gain_ref[...]).astype(BF)
            grad, gains = norm_back(fed, factor, gain_ref[...], upstream[at, :].astype(F32))
            gain_rows[...] += gains[:8] + gains[8:]
            mine[at, :] = grad.astype(BF)
            return carry

        lax.fori_loop(0, rows // 32, step, 0)

    share = Gather(size, t, mine, every, gather, own_sem)
    finish_rows(0)
    share.start(0)
    finish_rows(1)
    share.start(1)
    kept = pltpu.make_async_copy(output.at[pl.ds(0, piece), :], pieces.at[0], going[0].at[0])
    gone = [
        remote(output.at[pl.ds(j * piece, piece), :], pieces.at[j], going, j, {"context": flip(c, 2 * j)})
        for j in range(1, chips)
    ]
    for copy in [kept, *gone]:
        copy.start()
    share.pass_on()
    share.wait()
    kept.wait()
    for copy in gone:
        copy.wait_recv()
    act_out.wait()
    down_out.wait()
    line.end()
    share.end()
    for copy in [*sum([group.copies for group in rounds], []), *others, *gone]:
        copy.wait_send()


def feed(hidden_low, gate_up_weight, down_shard, cotangent, residual, gain, chips):
    size = lax.axis_size("tensor")
    count, width = hidden_low.shape
    rows = count // size
    own, hidden = down_shard.shape
    ranks = 2 * chips
    tile = min(512, hidden)
    links = links_of(size)
    dma = pltpu.SemaphoreType.DMA
    anywhere, whole = pl.BlockSpec(memory_space=pl.ANY), pl.BlockSpec(memory_space=pltpu.VMEM)
    shape = jax.ShapeDtypeStruct
    return pl.pallas_call(
        functools.partial(feed_kernel, size, chips, tile),
        in_specs=[anywhere] * 4 + [whole] * 2,
        out_specs=[anywhere] * 4 + [whole] * 4,
        out_shape=[
            shape((count, width), BF),
            shape((count, 2 * hidden), BF),
            shape((count, hidden), BF),
            shape((ranks * own, hidden), BF),
            shape((rows, width), BF),
            shape((rows, width), BF),
            shape((chips, rows // chips, width), BF),
            shape((8, width), F32),
        ],
        scratch_shapes=[
            pltpu.VMEM((count, width), BF),
            pltpu.VMEM((width, 2 * hidden), BF),
            pltpu.VMEM((count, hidden), BF),
            pltpu.VMEM((ranks * own, hidden), BF),
            pltpu.VMEM((size - 1, rows, width), BF),
            pltpu.VMEM((size - 1, rows, width), BF),
            pltpu.VMEM((rows, width), F32),
            pltpu.VMEM((rows, width), BF),
            pltpu.VMEM((2, 2, rows, tile), BF),
            dma((size,)),
            dma((hidden // tile, 2)),
            dma((2, 2)),
            dma((3,)),
            dma,
        ]
        + line_sems(chips)
        + [dma((links * chips,))] * 2
        + [dma((links,))] * 2
        + [dma((chips,))] * 4,
        compiler_params=pltpu.CompilerParams(vmem_limit_bytes=VMEM_LIMIT, collective_id=2, has_side_effects=True),
        cost_estimate=pl.CostEstimate(flops=6 * count * width * hidden, bytes_accessed=400_000_000, transcendentals=count * hidden),
        name="feed",
    )(hidden_low, gate_up_weight, down_shard, cotangent, residual, gain)


def turn(values, cosine, sine):
    heads = [values[:, i : i + HD] for i in range(0, values.shape[1], HD)]
    return jnp.concatenate([head * cosine + pltpu.roll(head, HD // 2, 1) * sine for head in heads], axis=1)


def turn_kernel(core_ref, raw_ref, column_ref, gain_ref, cosine_ref, sine_ref, keep_ref, send_ref):
    width = gain_ref.shape[1]
    half = width // 2
    cosine, sine = cosine_ref[...], sine_ref[...]
    first = core_ref[0] == 0
    for i in range(3):
        values = raw_ref[:, i * width : (i + 1) * width]
        if i < 2:
            values = turn(values * column_ref[:, i : i + 1] * gain_ref[i : i + 1, :], cosine, sine)
        low, high = values[:, :half].astype(BF), values[:, half:].astype(BF)
        keep_ref[i] = jnp.where(first, low, high)
        send_ref[i] = jnp.where(first, high, low)


def head_grads(core_ref, own_ref, other_ref, i):
    first = core_ref[0] == 0
    own, other = own_ref[i], other_ref[i]
    return jnp.concatenate([jnp.where(first, own, other), jnp.where(first, other, own)], axis=1).astype(F32)


def inner_kernel(core_ref, own_ref, other_ref, raw_ref, column_ref, gain_ref, cosine_ref, sine_ref, inner_ref, gains_ref):
    width = gain_ref.shape[1]
    cosine, sine = cosine_ref[...], -sine_ref[...]

    @pl.when(pl.program_id(0) == 0)
    def _():
        gains_ref[...] = jnp.zeros_like(gains_ref)

    for i in range(2):
        flat = turn(head_grads(core_ref, own_ref, other_ref, i), cosine, sine) * raw_ref[:, i * width : (i + 1) * width]
        inner_ref[i] = lax.dot_general(
            jnp.ones((8, width), F32),
            flat * gain_ref[i : i + 1, :],
            (((1,), (1,)), ((), ())),
            precision=lax.Precision.HIGHEST,
            preferred_element_type=F32,
        )
        flat = flat * column_ref[:, i : i + 1]
        gains_ref[i] += jnp.sum(flat.reshape(-1, 8, width), axis=0)


def raw_grad_kernel(core_ref, own_ref, other_ref, raw_ref, column_ref, gain_ref, cosine_ref, sine_ref, out_ref):
    width = gain_ref.shape[1]
    cosine, sine = cosine_ref[...], -sine_ref[...]
    for i in range(3):
        values = head_grads(core_ref, own_ref, other_ref, i)
        if i < 2:
            values = turn(values, cosine, sine) * column_ref[:, i : i + 1] * gain_ref[i : i + 1, :]
            values = values - raw_ref[:, i * width : (i + 1) * width] * column_ref[:, i + 2 : i + 3]
        out_ref[:, i * width : (i + 1) * width] = values.astype(BF)


def by_rows(kernel, name, core, ins, outs, rows=256):
    def spec(shape, dim):
        block = tuple(rows if i == dim else extent for i, extent in enumerate(shape))
        return pl.BlockSpec(block, lambda i, core: tuple(i if at == dim else 0 for at in range(len(shape))))

    count = next(out[0][dim] for *out, dim in outs if dim is not None)
    return pl.pallas_call(
        kernel,
        grid_spec=pltpu.PrefetchScalarGridSpec(
            num_scalar_prefetch=1,
            grid=(count // rows,),
            in_specs=[spec((array.shape[0], count, array.shape[2]) if dim == 1 else array.shape, dim) for array, dim in ins],
            out_specs=[spec(shape, dim) for shape, _, dim in outs],
        ),
        out_shape=[jax.ShapeDtypeStruct(shape, dtype) for shape, dtype, _ in outs],
        compiler_params=pltpu.CompilerParams(vmem_limit_bytes=VMEM_LIMIT),
        name=name,
    )(core[None].astype(jnp.int32), *[array for array, _ in ins])


def act_back_kernel(tile, grad_ref, w_ref, slopes_ref, out_ref):
    hidden = w_ref.shape[1]
    for j in range(0, hidden, tile):
        act_grad = dot_nn(grad_ref[...], w_ref[:, j : j + tile])
        for at in (j, hidden + j):
            out_ref[:, at : at + tile] = (act_grad * slopes_ref[:, at : at + tile].astype(F32)).astype(BF)


def act_back(fed_low, w_down, slopes):
    count, width = fed_low.shape
    hidden = w_down.shape[1]
    rows = 256
    return pl.pallas_call(
        functools.partial(act_back_kernel, 512),
        grid=(count // rows,),
        in_specs=[
            pl.BlockSpec((rows, width), lambda i: (i, 0)),
            pl.BlockSpec((width, hidden), lambda i: (0, 0)),
            pl.BlockSpec((rows, 2 * hidden), lambda i: (i, 0)),
        ],
        out_specs=pl.BlockSpec((rows, 2 * hidden), lambda i: (i, 0)),
        out_shape=jax.ShapeDtypeStruct((count, 2 * hidden), BF),
        compiler_params=pltpu.CompilerParams(vmem_limit_bytes=VMEM_LIMIT),
        cost_estimate=pl.CostEstimate(flops=2 * count * width * hidden, bytes_accessed=40_000_000, transcendentals=count * hidden),
        name="act_back",
    )(fed_low, w_down, slopes)


def rank_sums_kernel(chips, size, tile, count, carries, *refs):
    lefts, rights, refs = refs[:count], refs[count : 2 * count], refs[2 * count :]
    if carries:
        carried_ref, out_ref, every_ref, *refs = refs
    else:
        out_ref, *refs = refs
    left_bufs, right_bufs = refs[:count], refs[count : 2 * count]
    passed, got, out, left_sem, right_sem, out_sem, sent_sem, got_sem = refs[2 * count : 2 * count + 8]
    t, c = lax.axis_index("tensor"), lax.axis_index("context")
    core = c % 2
    own = out.shape[1]
    blocks = [(j, core_at) for core_at in (1, 0) for j in range(chips)]

    def left_copy(i, j, core_at):
        rank = 2 * j + (core if core_at == 0 else 1 - core)
        at = pl.ds(pl.multiple_of(rank * own, own), own)
        block = left_bufs[i].at[core_at * chips + j]
        return pltpu.make_async_copy(lefts[i].at[:, at], block, left_sem.at[i, core_at * chips + j])

    tiles = [right.shape[1] // tile for right in rights]

    def right_copy(i, n):
        at = pl.ds(pl.multiple_of(n * tile, tile), tile)
        return pltpu.make_async_copy(rights[i].at[:, at], right_bufs[i].at[:, at], right_sem.at[i, n])

    wait_others = meet(t, c, size if carries else 1, [1])
    for i in range(count):
        left_copy(i, *blocks[0]).start()
        for n in range(tiles[i]):
            right_copy(i, n).start()
        for block in blocks[1:]:
            left_copy(i, *block).start()
    wait_others()
    if carries:
        sent_out, got_out, own_sem = refs[2 * count + 8 :]
        part = carried_ref.at[pl.ds(carries[0], carries[1]), :]
        share = Gather(size, t, part, every_ref, (sent_out, got_out), own_sem)
        share.start(0)
        share.start(1)
    def send(j):
        return remote(passed.at[j], got.at[j], (sent_sem, got_sem), j, {"context": flip(c, 1)})

    def write(j):
        return pltpu.make_async_copy(out.at[j], out_ref.at[pl.ds(pl.multiple_of(j * own, own), own), :], out_sem.at[j])

    def block(core_at, j, carry):
        base = 0
        if core_at == 0:
            send(j).wait_recv()
        for i in range(count):
            left_copy(i, j, core_at).wait()
            left = left_bufs[i][core_at * chips + j].T
            for n in range(tiles[i]):
                if core_at:
                    pl.when(j == 0)(right_copy(i, n).wait)
                to = slice(base + n * tile, base + (n + 1) * tile)
                part = dot_nn(left, right_bufs[i][:, n * tile : (n + 1) * tile])
                if core_at:
                    passed[j, :, to] = part.astype(BF)
                else:
                    out[j, :, to] = (part + got[j, :, to].astype(F32)).astype(BF)
            base += tiles[i] * tile
        (send if core_at else write)(j).start()
        if carries and core_at == 0:
            pl.when(j == 1)(share.pass_on)
        return carry

    lax.fori_loop(0, chips, functools.partial(block, 1), 0)
    lax.fori_loop(0, chips, functools.partial(block, 0), 0)
    for j in range(chips):
        send(j).wait_send()
        write(j).wait()
    if carries:
        share.wait()
        share.end()


def rank_sums(number, pairs, own, carried=None):
    size = lax.axis_size("tensor")
    lefts, rights = [left for left, _ in pairs], [right for _, right in pairs]
    count, width = lefts[0].shape
    chips = width // (2 * own)
    across = sum(right.shape[1] for right in rights)
    tile = min(512, *[right.shape[1] for right in rights])
    most = max(right.shape[1] for right in rights) // tile
    more = [] if carried is None else [carried[0]]
    dma = pltpu.SemaphoreType.DMA
    return pl.pallas_call(
        functools.partial(rank_sums_kernel, chips, size, tile, len(pairs), carried and carried[1:]),
        in_specs=[pl.BlockSpec(memory_space=pl.ANY)] * (2 * len(pairs) + len(more)),
        out_specs=[pl.BlockSpec(memory_space=pl.ANY)] * (1 + len(more)),
        out_shape=[jax.ShapeDtypeStruct((chips * own, across), BF)]
        + [jax.ShapeDtypeStruct((size * carried[2], rows.shape[1]), BF) for rows in more],
        scratch_shapes=[pltpu.VMEM((2 * chips, count, own), BF)] * len(pairs)
        + [pltpu.VMEM(right.shape, BF) for right in rights]
        + [pltpu.VMEM((chips, own, across), BF)] * 3
        + [dma((len(pairs), 2 * chips)), dma((len(pairs), most)), dma((chips,)), dma((chips,)), dma((chips,))]
        + [dma((links_of(size),)), dma((links_of(size),)), dma] * len(more),
        compiler_params=pltpu.CompilerParams(vmem_limit_bytes=VMEM_LIMIT, collective_id=number, has_side_effects=True),
        cost_estimate=pl.CostEstimate(flops=2 * count * width * across, bytes_accessed=60_000_000, transcendentals=0),
        name="rank_sums",
    )(*lefts, *rights, *more)


def columns_of(*values):
    stacked = jnp.stack(values, axis=1)
    return jnp.pad(stacked, ((0, 0), (0, 8 - len(values))))


def in_order(at_ref, source, target, piece, other=None):
    rows = source.shape[0]

    def step(p, carry):
        start = at_ref[p]
        at = pl.ds(pl.multiple_of(start % rows, piece), piece)
        values = source[at, :]
        if other is not None:
            values = jnp.where(start < rows, values, other[at, :])
        target[pl.ds(pl.multiple_of(p * piece, piece), piece), :] = values
        return carry

    lax.fori_loop(0, target.shape[0] // piece, step, 0)


def out_of_order(at_ref, source, target, piece):
    def step(p, carry):
        start = pl.multiple_of(at_ref[p], piece)
        target[pl.ds(start, piece), :] = source[pl.ds(pl.multiple_of(p * piece, piece), piece), :].astype(target.dtype)
        return carry

    lax.fori_loop(0, source.shape[0] // piece, step, 0)


def causal(tile):
    key_at = lax.broadcasted_iota(jnp.int32, (tile, tile), 0)
    query_at = lax.broadcasted_iota(jnp.int32, (tile, tile), 1)
    return query_at >= key_at


def attend_kernel(piece, tile, at_ref, own_ref, other_ref, out_ref, log_ref, query, key, value, value_t, mixed):
    for slot, held in enumerate((query, key, value)):
        in_order(at_ref, own_ref.at[slot], held, piece, other_ref.at[slot])
    value_t[...] = value[...].astype(F32).T.astype(BF)
    allowed = causal(tile)
    for i in range(query.shape[0] // tile):
        low, high = i * tile, (i + 1) * tile
        rows = query[low:high, :]
        near = jnp.where(allowed, dot_nt(key[low:high, :], rows) * HD ** (-0.5), -1e30)
        top = jnp.max(near, axis=0, keepdims=True)
        if i:
            far = dot_nt(key[0:low, :], rows) * HD ** (-0.5)
            top = jnp.maximum(top, jnp.max(far, axis=0, keepdims=True))
        near = jnp.exp(near - top)
        total = jnp.sum(near, axis=0, keepdims=True)
        summed = dot_nn(value_t[:, low:high], near.astype(BF))
        if i:
            far = jnp.exp(far - top)
            total = total + jnp.sum(far, axis=0, keepdims=True)
            summed = summed + dot_nn(value_t[:, 0:low], far.astype(BF))
        mixed[low:high, :] = (summed / total).T
        log_ref[0, :, low:high] = top + jnp.log(total)
    out_of_order(at_ref, mixed, out_ref, piece)


def attend(own, other, at, piece):
    half, width = own.shape[1:]
    rows = 2 * half
    heads = width // HD
    return pl.pallas_call(
        functools.partial(attend_kernel, piece, 256),
        grid_spec=pltpu.PrefetchScalarGridSpec(
            num_scalar_prefetch=1,
            grid=(heads,),
            in_specs=[pl.BlockSpec((3, half, HD), lambda h, at: (0, 0, h))] * 2,
            out_specs=[
                pl.BlockSpec((rows, HD), lambda h, at: (0, h)),
                pl.BlockSpec((1, 1, rows), lambda h, at: (h, 0, 0)),
            ],
            scratch_shapes=[pltpu.VMEM((rows, HD), BF)] * 3 + [pltpu.VMEM((HD, rows), BF), pltpu.VMEM((rows, HD), F32)],
        ),
        out_shape=[jax.ShapeDtypeStruct((rows, width), BF), jax.ShapeDtypeStruct((heads, 1, rows), F32)],
        compiler_params=pltpu.CompilerParams(vmem_limit_bytes=VMEM_LIMIT),
        cost_estimate=pl.CostEstimate(
            flops=2 * 2 * heads * rows * rows * HD, bytes_accessed=8 * rows * width, transcendentals=heads * rows * rows // 2
        ),
        name="attend",
    )(at, own, other)


def attend_back_kernel(
    piece, tile, at_ref, own_ref, other_ref, out_ref, grad_ref, log_ref, dqkv_ref, query, key, value, key_t, grad, mixed, dquery, dkey, dvalue
):
    for slot, held in enumerate((query, key, value)):
        in_order(at_ref, own_ref.at[slot], held, piece, other_ref.at[slot])
    in_order(at_ref, grad_ref, grad, piece)
    in_order(at_ref, out_ref, mixed, piece)
    key_t[...] = key[...].astype(F32).T.astype(BF)
    allowed = causal(tile)
    dkey[...] = jnp.zeros_like(dkey)
    dvalue[...] = jnp.zeros_like(dvalue)
    scale = HD ** (-0.5)
    for i in range(query.shape[0] // tile):
        low, high = i * tile, (i + 1) * tile
        rows = query[low:high, :]
        rows_grad = grad[low:high, :]
        log = log_ref[0, :, low:high]
        spread = jnp.sum((rows_grad.astype(F32) * mixed[low:high, :].astype(F32)).T, axis=0, keepdims=True)
        dquery_t = None
        for start, stop, masked in ((0, low, False), (low, high, True)):
            if start == stop:
                continue
            scores = dot_nt(key[start:stop, :], rows) * scale
            if masked:
                scores = jnp.where(allowed, scores, -1e30)
            probs = jnp.exp(scores - log)
            probs_grad = dot_nt(value[start:stop, :], rows_grad)
            scores_grad = (probs * (probs_grad - spread)).astype(BF)
            dvalue[start:stop, :] += dot_nn(probs.astype(BF), rows_grad)
            dkey[start:stop, :] += dot_nn(scores_grad, rows)
            term = dot_nn(key_t[:, start:stop], scores_grad)
            dquery_t = term if dquery_t is None else dquery_t + term
        dquery[low:high, :] = dquery_t.T * scale
    dkey[...] = dkey[...] * scale
    for slot, held in enumerate((dquery, dkey, dvalue)):
        out_of_order(at_ref, held, dqkv_ref.at[slot], piece)


def attend_back(own, other, out, grad, log, at, piece):
    half, width = own.shape[1:]
    rows = 2 * half
    heads = width // HD
    return pl.pallas_call(
        functools.partial(attend_back_kernel, piece, 256),
        grid_spec=pltpu.PrefetchScalarGridSpec(
            num_scalar_prefetch=1,
            grid=(heads,),
            in_specs=[
                pl.BlockSpec((3, half, HD), lambda h, at: (0, 0, h)),
                pl.BlockSpec((3, half, HD), lambda h, at: (0, 0, h)),
                pl.BlockSpec((rows, HD), lambda h, at: (0, h)),
                pl.BlockSpec((rows, HD), lambda h, at: (0, h)),
                pl.BlockSpec((1, 1, rows), lambda h, at: (h, 0, 0)),
            ],
            out_specs=pl.BlockSpec((3, rows, HD), lambda h, at: (0, 0, h)),
            scratch_shapes=[pltpu.VMEM((rows, HD), BF)] * 3
            + [pltpu.VMEM((HD, rows), BF)]
            + [pltpu.VMEM((rows, HD), BF)] * 2
            + [pltpu.VMEM((rows, HD), F32)] * 3,
        ),
        out_shape=jax.ShapeDtypeStruct((3, rows, width), BF),
        compiler_params=pltpu.CompilerParams(vmem_limit_bytes=VMEM_LIMIT),
        cost_estimate=pl.CostEstimate(
            flops=5 * heads * rows * rows * HD * 2, bytes_accessed=16 * rows * width, transcendentals=heads * rows * rows // 2
        ),
        name="attend_back",
    )(at, own, other, out, grad, log)


def local(
    tokens,
    block_order,
    query_weight,
    key_weight,
    value_weight,
    output_weight,
    gate_weight,
    up_weight,
    down_weight,
    query_gain,
    key_gain,
    attention_gain,
    forward_gain,
    cotangent,
):
    seqs, local_len, width = tokens.shape
    ranks = lax.axis_size("context")
    columns = lax.axis_size("tensor")
    full_len = local_len * ranks
    piece_len = full_len // block_order.shape[0]
    piece = local_len // columns
    shard_rows = seqs * piece
    count = shard_rows * columns
    context = lax.axis_index("context")
    t = lax.axis_index("tensor")
    s, core = context // 2, context % 2
    head_width = query_weight.shape[1]
    half_width = head_width // 2
    hidden_width = gate_weight.shape[1]

    rows, w_first, gate_up_shard, row_shard = start(
        tokens,
        [query_weight, key_weight, value_weight],
        output_weight,
        jnp.stack([attention_gain, forward_gain]),
        [gate_weight, up_weight],
        seqs,
    )
    qkv_width = 3 * head_width
    gains = w_first[:, 4 * head_width :]
    gain_attn, gain_feed = gains[:, 0].astype(F32)[None], gains[:, 1].astype(F32)[None]
    w_gate_up = lax.all_gather(gate_up_shard, "context", axis=0, tiled=True)

    chips = s ^ jnp.arange(seqs, dtype=jnp.int32)
    shards = t ^ jnp.arange(columns, dtype=jnp.int32)
    starts = (2 * chips[None, :] + core) * local_len + shards[:, None] * piece
    stored = (starts[:, :, None] + jnp.arange(piece, dtype=jnp.int32)).reshape(count)
    block = stored // piece_len
    slots = jnp.arange(block_order.shape[0], dtype=jnp.int32)
    place = jnp.sum(jnp.where(block[:, None] == slots[None, :], block_order[None, :], 0), axis=1) * piece_len
    place = place + stored % piece_len
    freq = THETA ** (-jnp.arange(0, HD, 2, dtype=F32) / HD)
    angle = place.astype(F32)[:, None] * freq[None, :]
    cosine = jnp.concatenate([jnp.cos(angle), jnp.cos(angle)], axis=-1)
    sine = jnp.concatenate([-jnp.sin(angle), jnp.sin(angle)], axis=-1)
    per_block = piece_len // piece
    pieces = jnp.arange(full_len // piece, dtype=jnp.int32)
    hits = block_order[None, :] == (pieces // per_block)[:, None]
    block_at = jnp.sum(jnp.where(hits, slots[None, :], 0), axis=1)
    piece_at = block_at * per_block + pieces % per_block
    rank_of, shard_of = piece_at // columns, piece_at % columns
    at = (((rank_of % 2) ^ core) * columns + (shard_of ^ t)) * seqs + ((rank_of // 2) ^ s)
    at = (at * piece).astype(jnp.int32)

    qkv_raw = dot_nn(rows, w_first[:, :qkv_width])
    query_raw = qkv_raw[:, :head_width]
    key_raw = qkv_raw[:, head_width : 2 * head_width]
    totals = sum_over_tensor(jnp.stack([jnp.sum(query_raw * query_raw, axis=1), jnp.sum(key_raw * key_raw, axis=1)]))
    factors = lax.rsqrt(totals / width + EPS)
    scaling = jnp.stack([query_gain, key_gain]).astype(F32)
    keep, send = by_rows(
        turn_kernel,
        "turn",
        core,
        [(qkv_raw, 0), (columns_of(*factors), 0), (scaling, None), (cosine, 0), (sine, 0)],
        [((3, count, half_width), BF, 1)] * 2,
    )
    received = swap(send, "context", 1)
    mixed_heads, log = attend(keep, received, at, piece)

    def to_heads(values):
        keep = lax.dynamic_slice_in_dim(values, core * half_width, half_width, axis=1)
        send = lax.dynamic_slice_in_dim(values, (1 - core) * half_width, half_width, axis=1)
        return jnp.concatenate([keep, swap(send, "context", 1)], axis=0)

    def to_rows(values):
        own, other = values[:count], swap(values[count:], "context", 1)
        return jnp.concatenate([jnp.where(core == 0, own, other), jnp.where(core == 0, other, own)], axis=1)

    mixed_low = to_rows(mixed_heads)

    def chunk(values, k):
        return values[k * shard_rows : (k + 1) * shard_rows]

    order = list(range(columns))
    shard = (shard_rows, width)
    hidden_low, attended, hidden = exchange(
        "attended", 1, mixed_low, w_first, finish_attended, [row_shard, gain_attn], [(shard, F32), (shard, F32)], offset=qkv_width
    )

    fed_low, slopes, act_low, w_down, upstream, _, output_pieces, feed_gain_rows = feed(
        hidden_low, w_gate_up, down_weight.T, cotangent, hidden, gain_feed, seqs
    )

    own = width // ranks
    cores = [list(range(0, ranks, 2)), list(range(1, ranks, 2))]

    def scatter(values):
        return lax.psum_scatter(values, "context", scatter_dimension=0, axis_index_groups=cores, tiled=True)

    output_pieces = output_pieces.reshape(shard)
    split = seqs // 4 * piece
    down_part, first_rows = rank_sums(5, [(fed_low, act_low)], own, (output_pieces, 0, split))
    down_summed = scatter(down_part)
    down_grad = down_summed.astype(F32).T
    gate_up_low = act_back(after(fed_low, down_part), w_down, slopes)
    gate_up_part, other_rows = rank_sums(6, [(hidden_low, gate_up_low)], own, (output_pieces, split, shard_rows - split))
    layer_output = in_place([values.reshape(columns, -1, piece, width) for values in (first_rows, other_rows)], s, t, BF)
    gate_up_summed = scatter(gate_up_part)
    gate_up_low = after(gate_up_low, gate_up_part)
    attended_low, hidden_grad, attn_gain_rows = exchange(
        "hidden_grad",
        3,
        gate_up_low,
        w_gate_up,
        finish_hidden_grad,
        [attended, upstream, gain_attn],
        [(shard, F32), ((8, width), F32)],
    )
    attended_low = after(attended_low, layer_output)
    mixed_grad = dot_nn(attended_low, w_first[:, qkv_width : 4 * head_width]).astype(BF)
    dqkv = attend_back(keep, received, mixed_heads, to_heads(mixed_grad), log, at, piece)
    dqkv_other = swap(dqkv[:, count:], "context", 1)
    inner, head_gain_rows = by_rows(
        inner_kernel,
        "inner",
        core,
        [(dqkv, 1), (dqkv_other, 1), (qkv_raw, 0), (columns_of(*factors), 0), (scaling, None), (cosine, 0), (sine, 0)],
        [((2, 8, count), F32, 2), ((2, 8, head_width), F32, None)],
    )
    inner = sum_over_tensor(inner[:, 0])
    (qkv_low,) = by_rows(
        raw_grad_kernel,
        "raw_grad",
        core,
        [
            (dqkv, 1),
            (dqkv_other, 1),
            (qkv_raw, 0),
            (after(columns_of(*factors, *(inner * factors**3 / width)), down_grad), 0),
            (scaling, None),
            (cosine, 0),
            (sine, 0),
        ],
        [((count, 3 * head_width), BF, 0)],
    )
    (qkv_part,) = rank_sums(7, [(rows, qkv_low), (attended_low, mixed_low)], own)
    qkv_out_summed = scatter(after(qkv_part, gate_up_summed, down_summed))
    every, width_gains, head_gains = exchange(
        "tokens_grad",
        4,
        after(qkv_low, qkv_part),
        w_first,
        None,
        [hidden_grad, attn_gain_rows, feed_gain_rows, head_gain_rows.reshape(16, head_width)],
        [((8, own), F32), ((8, head_width), F32)],
        chips=seqs,
        last=True,
    )
    tokens_grad = in_place([every.reshape(columns, seqs, piece, width)], s, t, F32)

    gate_up_summed, qkv_out_summed = gate_up_summed.astype(F32), qkv_out_summed.astype(F32)
    return (
        layer_output,
        tokens_grad,
        qkv_out_summed[:, :head_width],
        qkv_out_summed[:, head_width : 2 * head_width],
        qkv_out_summed[:, 2 * head_width : 3 * head_width],
        qkv_out_summed[:, 3 * head_width :].T,
        gate_up_summed[:, :hidden_width],
        gate_up_summed[:, hidden_width:],
        down_grad,
        head_gains[0],
        head_gains[1],
        width_gains[0],
        width_gains[1],
    )


def solution(mesh):
    return jax.shard_map(
        local,
        mesh=mesh,
        in_specs=(
            P(None, "context", None),
            P(),
            P("context", "tensor"),
            P("context", "tensor"),
            P("context", "tensor"),
            P("tensor", "context"),
            P("context", "tensor"),
            P("context", "tensor"),
            P("tensor", "context"),
            P("tensor"),
            P("tensor"),
            P("context"),
            P("context"),
            P(None, "context", None),
        ),
        out_specs=(
            P(None, "context", None),
            P(None, "context", None),
            P("context", "tensor"),
            P("context", "tensor"),
            P("context", "tensor"),
            P("tensor", "context"),
            P("context", "tensor"),
            P("context", "tensor"),
            P("tensor", "context"),
            P("tensor"),
            P("tensor"),
            P("context"),
            P("context"),
        ),
        check_vma=False,
    )
```

```python
import functools

import jax
import jax.numpy as jnp
from jax import lax
from jax.experimental import pallas as pl
from jax.experimental.pallas import tpu as pltpu
from jax.sharding import PartitionSpec as P

HD = 128
EPS = 1e-06
THETA = 500000.0
BF = jnp.bfloat16
F32 = jnp.float32
VMEM_LIMIT = 60 * 1024 * 1024
MESH = pl.DeviceIdType.MESH


def dot_nn(left, right):
    return jnp.dot(left, right, preferred_element_type=F32)


def dot_nt(left, right):
    return lax.dot_general(left, right, (((1,), (1,)), ((), ())), preferred_element_type=F32)


def after(values, *others):
    return lax.optimization_barrier((values, *others))[0]


def swap(values, axis, mask):
    size = lax.axis_size(axis)
    return lax.ppermute(values, axis, [(i, i ^ mask) for i in range(size)])


def sum_over_tensor(values):
    size = lax.axis_size("tensor")
    chunks = values.reshape(values.shape[0], size, -1)
    total = chunks
    for m in range(1, size):
        other = swap(chunks, "tensor", m)
        total = total + jnp.stack([other[:, m ^ k] for k in range(size)], axis=1)
    return total.reshape(values.shape)


def place_kernel(at_ref, *refs):
    out_ref = refs[-1]
    for a in range(out_ref.shape[0]):
        at, base, values = a ^ at_ref[0], 0, None
        for ref in refs[:-1]:
            count = ref.shape[1]
            part = ref[0, jnp.clip(at - base, 0, count - 1)]
            values = part if values is None else jnp.where(at >= base, part, values)
            base += count
        out_ref[a, 0] = values.astype(out_ref.dtype)


def in_place(parts, s, t, dtype):
    size, _, piece, width = parts[0].shape
    seqs = sum(part.shape[1] for part in parts)
    full = pl.pallas_call(
        place_kernel,
        grid_spec=pltpu.PrefetchScalarGridSpec(
            num_scalar_prefetch=1,
            grid=(size,),
            in_specs=[pl.BlockSpec((1, *part.shape[1:]), lambda b, at: (b ^ at[1], 0, 0, 0)) for part in parts],
            out_specs=pl.BlockSpec((seqs, 1, piece, width), lambda b, at: (0, b, 0, 0)),
        ),
        out_shape=jax.ShapeDtypeStruct((seqs, size, piece, width), dtype),
        name="place_rows",
    )(jnp.stack([s, t]).astype(jnp.int32), *parts)
    return full.reshape(seqs, size * piece, width)


def norm_factor(values):
    return lax.rsqrt(jnp.mean(values * values, axis=-1, keepdims=True) + EPS)


def norm_back(values, factor, gain, grad):
    scaled = grad * gain
    inner = jnp.mean(values * scaled, axis=-1, keepdims=True)
    return factor * scaled - values * (factor**3 * inner), grad * values * factor


def flip(index, mask):
    bit = 1
    result = index
    while bit <= mask:
        if mask & bit:
            result = result + bit - 2 * bit * ((index // bit) % 2)
        bit *= 2
    return result


def exchange_kernel(size, width, depth, offset, tile, finish, chips, last, n_in, n_out, a_ref, w_ref, *refs):
    ins, rest = refs[:n_in], refs[n_in:]
    every, outs, rest = rest[0], rest[1 : 1 + n_out], rest[1 + n_out :]
    a_buf, w_buf, sent, got, total, mine, a_sem, w_sem, sent_sem, got_sem, out_sem, in_sem, own_sem = rest[:13]
    t = lax.axis_index("tensor")
    c = lax.axis_index("context")
    rows = total.shape[0]
    half = rows // 2

    def a_copy(k):
        at = pl.ds(k * rows, rows)
        return pltpu.make_async_copy(a_ref.at[at, :], a_buf.at[at, :], a_sem.at[k])

    def w_copy(j):
        at = pl.ds(pl.multiple_of(j * tile, tile), tile)
        return pltpu.make_async_copy(w_ref.at[at, pl.ds(offset, depth)], w_buf.at[at, :], w_sem.at[j])

    order = [3, 1, 2, 0] if size == 4 else [*range(1, size), 0]
    tiles = width // tile
    parts = tiles if size == 4 else 1
    across = width // parts
    a_copy(order[0]).start()
    for j in range(tiles):
        w_copy(j).start()
    for k in order[1:]:
        a_copy(k).start()
    barrier = pltpu.get_barrier_semaphore()
    for k in range(1, size):
        pl.semaphore_signal(barrier, inc=1, device_id={"tensor": flip(t, k)}, device_id_type=MESH)

    met = range(1, 2 * chips) if last else range(2, 2 * chips, 2)
    for mask in met:
        pl.semaphore_signal(barrier, inc=1, device_id={"context": flip(c, mask)}, device_id_type=MESH)
    for out in outs:
        if out.shape[0] == 8:
            out[...] = jnp.zeros_like(out)

    def cross(j, source, target, sems, base=0):
        if j == 0:
            return pltpu.make_async_copy(source, target, sems[0].at[base])
        return pltpu.make_async_remote_copy(
            src_ref=source,
            dst_ref=target,
            send_sem=sems[0].at[base + j],
            recv_sem=sems[1].at[base + j],
            device_id={"context": flip(c, 2 * j)},
            device_id_type=MESH,
        )

    def send(slot, source, target, partner, sems):
        return pltpu.make_async_remote_copy(
            src_ref=source,
            dst_ref=target,
            send_sem=sems[0].at[slot],
            recv_sem=sems[1].at[slot],
            device_id={"tensor": flip(t, partner)},
            device_id_type=MESH,
        )

    def product(k, first=False, part=0):
        if part == 0:
            a_copy(k).wait()

        def step(j, carry):
            if first:
                w_copy(j).wait()
            at = pl.ds(pl.multiple_of(j * tile, tile), tile)
            value = dot_nt(a_buf[k * rows : (k + 1) * rows, :], w_buf[at, :])
            if k:
                sent[k - 1, :, at] = value.astype(BF)
            else:
                total[:, at] = value
            return carry

        lax.fori_loop(part * tiles // parts, (part + 1) * tiles // parts, step, 0)

    def add(slot, other, first, columns):
        def step(i, carry):
            at = pl.ds(pl.multiple_of(first + i * 16, 16), 16)
            sent[slot, at, columns] = (sent[slot, at, columns].astype(F32) + got[other, at, columns].astype(F32)).astype(BF)
            return carry

        lax.fori_loop(0, half // 16, step, 0)

    def columns_of_part(part):
        return pl.ds(part * across, across)

    low, high = pl.ds(0, half), pl.ds(half, half)
    sums = (sent_sem, got_sem)
    product(order[0], first=True)
    pl.semaphore_wait(barrier, size - 1 + len(met))
    piece = rows // max(1, chips)
    crossing = []
    small = []
    if last:
        gain_rows, head_rows, gain_got, head_got, own_got, small_sent, small_got = rest[18:]
        attn_rows, feed_rows, two_heads = ins[1:]
        gain_rows[...] = jnp.zeros_like(gain_rows)
        head_rows[...] = jnp.zeros_like(head_rows)
        for i, part in enumerate((attn_rows, feed_rows)):
            gain_rows[i : i + 1, :] = jnp.sum(part[...], axis=0, keepdims=True)
            head_rows[i : i + 1, :] = jnp.sum(two_heads[8 * i : 8 * i + 8, :], axis=0, keepdims=True)
        own_width = outs[0].shape[1]

        def tell(source, target, device):
            copy = pltpu.make_async_remote_copy(
                src_ref=source,
                dst_ref=target,
                send_sem=small_sent.at[len(small)],
                recv_sem=small_got.at[len(small)],
                device_id=device,
                device_id_type=MESH,
            )
            copy.start()
            small.append(copy)

        for k in range(1, size):
            tell(gain_rows, gain_got.at[k - 1], {"tensor": flip(t, k)})
        for mask in met:
            tell(head_rows, head_got.at[mask - 1], {"context": flip(c, mask)})
    if chips and not last:
        source, target = ins[0], outs[0]
        for j in range(chips):
            crossing.append(
                cross(
                    j,
                    source.at[flip(c // 2, j), pl.ds(pl.multiple_of(t * piece, piece), piece), :],
                    target.at[pl.ds(j * piece, piece), :],
                    rest[13:15],
                )
            )
            crossing[-1].start()

    def home(part):
        at = columns_of_part(part)
        return [
            cross(j, mine.at[pl.ds(j * piece, piece), at], rest[17].at[pl.ds(j * piece, piece), at], rest[15:17], part * chips)
            for j in range(chips)
        ]

    def finish_last(part, group):
        at = columns_of_part(part)
        for copy in group[2:] if size == 4 else group:
            copy.wait_recv()

        def step(i, carry):
            row = pl.ds(pl.multiple_of(i * 16, 16), 16)
            summed = ins[0][row, at] + total[row, at]
            for other in range(2 if size == 4 else size - 1):
                summed = summed + got[other, row, at].astype(F32)
            mine[row, at] = summed.astype(BF)
            return carry

        lax.fori_loop(0, rows // 16, step, 0)
        for copy in home(part):
            copy.start()

    def sums_of(part):
        at = columns_of_part(part)
        return [
            send(6 * part + 0, sent.at[2, low, at], got.at[2, low, at], 1, sums),
            send(6 * part + 1, sent.at[2, high, at], got.at[2, high, at], 2, sums),
            send(6 * part + 2, sent.at[0, low, at], got.at[0, low, at], 1, sums),
            send(6 * part + 3, sent.at[1, high, at], got.at[1, high, at], 2, sums),
            send(6 * part + 4, sent.at[1, low, at], got.at[1, low, at], 2, sums),
            send(6 * part + 5, sent.at[0, high, at], got.at[0, high, at], 1, sums),
        ]

    if size == 4:
        groups = [sums_of(part) for part in range(parts)]
        copies = sum(groups, [])
        for part, group in enumerate(groups):
            for k, ready in ((3, group[:2]), (1, group[2:3]), (2, group[3:4])):
                if k != 3 or part:
                    product(k, first=k == 3, part=part)
                for copy in [] if last and part else ready:
                    copy.start()
        for part, group in enumerate(groups):
            at = columns_of_part(part)
            group[0].wait_recv()
            add(1, 2, 0, at)
            group[4].start()
            group[1].wait_recv()
            add(0, 2, half, at)
            group[5].start()
            for copy in groups[part + 1][:4] if last and part + 1 < parts else []:
                copy.start()
            product(0, part=part)
            if last and part + 1 < parts:
                finish_last(part, group)
        for group in [] if last else groups:
            for copy in group[2:]:
                copy.wait_recv()
        used = 2
    else:
        copies = [send(k - 1, sent.at[k - 1], got.at[k - 1], k, sums) for k in range(1, size)]
        copies[0].start()
        for k in range(2, size):
            product(k)
            copies[k - 1].start()
        product(0)
        groups = [copies]
        if not last:
            for copy in copies:
                copy.wait_recv()
        used = size - 1
    if last:
        finish_last(parts - 1, groups[-1])
    if chips and not last:
        crossing[0].wait()
        for copy in crossing[1:]:
            copy.wait_recv()

    def finish_rows(first, count, part=0):
        def step(i, carry):
            at = pl.ds(pl.multiple_of(first + i * 16, 16), 16)
            summed = total[at, :]
            for other in range(used):
                summed = summed + got[other, at, :].astype(F32)
            mine[at, :] = finish(at, summed, ins, outs).astype(BF)
            return carry

        lax.fori_loop(0, count // 16, step, 0)

    gather = (out_sem, in_sem)
    shared = rest[17] if last else mine
    own = pltpu.make_async_copy(shared, every.at[pl.ds(0, rows), :], own_sem)
    if last:
        going_home = [home(part) for part in range(parts)]
    else:
        going_home = [[cross(j, outs[1].at[pl.ds(j * piece, piece), :], outs[2].at[j], rest[15:17]) for j in range(chips)]]
    if last:
        for copy in small:
            copy.wait()
        for k in range(1, size):
            gain_rows[...] += gain_got[k - 1]
        outs[1][...] = head_rows[...]
        for mask in met:
            outs[1][...] += head_got[mask - 1]
        for mask in met:
            at = pl.ds(pl.multiple_of(flip(c, mask) * own_width, own_width), own_width)
            tell(gain_rows.at[:, at], own_got.at[mask - 1], {"context": flip(c, mask)})

    def came_home(first, count, part=0):
        for j in range(first // piece, (first + count) // piece):
            if j == 0:
                going_home[part][j].wait()
            else:
                going_home[part][j].wait_recv()

    out_parts = parts if last else 1
    make_ready = came_home if last else finish_rows
    then = [own] if last else [own, *going_home[0]]
    if size == 4:

        def out_columns(part):
            return pl.ds(part * (width // out_parts), width // out_parts)

        def chunk(k, side, part):
            return every.at[pl.ds(k * rows + side * half, half), out_columns(part)]

        def share(k, side, part):
            source = shared.at[pl.ds(side * half, half), out_columns(part)]
            return send(6 * part + 2 * k + side, source, chunk(k + 1, side, part), k + 1, gather)

        groups = []
        for part in range(out_parts):
            shares = [share(k, side, part) for k in (0, 1) for side in (0, 1)]
            passed = [
                send(6 * part + 4, chunk(1, 0, part), chunk(3, 0, part), 2, gather),
                send(6 * part + 5, chunk(2, 1, part), chunk(3, 1, part), 1, gather),
            ]
            groups.append(shares + passed)
        for part, group in enumerate(groups):
            make_ready(0, half, part)
            group[0].start()
            group[2].start()
            make_ready(half, half, part)
            group[3].start()
            group[1].start()
            if part == out_parts - 1:
                for copy in then:
                    copy.start()
            group[0].wait_recv()
            group[4].start()
            group[3].wait_recv()
            group[5].start()
        for group in groups:
            for at in (1, 2, 4, 5):
                group[at].wait_recv()
        shares = sum(groups, [])
    else:
        make_ready(0, rows)
        shares = [send(k - 1, shared, every.at[pl.ds(k * rows, rows), :], k, gather) for k in range(1, size)]
        for copy in [*shares, *then]:
            copy.start()
        for copy in shares:
            copy.wait_recv()
    own.wait()
    if chips and not last:
        came_home(0, rows)
    if last:
        for copy in small[size - 1 + len(met) :]:
            copy.wait()
        outs[0][...] = gain_rows[:, pl.ds(pl.multiple_of(c * own_width, own_width), own_width)]
        for mask in met:
            outs[0][...] += own_got[mask - 1]
    for copy in copies + shares + crossing[1:] + sum([group[1:] for group in going_home], []):
        copy.wait_send()


def exchange(name, number, a, w, finish, ins, outs, offset=0, chips=0, last=False):
    size = lax.axis_size("tensor")
    rows, width, depth = a.shape[0] // size, w.shape[0], a.shape[1]
    tile = min(512, width)
    parts = width // tile if size == 4 else 1
    links = 6 * parts if size == 4 else size - 1
    whole = pl.BlockSpec(memory_space=pltpu.VMEM)
    anywhere = pl.BlockSpec(memory_space=pl.ANY)
    dma = pltpu.SemaphoreType.DMA
    gain_scratch = []
    if last:
        own, head_width = outs[0][0][1], outs[1][0][1]
        ranks = 2 * chips
        gain_scratch = [
            pltpu.VMEM((rows, width), BF),
            pltpu.VMEM((8, width), F32),
            pltpu.VMEM((8, head_width), F32),
            pltpu.VMEM((size - 1, 8, width), F32),
            pltpu.VMEM((ranks - 1, 8, head_width), F32),
            pltpu.VMEM((ranks - 1, 8, own), F32),
            dma((size - 1 + 2 * (ranks - 1),)),
            dma((size - 1 + 2 * (ranks - 1),)),
        ]
    return pl.pallas_call(
        functools.partial(exchange_kernel, size, width, depth, offset, tile, finish, chips, last, len(ins), len(outs)),
        in_specs=[anywhere, anywhere] + [anywhere if chips and not last and i == 0 else whole for i in range(len(ins))],
        out_specs=[anywhere] + [whole] * len(outs),
        out_shape=[jax.ShapeDtypeStruct((size * rows, width), BF)] + [jax.ShapeDtypeStruct(*out) for out in outs],
        scratch_shapes=[
            pltpu.VMEM((size * rows, depth), BF),
            pltpu.VMEM((width, depth), BF),
            pltpu.VMEM((size - 1, rows, width), BF),
            pltpu.VMEM((size - 1, rows, width), BF),
            pltpu.VMEM((rows, width), F32),
            pltpu.VMEM((rows, width), BF),
            dma((size,)),
            dma((width // tile,)),
            dma((links,)),
            dma((links,)),
            dma((links,)),
            dma((links,)),
            dma,
        ]
        + [dma((chips * parts,))] * (4 if chips else 0)
        + gain_scratch,
        compiler_params=pltpu.CompilerParams(vmem_limit_bytes=VMEM_LIMIT, collective_id=number, has_side_effects=True),
        cost_estimate=pl.CostEstimate(flops=2 * size * rows * width * depth, bytes_accessed=240_000_000, transcendentals=0),
        name=name,
    )(a, w, *ins)


def add_rows(ref, values):
    ref[...] += values[:8] + values[8:]


def finish_attended(at, attended, ins, outs):
    tokens, gain = ins
    outs[0][at, :] = attended
    hidden = tokens[at, :].astype(F32) + attended * norm_factor(attended) * gain[...]
    outs[1][at, :] = hidden
    return hidden


def finish_hidden_grad(at, summed, ins, outs):
    attended, cotangent, gain = ins
    hidden_grad = cotangent[at, :].astype(F32) + summed
    outs[0][at, :] = hidden_grad
    values = attended[at, :]
    grad, gain_rows = norm_back(values, norm_factor(values), gain[...], hidden_grad)
    add_rows(outs[1], gain_rows)
    return grad


def remote(source, target, sems, slot, device):
    return pltpu.make_async_remote_copy(
        src_ref=source,
        dst_ref=target,
        send_sem=sems[0].at[slot],
        recv_sem=sems[1].at[slot],
        device_id=device,
        device_id_type=MESH,
    )


def meet(t, c, size, masks):
    barrier = pltpu.get_barrier_semaphore()
    for k in range(1, size):
        pl.semaphore_signal(barrier, inc=1, device_id={"tensor": flip(t, k)}, device_id_type=MESH)
    for mask in masks:
        pl.semaphore_signal(barrier, inc=1, device_id={"context": flip(c, mask)}, device_id_type=MESH)
    return lambda: pl.semaphore_wait(barrier, size - 1 + len(masks))


class Line:
    def __init__(self, chips, own, buf, up_sems, down_sems, core_sems):
        self.chips, self.own, self.buf = chips, own, buf
        self.sems, self.core_sems = {1: up_sems, -1: down_sems}, core_sems
        self.c = lax.axis_index("context")
        self.s, self.core = self.c // 2, self.c % 2

    def rows(self, chip, part=None):
        base = (2 * chip + self.core) * self.own
        if part is None:
            return pl.ds(pl.multiple_of(base, self.own), self.own)
        half = self.own // 2
        return pl.ds(pl.multiple_of(base + part * half, half), half)

    def hop(self, k, way, chip, part):
        ref = self.buf.at[self.rows(chip, part), :]
        return remote(ref, ref, self.sems[way], 2 * k + part, {"context": self.c + 2 * way})

    def cross(self, k, way, chip, part):
        ref = self.buf.at[self.rows(chip, part), :]
        slot = 0 if k < 0 else 1 + 2 * k + (way < 0)
        return remote(ref, ref, self.core_sems, 2 * slot + part, {"context": flip(self.c, 1)})

    def sends(self, k, way):
        if way > 0:
            return (self.s >= k) & (self.s < self.chips - 1)
        return (self.s + k < self.chips) & (self.s > 0)

    def gets(self, k, way):
        return self.s >= k + 1 if way > 0 else self.s + k + 1 < self.chips

    def each(self, test, k, act):
        for way in (1, -1):
            pl.when(test(k, way))(functools.partial(act, k, way))

    def start(self, k, part):
        self.each(self.sends, k, lambda k, way: self.hop(k, way, self.s - way * k, part).start())

    def begin(self):
        for part in range(2):
            self.start(0, part)
            self.cross(-1, 1, self.s, part).start()

    def advance(self, k, parts=(0, 1)):
        for part in parts:

            def got(k, way):
                chip = self.s - way * (k + 1)
                self.hop(k, way, chip, part).wait_recv()
                self.cross(k, way, chip, part).start()

            self.each(self.gets, k, got)
            if k + 1 < self.chips - 1:
                self.start(k + 1, part)

    def other_core(self, k):
        for part in range(2):
            if k < 0:
                self.cross(-1, 1, self.s, part).wait_recv()
            else:
                self.each(self.gets, k, lambda k, way: self.cross(k, way, self.s - way * (k + 1), part).wait_recv())

    def end(self):
        for part in range(2):
            self.cross(-1, 1, self.s, part).wait_send()
            for k in range(self.chips - 1):
                self.each(self.sends, k, lambda k, way: self.hop(k, way, self.s - way * k, part).wait_send())
                self.each(self.gets, k, lambda k, way: self.cross(k, way, self.s - way * (k + 1), part).wait_send())


def line_sems(chips):
    dma = pltpu.SemaphoreType.DMA
    return [dma((2 * (chips - 1),))] * 4 + [dma((2 * (2 * chips - 1),))] * 2


class Sums:
    def __init__(self, size, t, sent, got, columns, sems, base):
        rows = sent.shape[1]
        low, high = pl.ds(0, rows // 2), pl.ds(rows // 2, rows // 2)
        self.size, self.sent, self.got, self.columns, self.half = size, sent, got, columns, rows // 2

        def send(slot, of, to, at, partner):
            return remote(sent.at[of, at, columns], got.at[to, at, columns], sems, base + slot, {"tensor": flip(t, partner)})

        if size == 4:
            self.copies = [
                send(0, 2, 2, low, 1),
                send(1, 2, 2, high, 2),
                send(2, 0, 0, low, 1),
                send(3, 1, 1, high, 2),
                send(4, 1, 1, low, 2),
                send(5, 0, 0, high, 1),
            ]
            self.after_product = {3: self.copies[:2], 1: self.copies[2:3], 2: self.copies[3:4]}
        else:
            self.copies = [send(k - 1, k - 1, k - 1, pl.ds(0, rows), k) for k in range(1, size)]
            self.after_product = {k: self.copies[k - 1 : k] for k in range(1, size)}

    def pass_on(self):
        if self.size != 4:
            return
        for copy, slot, first, then in ((0, 1, 0, 4), (1, 0, self.half, 5)):
            self.copies[copy].wait_recv()

            def step(i, carry):
                at = pl.ds(pl.multiple_of(first + i * 16, 16), 16)
                summed = self.sent[slot, at, self.columns].astype(F32) + self.got[2, at, self.columns].astype(F32)
                self.sent[slot, at, self.columns] = summed.astype(BF)
                return carry

            lax.fori_loop(0, self.half // 16, step, 0)
            self.copies[then].start()

    def wait(self):
        for copy in self.copies[2:] if self.size == 4 else self.copies:
            copy.wait_recv()


class Gather:
    def __init__(self, size, t, shared, every, sems, own_sem):
        rows = every.shape[0] // size
        half = rows // 2
        self.size = size
        self.own = pltpu.make_async_copy(shared, every.at[pl.ds(0, rows), :], own_sem)

        def chunk(k, side):
            return every.at[pl.ds(k * rows + side * half, half), :]

        def send(slot, source, target, partner):
            return remote(source, target, sems, slot, {"tensor": flip(t, partner)})

        if size == 4:
            self.copies = [send(2 * k + side, shared.at[pl.ds(side * half, half), :], chunk(k + 1, side), k + 1) for k in (0, 1) for side in (0, 1)]
            self.copies += [send(4, chunk(1, 0), chunk(3, 0), 2), send(5, chunk(2, 1), chunk(3, 1), 1)]
            self.ready = (self.copies[0:3:2], self.copies[3:0:-2])
        else:
            self.copies = [send(k - 1, shared, every.at[pl.ds(k * rows, rows), :], k) for k in range(1, size)]
            self.ready = ((), self.copies)

    def start(self, side):
        for copy in self.ready[side]:
            copy.start()
        if side:
            self.own.start()

    def pass_on(self):
        if self.size == 4:
            self.copies[0].wait_recv()
            self.copies[4].start()
            self.copies[3].wait_recv()
            self.copies[5].start()

    def wait(self):
        for at, copy in enumerate(self.copies):
            if self.size != 4 or at not in (0, 3):
                copy.wait_recv()
        self.own.wait()

    def end(self):
        for copy in self.copies:
            copy.wait_send()


def links_of(size):
    return 6 if size == 4 else size - 1


def start_kernel(size, chips, offsets, n_pair, *refs):
    tokens_ref, firsts, refs = refs[0], refs[1 : 1 + len(offsets)], refs[1 + len(offsets) :]
    turned_ref, gains_ref, pair, refs = refs[0], refs[1], refs[2 : 2 + n_pair], refs[2 + n_pair :]
    every, out, both, shard = refs[:4]
    line_refs, gather, coming, own_sem, keep_sem, whole, turned, out_sem = refs[4:10], refs[10:12], refs[12:14], *refs[14:19]
    t, c = lax.axis_index("tensor"), lax.axis_index("context")
    s = c // 2
    rows = shard.shape[0]
    piece = rows // chips
    own = firsts[0].shape[0]
    line = Line(chips, own, whole, line_refs[0:2], line_refs[2:4], line_refs[4:6])
    wait_others = meet(t, c, size, [1, *range(2, 2 * chips, 2)])
    kept = [
        pltpu.make_async_copy(first, whole.at[line.rows(s), pl.ds(offset, first.shape[1])], keep_sem.at[i])
        for i, (first, offset) in enumerate(zip(firsts, offsets))
    ]
    across = pair[0].shape[1]
    kept += [
        pltpu.make_async_copy(part, both.at[:, pl.ds(i * across, across)], keep_sem.at[len(offsets) + i]) for i, part in enumerate(pair)
    ]
    turned_copy = pltpu.make_async_copy(turned_ref, turned, keep_sem.at[len(offsets) + n_pair])
    for copy in [turned_copy, *kept]:
        copy.start()
    after_firsts = sum(first.shape[1] for first in firsts)
    height = turned.shape[0]
    turned_copy.wait()
    whole[line.rows(s), after_firsts : after_firsts + height] = turned[...].astype(F32).T.astype(BF)
    gains = jnp.concatenate([gains_ref[...].astype(F32), jnp.zeros((HD - gains_ref.shape[0], own), F32)], axis=0)
    whole[line.rows(s), after_firsts + height :] = gains.T.astype(BF)
    arrivals = [
        (tokens_ref.at[flip(s, j), pl.ds(pl.multiple_of(t * piece, piece), piece), :], shard.at[pl.ds(j * piece, piece), :])
        for j in range(chips)
    ]
    first = pltpu.make_async_copy(*arrivals[0], coming[0].at[0])
    others = [remote(*arrivals[j], coming, j, {"context": flip(c, 2 * j)}) for j in range(1, chips)]
    wait_others()
    for copy in [first, *others]:
        copy.start()
    for copy in kept:
        copy.wait()
    line.begin()
    first.wait()
    for copy in others:
        copy.wait_recv()
    share = Gather(size, t, shard, every, gather, own_sem)
    share.start(0)
    share.start(1)

    def write(k, way, chip):
        at = pl.ds(pl.multiple_of(chip * 2 * own, 2 * own), 2 * own)
        return pltpu.make_async_copy(whole.at[at, :], out.at[at, :], out_sem.at[0 if k < 0 else 1 + 2 * k + (way < 0)])

    def keep(k):
        line.other_core(k)
        line.each(line.gets, k, lambda k, way: write(k, way, s - way * (k + 1)).start())

    line.advance(0)
    line.other_core(-1)
    write(-1, 1, s).start()
    share.pass_on()
    for k in range(1, chips - 1):
        line.advance(k)
        keep(k - 1)
    share.wait()
    keep(chips - 2)
    line.end()
    share.end()
    for copy in others:
        copy.wait_send()
    write(-1, 1, s).wait()
    for k in range(chips - 1):
        line.each(line.gets, k, lambda k, way: write(k, way, s - way * (k + 1)).wait())


def start(tokens, firsts, turned, gains, pair, chips):
    size = lax.axis_size("tensor")
    seqs, local_len, width = tokens.shape
    rows = seqs * local_len // size
    own = firsts[0].shape[0]
    offsets, across = [], 0
    for first in firsts:
        offsets.append(across)
        across += first.shape[1]
    across += turned.shape[0] + HD
    dma = pltpu.SemaphoreType.DMA
    anywhere, in_vmem = pl.BlockSpec(memory_space=pl.ANY), pl.BlockSpec(memory_space=pltpu.VMEM)
    shape = jax.ShapeDtypeStruct
    return pl.pallas_call(
        functools.partial(start_kernel, size, chips, offsets, len(pair)),
        in_specs=[anywhere] * (2 + len(firsts)) + [in_vmem] + [anywhere] * len(pair),
        out_specs=[anywhere] * 2 + [in_vmem] * 2,
        out_shape=[
            shape((size * rows, width), BF),
            shape((2 * chips * own, across), BF),
            shape((own, sum(part.shape[1] for part in pair)), BF),
            shape((rows, width), BF),
        ],
        scratch_shapes=line_sems(chips)
        + [dma((links_of(size),))] * 2
        + [dma((chips,))] * 2
        + [dma, dma((len(firsts) + len(pair) + 1,))]
        + [pltpu.VMEM((2 * chips * own, across), BF), pltpu.VMEM(turned.shape, BF), dma((2 * chips - 1,))],
        compiler_params=pltpu.CompilerParams(vmem_limit_bytes=VMEM_LIMIT, collective_id=8, has_side_effects=True),
        cost_estimate=pl.CostEstimate(flops=0, bytes_accessed=300_000_000, transcendentals=0),
        name="start",
    )(tokens, *firsts, turned, gains, *pair)


def feed_kernel(size, chips, tile, *refs):
    h_ref, gate_up_w_ref, down_ref, cotangent_ref, residual_ref, gain_ref = refs[:6]
    every, slopes_ref, act_ref, down_all_ref, upstream, output, pieces, gain_rows = refs[6:14]
    h_buf, w_buf, act, down, sent, got, total, mine, stage = refs[14:23]
    h_sem, w_sem, stage_sem, keep_sem, own_sem = refs[23:28]
    line_refs, sums, gather, coming, going = refs[28:34], refs[34:36], refs[36:38], refs[38:40], refs[40:42]
    t, c = lax.axis_index("tensor"), lax.axis_index("context")
    s = c // 2
    rows, width = total.shape
    hidden = act.shape[1]
    own = down_ref.shape[0]
    piece = rows // chips
    tiles = hidden // tile
    order = [3, 1, 2, 0] if size == 4 else [*range(1, size), 0]
    line = Line(chips, own, down, line_refs[0:2], line_refs[2:4], line_refs[4:6])

    def h_copy(k):
        at = pl.ds(k * rows, rows)
        return pltpu.make_async_copy(h_ref.at[at, :], h_buf.at[at, :], h_sem.at[k])

    def w_copy(j, i):
        at = pl.ds(pl.multiple_of(i * hidden + j * tile, tile), tile)
        return pltpu.make_async_copy(gate_up_w_ref.at[:, at], w_buf.at[:, at], w_sem.at[j, i])

    own_rows = line.rows(s)
    own_down = pltpu.make_async_copy(down_ref, down.at[own_rows, :], keep_sem.at[0])
    own_down.start()
    wait_others = meet(t, c, size, [1, *range(2, 2 * chips, 2)])
    h_copy(order[0]).start()
    for j in range(tiles):
        for i in range(2):
            w_copy(j, i).start()
    for k in order[1:]:
        h_copy(k).start()
    gain_rows[...] = jnp.zeros_like(gain_rows)
    own_down.wait()
    wait_others()
    line.begin()

    def stage_copy(slot, i, k, j):
        at = pl.ds(pl.multiple_of(i * hidden + j * tile, tile), tile)
        return pltpu.make_async_copy(stage.at[slot, i], slopes_ref.at[pl.ds(k * rows, rows), at], stage_sem.at[slot, i])

    for n, k in enumerate(order):
        h_copy(k).wait()
        chunk = pl.ds(k * rows, rows)

        def step(j, carry):
            slot = (n * tiles + j) % 2
            if n == 0:
                for i in range(2):
                    w_copy(j, i).wait()

            @pl.when(n * tiles + j >= 2)
            def _():
                for i in range(2):
                    stage_copy(slot, i, k, j).wait()

            gate, up = [
                dot_nn(h_buf[chunk, :], w_buf[:, pl.ds(pl.multiple_of(i * hidden + j * tile, tile), tile)]) for i in range(2)
            ]
            logistic = jax.nn.sigmoid(gate)
            silu = gate * logistic
            act[chunk, pl.ds(pl.multiple_of(j * tile, tile), tile)] = (silu * up).astype(BF)
            stage[slot, 0] = (up * (logistic + silu * (1.0 - logistic))).astype(BF)
            stage[slot, 1] = silu.astype(BF)
            for i in range(2):
                stage_copy(slot, i, k, j).start()
            return carry

        lax.fori_loop(0, tiles, step, 0)
        if n + 1 == size // 2:
            line.advance(0, (0,))
        if n + 1 == size * 3 // 4:
            line.advance(0, (1,))
    for slot in range(2):
        for i in range(2):
            stage_copy(slot, i, 0, 0).wait()
    act_out = pltpu.make_async_copy(act, act_ref, keep_sem.at[1])
    act_out.start()

    rounds = []

    def fed_round(i):
        at = pl.ds(pl.multiple_of(flip(s, i) * 2 * own, 2 * own), 2 * own)
        group = Sums(size, t, sent, got, at, sums, links_of(size) * i)
        for k in order:
            value = dot_nt(act[k * rows : (k + 1) * rows, :], down[at, :])
            if k:
                sent[k - 1, :, at] = value.astype(BF)
                for copy in group.after_product[k]:
                    copy.start()
            else:
                total[:, at] = value
        rounds.append(group)

    if chips > 2:
        line.advance(1, (0,))
    line.other_core(-1)
    fed_round(0)
    line.other_core(0)
    fed_round(1)
    if chips > 2:
        line.advance(1, (1,))
    rounds[0].pass_on()
    rounds[1].pass_on()
    arrivals = [
        (cotangent_ref.at[flip(s, j), pl.ds(pl.multiple_of(t * piece, piece), piece), :], upstream.at[pl.ds(j * piece, piece), :])
        for j in range(chips)
    ]
    first = pltpu.make_async_copy(*arrivals[0], coming[0].at[0])
    others = [remote(*arrivals[j], coming, j, {"context": flip(c, 2 * j)}) for j in range(1, chips)]
    for k in range(1, chips - 1):
        if k > 1:
            line.advance(k)
        if k + 1 == chips - 1:
            for copy in [first, *others]:
                copy.start()
        line.other_core(k)
        fed_round(k + 1)
        rounds[k + 1].pass_on()
    down_out = pltpu.make_async_copy(down, down_all_ref, keep_sem.at[2])
    down_out.start()
    for group in rounds:
        group.wait()
    first.wait()
    for copy in others:
        copy.wait_recv()

    used = 2 if size == 4 else size - 1

    def finish_rows(side):
        def step(i, carry):
            at = pl.ds(pl.multiple_of(side * (rows // 2) + i * 16, 16), 16)
            fed = total[at, :]
            for other in range(used):
                fed = fed + got[other, at, :].astype(F32)
            factor = norm_factor(fed)
            output[at, :] = (residual_ref[at, :] + fed * factor * gain_ref[...]).astype(BF)
            grad, gains = norm_back(fed, factor, gain_ref[...], upstream[at, :].astype(F32))
            gain_rows[...] += gains[:8] + gains[8:]
            mine[at, :] = grad.astype(BF)
            return carry

        lax.fori_loop(0, rows // 32, step, 0)

    share = Gather(size, t, mine, every, gather, own_sem)
    finish_rows(0)
    share.start(0)
    finish_rows(1)
    share.start(1)
    kept = pltpu.make_async_copy(output.at[pl.ds(0, piece), :], pieces.at[0], going[0].at[0])
    gone = [
        remote(output.at[pl.ds(j * piece, piece), :], pieces.at[j], going, j, {"context": flip(c, 2 * j)})
        for j in range(1, chips)
    ]
    for copy in [kept, *gone]:
        copy.start()
    share.pass_on()
    share.wait()
    kept.wait()
    for copy in gone:
        copy.wait_recv()
    act_out.wait()
    down_out.wait()
    line.end()
    share.end()
    for copy in [*sum([group.copies for group in rounds], []), *others, *gone]:
        copy.wait_send()


def feed(hidden_low, gate_up_weight, down_shard, cotangent, residual, gain, chips):
    size = lax.axis_size("tensor")
    count, width = hidden_low.shape
    rows = count // size
    own, hidden = down_shard.shape
    ranks = 2 * chips
    tile = min(512, hidden)
    links = links_of(size)
    dma = pltpu.SemaphoreType.DMA
    anywhere, whole = pl.BlockSpec(memory_space=pl.ANY), pl.BlockSpec(memory_space=pltpu.VMEM)
    shape = jax.ShapeDtypeStruct
    return pl.pallas_call(
        functools.partial(feed_kernel, size, chips, tile),
        in_specs=[anywhere] * 4 + [whole] * 2,
        out_specs=[anywhere] * 4 + [whole] * 4,
        out_shape=[
            shape((count, width), BF),
            shape((count, 2 * hidden), BF),
            shape((count, hidden), BF),
            shape((ranks * own, hidden), BF),
            shape((rows, width), BF),
            shape((rows, width), BF),
            shape((chips, rows // chips, width), BF),
            shape((8, width), F32),
        ],
        scratch_shapes=[
            pltpu.VMEM((count, width), BF),
            pltpu.VMEM((width, 2 * hidden), BF),
            pltpu.VMEM((count, hidden), BF),
            pltpu.VMEM((ranks * own, hidden), BF),
            pltpu.VMEM((size - 1, rows, width), BF),
            pltpu.VMEM((size - 1, rows, width), BF),
            pltpu.VMEM((rows, width), F32),
            pltpu.VMEM((rows, width), BF),
            pltpu.VMEM((2, 2, rows, tile), BF),
            dma((size,)),
            dma((hidden // tile, 2)),
            dma((2, 2)),
            dma((3,)),
            dma,
        ]
        + line_sems(chips)
        + [dma((links * chips,))] * 2
        + [dma((links,))] * 2
        + [dma((chips,))] * 4,
        compiler_params=pltpu.CompilerParams(vmem_limit_bytes=VMEM_LIMIT, collective_id=2, has_side_effects=True),
        cost_estimate=pl.CostEstimate(flops=6 * count * width * hidden, bytes_accessed=400_000_000, transcendentals=count * hidden),
        name="feed",
    )(hidden_low, gate_up_weight, down_shard, cotangent, residual, gain)


def turn(values, cosine, sine):
    heads = [values[:, i : i + HD] for i in range(0, values.shape[1], HD)]
    return jnp.concatenate([head * cosine + pltpu.roll(head, HD // 2, 1) * sine for head in heads], axis=1)


def turn_kernel(core_ref, raw_ref, column_ref, gain_ref, cosine_ref, sine_ref, keep_ref, send_ref):
    width = gain_ref.shape[1]
    half = width // 2
    cosine, sine = cosine_ref[...], sine_ref[...]
    first = core_ref[0] == 0
    for i in range(3):
        values = raw_ref[:, i * width : (i + 1) * width]
        if i < 2:
            values = turn(values * column_ref[:, i : i + 1] * gain_ref[i : i + 1, :], cosine, sine)
        low, high = values[:, :half].astype(BF), values[:, half:].astype(BF)
        keep_ref[i] = jnp.where(first, low, high)
        send_ref[i] = jnp.where(first, high, low)


def head_grads(core_ref, own_ref, other_ref, i):
    first = core_ref[0] == 0
    own, other = own_ref[i], other_ref[i]
    return jnp.concatenate([jnp.where(first, own, other), jnp.where(first, other, own)], axis=1).astype(F32)


def inner_kernel(core_ref, own_ref, other_ref, raw_ref, column_ref, gain_ref, cosine_ref, sine_ref, inner_ref, gains_ref):
    width = gain_ref.shape[1]
    cosine, sine = cosine_ref[...], -sine_ref[...]

    @pl.when(pl.program_id(0) == 0)
    def _():
        gains_ref[...] = jnp.zeros_like(gains_ref)

    for i in range(2):
        flat = turn(head_grads(core_ref, own_ref, other_ref, i), cosine, sine) * raw_ref[:, i * width : (i + 1) * width]
        inner_ref[i] = lax.dot_general(
            jnp.ones((8, width), F32),
            flat * gain_ref[i : i + 1, :],
            (((1,), (1,)), ((), ())),
            precision=lax.Precision.HIGHEST,
            preferred_element_type=F32,
        )
        flat = flat * column_ref[:, i : i + 1]
        gains_ref[i] += jnp.sum(flat.reshape(-1, 8, width), axis=0)


def raw_grad_kernel(core_ref, own_ref, other_ref, raw_ref, column_ref, gain_ref, cosine_ref, sine_ref, out_ref):
    width = gain_ref.shape[1]
    cosine, sine = cosine_ref[...], -sine_ref[...]
    for i in range(3):
        values = head_grads(core_ref, own_ref, other_ref, i)
        if i < 2:
            values = turn(values, cosine, sine) * column_ref[:, i : i + 1] * gain_ref[i : i + 1, :]
            values = values - raw_ref[:, i * width : (i + 1) * width] * column_ref[:, i + 2 : i + 3]
        out_ref[:, i * width : (i + 1) * width] = values.astype(BF)


def by_rows(kernel, name, core, ins, outs, rows=256):
    def spec(shape, dim):
        block = tuple(rows if i == dim else extent for i, extent in enumerate(shape))
        return pl.BlockSpec(block, lambda i, core: tuple(i if at == dim else 0 for at in range(len(shape))))

    count = next(out[0][dim] for *out, dim in outs if dim is not None)
    return pl.pallas_call(
        kernel,
        grid_spec=pltpu.PrefetchScalarGridSpec(
            num_scalar_prefetch=1,
            grid=(count // rows,),
            in_specs=[spec((array.shape[0], count, array.shape[2]) if dim == 1 else array.shape, dim) for array, dim in ins],
            out_specs=[spec(shape, dim) for shape, _, dim in outs],
        ),
        out_shape=[jax.ShapeDtypeStruct(shape, dtype) for shape, dtype, _ in outs],
        compiler_params=pltpu.CompilerParams(vmem_limit_bytes=VMEM_LIMIT),
        name=name,
    )(core[None].astype(jnp.int32), *[array for array, _ in ins])


def act_back_kernel(tile, grad_ref, w_ref, slopes_ref, out_ref):
    hidden = w_ref.shape[1]
    for j in range(0, hidden, tile):
        act_grad = dot_nn(grad_ref[...], w_ref[:, j : j + tile])
        for at in (j, hidden + j):
            out_ref[:, at : at + tile] = (act_grad * slopes_ref[:, at : at + tile].astype(F32)).astype(BF)


def act_back(fed_low, w_down, slopes):
    count, width = fed_low.shape
    hidden = w_down.shape[1]
    rows = 256
    return pl.pallas_call(
        functools.partial(act_back_kernel, 512),
        grid=(count // rows,),
        in_specs=[
            pl.BlockSpec((rows, width), lambda i: (i, 0)),
            pl.BlockSpec((width, hidden), lambda i: (0, 0)),
            pl.BlockSpec((rows, 2 * hidden), lambda i: (i, 0)),
        ],
        out_specs=pl.BlockSpec((rows, 2 * hidden), lambda i: (i, 0)),
        out_shape=jax.ShapeDtypeStruct((count, 2 * hidden), BF),
        compiler_params=pltpu.CompilerParams(vmem_limit_bytes=VMEM_LIMIT),
        cost_estimate=pl.CostEstimate(flops=2 * count * width * hidden, bytes_accessed=40_000_000, transcendentals=count * hidden),
        name="act_back",
    )(fed_low, w_down, slopes)


def rank_sums_kernel(chips, size, tile, count, carries, *refs):
    lefts, rights, refs = refs[:count], refs[count : 2 * count], refs[2 * count :]
    if carries:
        carried_ref, out_ref, every_ref, *refs = refs
    else:
        out_ref, *refs = refs
    left_bufs, right_bufs = refs[:count], refs[count : 2 * count]
    passed, got, out, left_sem, right_sem, out_sem, sent_sem, got_sem = refs[2 * count : 2 * count + 8]
    t, c = lax.axis_index("tensor"), lax.axis_index("context")
    core = c % 2
    own = out.shape[1]
    blocks = [(j, core_at) for core_at in (1, 0) for j in range(chips)]

    def left_copy(i, j, core_at):
        rank = 2 * j + (core if core_at == 0 else 1 - core)
        at = pl.ds(pl.multiple_of(rank * own, own), own)
        block = left_bufs[i].at[core_at * chips + j]
        return pltpu.make_async_copy(lefts[i].at[:, at], block, left_sem.at[i, core_at * chips + j])

    tiles = [right.shape[1] // tile for right in rights]

    def right_copy(i, n):
        at = pl.ds(pl.multiple_of(n * tile, tile), tile)
        return pltpu.make_async_copy(rights[i].at[:, at], right_bufs[i].at[:, at], right_sem.at[i, n])

    wait_others = meet(t, c, size if carries else 1, [1])
    for i in range(count):
        left_copy(i, *blocks[0]).start()
        for n in range(tiles[i]):
            right_copy(i, n).start()
        for block in blocks[1:]:
            left_copy(i, *block).start()
    wait_others()
    if carries:
        sent_out, got_out, own_sem = refs[2 * count + 8 :]
        part = carried_ref.at[pl.ds(carries[0], carries[1]), :]
        share = Gather(size, t, part, every_ref, (sent_out, got_out), own_sem)
        share.start(0)
        share.start(1)
    def send(j):
        return remote(passed.at[j], got.at[j], (sent_sem, got_sem), j, {"context": flip(c, 1)})

    def write(j):
        return pltpu.make_async_copy(out.at[j], out_ref.at[pl.ds(pl.multiple_of(j * own, own), own), :], out_sem.at[j])

    def block(core_at, j, carry):
        base = 0
        if core_at == 0:
            send(j).wait_recv()
        for i in range(count):
            left_copy(i, j, core_at).wait()
            left = left_bufs[i][core_at * chips + j].T
            for n in range(tiles[i]):
                if core_at:
                    pl.when(j == 0)(right_copy(i, n).wait)
                to = slice(base + n * tile, base + (n + 1) * tile)
                part = dot_nn(left, right_bufs[i][:, n * tile : (n + 1) * tile])
                if core_at:
                    passed[j, :, to] = part.astype(BF)
                else:
                    out[j, :, to] = (part + got[j, :, to].astype(F32)).astype(BF)
            base += tiles[i] * tile
        (send if core_at else write)(j).start()
        if carries and core_at == 0:
            pl.when(j == 1)(share.pass_on)
        return carry

    lax.fori_loop(0, chips, functools.partial(block, 1), 0)
    lax.fori_loop(0, chips, functools.partial(block, 0), 0)
    for j in range(chips):
        send(j).wait_send()
        write(j).wait()
    if carries:
        share.wait()
        share.end()


def rank_sums(number, pairs, own, carried=None):
    size = lax.axis_size("tensor")
    lefts, rights = [left for left, _ in pairs], [right for _, right in pairs]
    count, width = lefts[0].shape
    chips = width // (2 * own)
    across = sum(right.shape[1] for right in rights)
    tile = min(512, *[right.shape[1] for right in rights])
    most = max(right.shape[1] for right in rights) // tile
    more = [] if carried is None else [carried[0]]
    dma = pltpu.SemaphoreType.DMA
    return pl.pallas_call(
        functools.partial(rank_sums_kernel, chips, size, tile, len(pairs), carried and carried[1:]),
        in_specs=[pl.BlockSpec(memory_space=pl.ANY)] * (2 * len(pairs) + len(more)),
        out_specs=[pl.BlockSpec(memory_space=pl.ANY)] * (1 + len(more)),
        out_shape=[jax.ShapeDtypeStruct((chips * own, across), BF)]
        + [jax.ShapeDtypeStruct((size * carried[2], rows.shape[1]), BF) for rows in more],
        scratch_shapes=[pltpu.VMEM((2 * chips, count, own), BF)] * len(pairs)
        + [pltpu.VMEM(right.shape, BF) for right in rights]
        + [pltpu.VMEM((chips, own, across), BF)] * 3
        + [dma((len(pairs), 2 * chips)), dma((len(pairs), most)), dma((chips,)), dma((chips,)), dma((chips,))]
        + [dma((links_of(size),)), dma((links_of(size),)), dma] * len(more),
        compiler_params=pltpu.CompilerParams(vmem_limit_bytes=VMEM_LIMIT, collective_id=number, has_side_effects=True),
        cost_estimate=pl.CostEstimate(flops=2 * count * width * across, bytes_accessed=60_000_000, transcendentals=0),
        name="rank_sums",
    )(*lefts, *rights, *more)


def columns_of(*values):
    stacked = jnp.stack(values, axis=1)
    return jnp.pad(stacked, ((0, 0), (0, 8 - len(values))))


def in_order(at_ref, source, target, piece, other=None):
    rows = source.shape[0]

    def step(p, carry):
        start = at_ref[p]
        at = pl.ds(pl.multiple_of(start % rows, piece), piece)
        values = source[at, :]
        if other is not None:
            values = jnp.where(start < rows, values, other[at, :])
        target[pl.ds(pl.multiple_of(p * piece, piece), piece), :] = values
        return carry

    lax.fori_loop(0, target.shape[0] // piece, step, 0)


def out_of_order(at_ref, source, target, piece):
    def step(p, carry):
        start = pl.multiple_of(at_ref[p], piece)
        target[pl.ds(start, piece), :] = source[pl.ds(pl.multiple_of(p * piece, piece), piece), :].astype(target.dtype)
        return carry

    lax.fori_loop(0, source.shape[0] // piece, step, 0)


def causal(tile):
    key_at = lax.broadcasted_iota(jnp.int32, (tile, tile), 0)
    query_at = lax.broadcasted_iota(jnp.int32, (tile, tile), 1)
    return query_at >= key_at


def attend_kernel(piece, tile, at_ref, own_ref, other_ref, out_ref, log_ref, query, key, value, value_t, mixed):
    for slot, held in enumerate((query, key, value)):
        in_order(at_ref, own_ref.at[slot], held, piece, other_ref.at[slot])
    value_t[...] = value[...].astype(F32).T.astype(BF)
    allowed = causal(tile)
    for i in range(query.shape[0] // tile):
        low, high = i * tile, (i + 1) * tile
        rows = query[low:high, :]
        near = jnp.where(allowed, dot_nt(key[low:high, :], rows) * HD ** (-0.5), -1e30)
        top = jnp.max(near, axis=0, keepdims=True)
        if i:
            far = dot_nt(key[0:low, :], rows) * HD ** (-0.5)
            top = jnp.maximum(top, jnp.max(far, axis=0, keepdims=True))
        near = jnp.exp(near - top)
        total = jnp.sum(near, axis=0, keepdims=True)
        summed = dot_nn(value_t[:, low:high], near.astype(BF))
        if i:
            far = jnp.exp(far - top)
            total = total + jnp.sum(far, axis=0, keepdims=True)
            summed = summed + dot_nn(value_t[:, 0:low], far.astype(BF))
        mixed[low:high, :] = (summed / total).T
        log_ref[0, :, low:high] = top + jnp.log(total)
    out_of_order(at_ref, mixed, out_ref, piece)


def attend(own, other, at, piece):
    half, width = own.shape[1:]
    rows = 2 * half
    heads = width // HD
    return pl.pallas_call(
        functools.partial(attend_kernel, piece, 256),
        grid_spec=pltpu.PrefetchScalarGridSpec(
            num_scalar_prefetch=1,
            grid=(heads,),
            in_specs=[pl.BlockSpec((3, half, HD), lambda h, at: (0, 0, h))] * 2,
            out_specs=[
                pl.BlockSpec((rows, HD), lambda h, at: (0, h)),
                pl.BlockSpec((1, 1, rows), lambda h, at: (h, 0, 0)),
            ],
            scratch_shapes=[pltpu.VMEM((rows, HD), BF)] * 3 + [pltpu.VMEM((HD, rows), BF), pltpu.VMEM((rows, HD), F32)],
        ),
        out_shape=[jax.ShapeDtypeStruct((rows, width), BF), jax.ShapeDtypeStruct((heads, 1, rows), F32)],
        compiler_params=pltpu.CompilerParams(vmem_limit_bytes=VMEM_LIMIT),
        cost_estimate=pl.CostEstimate(
            flops=2 * 2 * heads * rows * rows * HD, bytes_accessed=8 * rows * width, transcendentals=heads * rows * rows // 2
        ),
        name="attend",
    )(at, own, other)


def attend_back_kernel(
    piece, tile, at_ref, own_ref, other_ref, out_ref, grad_ref, log_ref, dqkv_ref, query, key, value, key_t, grad, mixed, dquery, dkey, dvalue
):
    for slot, held in enumerate((query, key, value)):
        in_order(at_ref, own_ref.at[slot], held, piece, other_ref.at[slot])
    in_order(at_ref, grad_ref, grad, piece)
    in_order(at_ref, out_ref, mixed, piece)
    key_t[...] = key[...].astype(F32).T.astype(BF)
    allowed = causal(tile)
    dkey[...] = jnp.zeros_like(dkey)
    dvalue[...] = jnp.zeros_like(dvalue)
    scale = HD ** (-0.5)
    for i in range(query.shape[0] // tile):
        low, high = i * tile, (i + 1) * tile
        rows = query[low:high, :]
        rows_grad = grad[low:high, :]
        log = log_ref[0, :, low:high]
        spread = jnp.sum((rows_grad.astype(F32) * mixed[low:high, :].astype(F32)).T, axis=0, keepdims=True)
        dquery_t = None
        for start, stop, masked in ((0, low, False), (low, high, True)):
            if start == stop:
                continue
            scores = dot_nt(key[start:stop, :], rows) * scale
            if masked:
                scores = jnp.where(allowed, scores, -1e30)
            probs = jnp.exp(scores - log)
            probs_grad = dot_nt(value[start:stop, :], rows_grad)
            scores_grad = (probs * (probs_grad - spread)).astype(BF)
            dvalue[start:stop, :] += dot_nn(probs.astype(BF), rows_grad)
            dkey[start:stop, :] += dot_nn(scores_grad, rows)
            term = dot_nn(key_t[:, start:stop], scores_grad)
            dquery_t = term if dquery_t is None else dquery_t + term
        dquery[low:high, :] = dquery_t.T * scale
    dkey[...] = dkey[...] * scale
    for slot, held in enumerate((dquery, dkey, dvalue)):
        out_of_order(at_ref, held, dqkv_ref.at[slot], piece)


def attend_back(own, other, out, grad, log, at, piece):
    half, width = own.shape[1:]
    rows = 2 * half
    heads = width // HD
    return pl.pallas_call(
        functools.partial(attend_back_kernel, piece, 256),
        grid_spec=pltpu.PrefetchScalarGridSpec(
            num_scalar_prefetch=1,
            grid=(heads,),
            in_specs=[
                pl.BlockSpec((3, half, HD), lambda h, at: (0, 0, h)),
                pl.BlockSpec((3, half, HD), lambda h, at: (0, 0, h)),
                pl.BlockSpec((rows, HD), lambda h, at: (0, h)),
                pl.BlockSpec((rows, HD), lambda h, at: (0, h)),
                pl.BlockSpec((1, 1, rows), lambda h, at: (h, 0, 0)),
            ],
            out_specs=pl.BlockSpec((3, rows, HD), lambda h, at: (0, 0, h)),
            scratch_shapes=[pltpu.VMEM((rows, HD), BF)] * 3
            + [pltpu.VMEM((HD, rows), BF)]
            + [pltpu.VMEM((rows, HD), BF)] * 2
            + [pltpu.VMEM((rows, HD), F32)] * 3,
        ),
        out_shape=jax.ShapeDtypeStruct((3, rows, width), BF),
        compiler_params=pltpu.CompilerParams(vmem_limit_bytes=VMEM_LIMIT),
        cost_estimate=pl.CostEstimate(
            flops=5 * heads * rows * rows * HD * 2, bytes_accessed=16 * rows * width, transcendentals=heads * rows * rows // 2
        ),
        name="attend_back",
    )(at, own, other, out, grad, log)


def local(
    tokens,
    block_order,
    query_weight,
    key_weight,
    value_weight,
    output_weight,
    gate_weight,
    up_weight,
    down_weight,
    query_gain,
    key_gain,
    attention_gain,
    forward_gain,
    cotangent,
):
    seqs, local_len, width = tokens.shape
    ranks = lax.axis_size("context")
    columns = lax.axis_size("tensor")
    full_len = local_len * ranks
    piece_len = full_len // block_order.shape[0]
    piece = local_len // columns
    shard_rows = seqs * piece
    count = shard_rows * columns
    context = lax.axis_index("context")
    t = lax.axis_index("tensor")
    s, core = context // 2, context % 2
    head_width = query_weight.shape[1]
    half_width = head_width // 2
    hidden_width = gate_weight.shape[1]

    rows, w_first, gate_up_shard, row_shard = start(
        tokens,
        [query_weight, key_weight, value_weight],
        output_weight,
        jnp.stack([attention_gain, forward_gain]),
        [gate_weight, up_weight],
        seqs,
    )
    qkv_width = 3 * head_width
    gains = w_first[:, 4 * head_width :]
    gain_attn, gain_feed = gains[:, 0].astype(F32)[None], gains[:, 1].astype(F32)[None]
    w_gate_up = lax.all_gather(gate_up_shard, "context", axis=0, tiled=True)

    chips = s ^ jnp.arange(seqs, dtype=jnp.int32)
    shards = t ^ jnp.arange(columns, dtype=jnp.int32)
    starts = (2 * chips[None, :] + core) * local_len + shards[:, None] * piece
    stored = (starts[:, :, None] + jnp.arange(piece, dtype=jnp.int32)).reshape(count)
    block = stored // piece_len
    slots = jnp.arange(block_order.shape[0], dtype=jnp.int32)
    place = jnp.sum(jnp.where(block[:, None] == slots[None, :], block_order[None, :], 0), axis=1) * piece_len
    place = place + stored % piece_len
    freq = THETA ** (-jnp.arange(0, HD, 2, dtype=F32) / HD)
    angle = place.astype(F32)[:, None] * freq[None, :]
    cosine = jnp.concatenate([jnp.cos(angle), jnp.cos(angle)], axis=-1)
    sine = jnp.concatenate([-jnp.sin(angle), jnp.sin(angle)], axis=-1)
    per_block = piece_len // piece
    pieces = jnp.arange(full_len // piece, dtype=jnp.int32)
    hits = block_order[None, :] == (pieces // per_block)[:, None]
    block_at = jnp.sum(jnp.where(hits, slots[None, :], 0), axis=1)
    piece_at = block_at * per_block + pieces % per_block
    rank_of, shard_of = piece_at // columns, piece_at % columns
    at = (((rank_of % 2) ^ core) * columns + (shard_of ^ t)) * seqs + ((rank_of // 2) ^ s)
    at = (at * piece).astype(jnp.int32)

    qkv_raw = dot_nn(rows, w_first[:, :qkv_width])
    query_raw = qkv_raw[:, :head_width]
    key_raw = qkv_raw[:, head_width : 2 * head_width]
    totals = sum_over_tensor(jnp.stack([jnp.sum(query_raw * query_raw, axis=1), jnp.sum(key_raw * key_raw, axis=1)]))
    factors = lax.rsqrt(totals / width + EPS)
    scaling = jnp.stack([query_gain, key_gain]).astype(F32)
    keep, send = by_rows(
        turn_kernel,
        "turn",
        core,
        [(qkv_raw, 0), (columns_of(*factors), 0), (scaling, None), (cosine, 0), (sine, 0)],
        [((3, count, half_width), BF, 1)] * 2,
    )
    received = swap(send, "context", 1)
    mixed_heads, log = attend(keep, received, at, piece)

    def to_heads(values):
        keep = lax.dynamic_slice_in_dim(values, core * half_width, half_width, axis=1)
        send = lax.dynamic_slice_in_dim(values, (1 - core) * half_width, half_width, axis=1)
        return jnp.concatenate([keep, swap(send, "context", 1)], axis=0)

    def to_rows(values):
        own, other = values[:count], swap(values[count:], "context", 1)
        return jnp.concatenate([jnp.where(core == 0, own, other), jnp.where(core == 0, other, own)], axis=1)

    mixed_low = to_rows(mixed_heads)

    def chunk(values, k):
        return values[k * shard_rows : (k + 1) * shard_rows]

    order = list(range(columns))
    shard = (shard_rows, width)
    hidden_low, attended, hidden = exchange(
        "attended", 1, mixed_low, w_first, finish_attended, [row_shard, gain_attn], [(shard, F32), (shard, F32)], offset=qkv_width
    )

    fed_low, slopes, act_low, w_down, upstream, _, output_pieces, feed_gain_rows = feed(
        hidden_low, w_gate_up, down_weight.T, cotangent, hidden, gain_feed, seqs
    )

    own = width // ranks
    cores = [list(range(0, ranks, 2)), list(range(1, ranks, 2))]

    def scatter(values):
        return lax.psum_scatter(values, "context", scatter_dimension=0, axis_index_groups=cores, tiled=True)

    output_pieces = output_pieces.reshape(shard)
    split = seqs // 4 * piece
    down_part, first_rows = rank_sums(5, [(fed_low, act_low)], own, (output_pieces, 0, split))
    down_summed = scatter(down_part)
    down_grad = down_summed.astype(F32).T
    gate_up_low = act_back(after(fed_low, down_part), w_down, slopes)
    gate_up_part, other_rows = rank_sums(6, [(hidden_low, gate_up_low)], own, (output_pieces, split, shard_rows - split))
    layer_output = in_place([values.reshape(columns, -1, piece, width) for values in (first_rows, other_rows)], s, t, BF)
    gate_up_summed = scatter(gate_up_part)
    gate_up_low = after(gate_up_low, gate_up_part)
    attended_low, hidden_grad, attn_gain_rows = exchange(
        "hidden_grad",
        3,
        gate_up_low,
        w_gate_up,
        finish_hidden_grad,
        [attended, upstream, gain_attn],
        [(shard, F32), ((8, width), F32)],
    )
    attended_low = after(attended_low, layer_output)
    mixed_grad = dot_nn(attended_low, w_first[:, qkv_width : 4 * head_width]).astype(BF)
    dqkv = attend_back(keep, received, mixed_heads, to_heads(mixed_grad), log, at, piece)
    dqkv_other = swap(dqkv[:, count:], "context", 1)
    inner, head_gain_rows = by_rows(
        inner_kernel,
        "inner",
        core,
        [(dqkv, 1), (dqkv_other, 1), (qkv_raw, 0), (columns_of(*factors), 0), (scaling, None), (cosine, 0), (sine, 0)],
        [((2, 8, count), F32, 2), ((2, 8, head_width), F32, None)],
    )
    inner = sum_over_tensor(inner[:, 0])
    (qkv_low,) = by_rows(
        raw_grad_kernel,
        "raw_grad",
        core,
        [
            (dqkv, 1),
            (dqkv_other, 1),
            (qkv_raw, 0),
            (after(columns_of(*factors, *(inner * factors**3 / width)), down_grad), 0),
            (scaling, None),
            (cosine, 0),
            (sine, 0),
        ],
        [((count, 3 * head_width), BF, 0)],
    )
    (qkv_part,) = rank_sums(7, [(rows, qkv_low), (attended_low, mixed_low)], own)
    qkv_out_summed = scatter(after(qkv_part, gate_up_summed, down_summed))
    every, width_gains, head_gains = exchange(
        "tokens_grad",
        4,
        after(qkv_low, qkv_part),
        w_first,
        None,
        [hidden_grad, attn_gain_rows, feed_gain_rows, head_gain_rows.reshape(16, head_width)],
        [((8, own), F32), ((8, head_width), F32)],
        chips=seqs,
        last=True,
    )
    tokens_grad = in_place([every.reshape(columns, seqs, piece, width)], s, t, F32)

    gate_up_summed, qkv_out_summed = gate_up_summed.astype(F32), qkv_out_summed.astype(F32)
    return (
        layer_output,
        tokens_grad,
        qkv_out_summed[:, :head_width],
        qkv_out_summed[:, head_width : 2 * head_width],
        qkv_out_summed[:, 2 * head_width : 3 * head_width],
        qkv_out_summed[:, 3 * head_width :].T,
        gate_up_summed[:, :hidden_width],
        gate_up_summed[:, hidden_width:],
        down_grad,
        head_gains[0],
        head_gains[1],
        width_gains[0],
        width_gains[1],
    )


def solution(mesh):
    return jax.shard_map(
        local,
        mesh=mesh,
        in_specs=(
            P(None, "context", None),
            P(),
            P("context", "tensor"),
            P("context", "tensor"),
            P("context", "tensor"),
            P("tensor", "context"),
            P("context", "tensor"),
            P("context", "tensor"),
            P("tensor", "context"),
            P("tensor"),
            P("tensor"),
            P("context"),
            P("context"),
            P(None, "context", None),
        ),
        out_specs=(
            P(None, "context", None),
            P(None, "context", None),
            P("context", "tensor"),
            P("context", "tensor"),
            P("context", "tensor"),
            P("tensor", "context"),
            P("context", "tensor"),
            P("context", "tensor"),
            P("tensor", "context"),
            P("tensor"),
            P("tensor"),
            P("context"),
            P("context"),
        ),
        check_vma=False,
    )
```

```python
import functools

import jax
import jax.numpy as jnp
from jax import lax
from jax.experimental import pallas as pl
from jax.experimental.pallas import tpu as pltpu
from jax.sharding import PartitionSpec as P

HD = 128
EPS = 1e-06
THETA = 500000.0
BF = jnp.bfloat16
F32 = jnp.float32
VMEM_LIMIT = 60 * 1024 * 1024
MESH = pl.DeviceIdType.MESH


def dot_nn(left, right):
    return jnp.dot(left, right, preferred_element_type=F32)


def dot_nt(left, right):
    return lax.dot_general(left, right, (((1,), (1,)), ((), ())), preferred_element_type=F32)


def after(values, *others):
    return lax.optimization_barrier((values, *others))[0]


def swap(values, axis, mask):
    size = lax.axis_size(axis)
    return lax.ppermute(values, axis, [(i, i ^ mask) for i in range(size)])


def sum_over_tensor(values):
    size = lax.axis_size("tensor")
    chunks = values.reshape(values.shape[0], size, -1)
    total = chunks
    for m in range(1, size):
        other = swap(chunks, "tensor", m)
        total = total + jnp.stack([other[:, m ^ k] for k in range(size)], axis=1)
    return total.reshape(values.shape)


def place_kernel(at_ref, *refs):
    out_ref = refs[-1]
    for a in range(out_ref.shape[0]):
        at, base, values = a ^ at_ref[0], 0, None
        for ref in refs[:-1]:
            count = ref.shape[1]
            part = ref[0, jnp.clip(at - base, 0, count - 1)]
            values = part if values is None else jnp.where(at >= base, part, values)
            base += count
        out_ref[a, 0] = values.astype(out_ref.dtype)


def in_place(parts, s, t, dtype):
    size, _, piece, width = parts[0].shape
    seqs = sum(part.shape[1] for part in parts)
    full = pl.pallas_call(
        place_kernel,
        grid_spec=pltpu.PrefetchScalarGridSpec(
            num_scalar_prefetch=1,
            grid=(size,),
            in_specs=[pl.BlockSpec((1, *part.shape[1:]), lambda b, at: (b ^ at[1], 0, 0, 0)) for part in parts],
            out_specs=pl.BlockSpec((seqs, 1, piece, width), lambda b, at: (0, b, 0, 0)),
        ),
        out_shape=jax.ShapeDtypeStruct((seqs, size, piece, width), dtype),
        name="place_rows",
    )(jnp.stack([s, t]).astype(jnp.int32), *parts)
    return full.reshape(seqs, size * piece, width)


def norm_factor(values):
    return lax.rsqrt(jnp.mean(values * values, axis=-1, keepdims=True) + EPS)


def norm_back(values, factor, gain, grad):
    scaled = grad * gain
    inner = jnp.mean(values * scaled, axis=-1, keepdims=True)
    return factor * scaled - values * (factor**3 * inner), grad * values * factor


def flip(index, mask):
    bit = 1
    result = index
    while bit <= mask:
        if mask & bit:
            result = result + bit - 2 * bit * ((index // bit) % 2)
        bit *= 2
    return result


def exchange_kernel(size, width, depth, offset, tile, finish, chips, last, n_in, n_out, a_ref, w_ref, *refs):
    ins, rest = refs[:n_in], refs[n_in:]
    every, outs, rest = rest[0], rest[1 : 1 + n_out], rest[1 + n_out :]
    a_buf, w_buf, sent, got, total, mine, a_sem, w_sem, sent_sem, got_sem, out_sem, in_sem, own_sem = rest[:13]
    t = lax.axis_index("tensor")
    c = lax.axis_index("context")
    rows = total.shape[0]
    half = rows // 2

    def a_copy(k):
        at = pl.ds(k * rows, rows)
        return pltpu.make_async_copy(a_ref.at[at, :], a_buf.at[at, :], a_sem.at[k])

    def w_copy(j):
        at = pl.ds(pl.multiple_of(j * tile, tile), tile)
        return pltpu.make_async_copy(w_ref.at[at, pl.ds(offset, depth)], w_buf.at[at, :], w_sem.at[j])

    order = [3, 1, 2, 0] if size == 4 else [*range(1, size), 0]
    tiles = width // tile
    parts = tiles if size == 4 else 1
    across = width // parts
    a_copy(order[0]).start()
    for j in range(tiles):
        w_copy(j).start()
    for k in order[1:]:
        a_copy(k).start()
    barrier = pltpu.get_barrier_semaphore()
    for k in range(1, size):
        pl.semaphore_signal(barrier, inc=1, device_id={"tensor": flip(t, k)}, device_id_type=MESH)

    met = range(1, 2 * chips) if last else range(2, 2 * chips, 2)
    for mask in met:
        pl.semaphore_signal(barrier, inc=1, device_id={"context": flip(c, mask)}, device_id_type=MESH)
    for out in outs:
        if out.shape[0] == 8:
            out[...] = jnp.zeros_like(out)

    def cross(j, source, target, sems, base=0):
        if j == 0:
            return pltpu.make_async_copy(source, target, sems[0].at[base])
        return pltpu.make_async_remote_copy(
            src_ref=source,
            dst_ref=target,
            send_sem=sems[0].at[base + j],
            recv_sem=sems[1].at[base + j],
            device_id={"context": flip(c, 2 * j)},
            device_id_type=MESH,
        )

    def send(slot, source, target, partner, sems):
        return pltpu.make_async_remote_copy(
            src_ref=source,
            dst_ref=target,
            send_sem=sems[0].at[slot],
            recv_sem=sems[1].at[slot],
            device_id={"tensor": flip(t, partner)},
            device_id_type=MESH,
        )

    def product(k, first=False, part=0):
        if part == 0:
            a_copy(k).wait()

        def step(j, carry):
            if first:
                w_copy(j).wait()
            at = pl.ds(pl.multiple_of(j * tile, tile), tile)
            value = dot_nt(a_buf[k * rows : (k + 1) * rows, :], w_buf[at, :])
            if k:
                sent[k - 1, :, at] = value.astype(BF)
            else:
                total[:, at] = value
            return carry

        lax.fori_loop(part * tiles // parts, (part + 1) * tiles // parts, step, 0)

    def add(slot, other, first, columns):
        def step(i, carry):
            at = pl.ds(pl.multiple_of(first + i * 16, 16), 16)
            sent[slot, at, columns] = (sent[slot, at, columns].astype(F32) + got[other, at, columns].astype(F32)).astype(BF)
            return carry

        lax.fori_loop(0, half // 16, step, 0)

    def columns_of_part(part):
        return pl.ds(part * across, across)

    low, high = pl.ds(0, half), pl.ds(half, half)
    sums = (sent_sem, got_sem)
    product(order[0], first=True)
    pl.semaphore_wait(barrier, size - 1 + len(met))
    piece = rows // max(1, chips)
    crossing = []
    small = []
    if last:
        gain_rows, head_rows, gain_got, head_got, own_got, small_sent, small_got = rest[18:]
        attn_rows, feed_rows, two_heads = ins[1:]
        gain_rows[...] = jnp.zeros_like(gain_rows)
        head_rows[...] = jnp.zeros_like(head_rows)
        for i, part in enumerate((attn_rows, feed_rows)):
            gain_rows[i : i + 1, :] = jnp.sum(part[...], axis=0, keepdims=True)
            head_rows[i : i + 1, :] = jnp.sum(two_heads[8 * i : 8 * i + 8, :], axis=0, keepdims=True)
        own_width = outs[0].shape[1]

        def tell(source, target, device):
            copy = pltpu.make_async_remote_copy(
                src_ref=source,
                dst_ref=target,
                send_sem=small_sent.at[len(small)],
                recv_sem=small_got.at[len(small)],
                device_id=device,
                device_id_type=MESH,
            )
            copy.start()
            small.append(copy)

        for k in range(1, size):
            tell(gain_rows, gain_got.at[k - 1], {"tensor": flip(t, k)})
        for mask in met:
            tell(head_rows, head_got.at[mask - 1], {"context": flip(c, mask)})
    if chips and not last:
        source, target = ins[0], outs[0]
        for j in range(chips):
            crossing.append(
                cross(
                    j,
                    source.at[flip(c // 2, j), pl.ds(pl.multiple_of(t * piece, piece), piece), :],
                    target.at[pl.ds(j * piece, piece), :],
                    rest[13:15],
                )
            )
            crossing[-1].start()

    def home(part):
        at = columns_of_part(part)
        return [
            cross(j, mine.at[pl.ds(j * piece, piece), at], rest[17].at[pl.ds(j * piece, piece), at], rest[15:17], part * chips)
            for j in range(chips)
        ]

    def finish_last(part, group):
        at = columns_of_part(part)
        for copy in group[2:] if size == 4 else group:
            copy.wait_recv()

        def step(i, carry):
            row = pl.ds(pl.multiple_of(i * 16, 16), 16)
            summed = ins[0][row, at] + total[row, at]
            for other in range(2 if size == 4 else size - 1):
                summed = summed + got[other, row, at].astype(F32)
            mine[row, at] = summed.astype(BF)
            return carry

        lax.fori_loop(0, rows // 16, step, 0)
        for copy in home(part):
            copy.start()

    def sums_of(part):
        at = columns_of_part(part)
        return [
            send(6 * part + 0, sent.at[2, low, at], got.at[2, low, at], 1, sums),
            send(6 * part + 1, sent.at[2, high, at], got.at[2, high, at], 2, sums),
            send(6 * part + 2, sent.at[0, low, at], got.at[0, low, at], 1, sums),
            send(6 * part + 3, sent.at[1, high, at], got.at[1, high, at], 2, sums),
            send(6 * part + 4, sent.at[1, low, at], got.at[1, low, at], 2, sums),
            send(6 * part + 5, sent.at[0, high, at], got.at[0, high, at], 1, sums),
        ]

    if size == 4:
        groups = [sums_of(part) for part in range(parts)]
        copies = sum(groups, [])
        for part, group in enumerate(groups):
            for k, ready in ((3, group[:2]), (1, group[2:3]), (2, group[3:4])):
                if k != 3 or part:
                    product(k, first=k == 3, part=part)
                for copy in [] if last and part else ready:
                    copy.start()
        for part, group in enumerate(groups):
            at = columns_of_part(part)
            group[0].wait_recv()
            add(1, 2, 0, at)
            group[4].start()
            group[1].wait_recv()
            add(0, 2, half, at)
            group[5].start()
            for copy in groups[part + 1][:4] if last and part + 1 < parts else []:
                copy.start()
            product(0, part=part)
            if last and part + 1 < parts:
                finish_last(part, group)
        for group in [] if last else groups:
            for copy in group[2:]:
                copy.wait_recv()
        used = 2
    else:
        copies = [send(k - 1, sent.at[k - 1], got.at[k - 1], k, sums) for k in range(1, size)]
        copies[0].start()
        for k in range(2, size):
            product(k)
            copies[k - 1].start()
        product(0)
        groups = [copies]
        if not last:
            for copy in copies:
                copy.wait_recv()
        used = size - 1
    if last:
        finish_last(parts - 1, groups[-1])
    if chips and not last:
        crossing[0].wait()
        for copy in crossing[1:]:
            copy.wait_recv()

    def finish_rows(first, count, part=0):
        def step(i, carry):
            at = pl.ds(pl.multiple_of(first + i * 16, 16), 16)
            summed = total[at, :]
            for other in range(used):
                summed = summed + got[other, at, :].astype(F32)
            mine[at, :] = finish(at, summed, ins, outs).astype(BF)
            return carry

        lax.fori_loop(0, count // 16, step, 0)

    gather = (out_sem, in_sem)
    shared = rest[17] if last else mine
    own = pltpu.make_async_copy(shared, every.at[pl.ds(0, rows), :], own_sem)
    if last:
        going_home = [home(part) for part in range(parts)]
    else:
        going_home = [[cross(j, outs[1].at[pl.ds(j * piece, piece), :], outs[2].at[j], rest[15:17]) for j in range(chips)]]
    if last:
        for copy in small:
            copy.wait()
        for k in range(1, size):
            gain_rows[...] += gain_got[k - 1]
        outs[1][...] = head_rows[...]
        for mask in met:
            outs[1][...] += head_got[mask - 1]
        for mask in met:
            at = pl.ds(pl.multiple_of(flip(c, mask) * own_width, own_width), own_width)
            tell(gain_rows.at[:, at], own_got.at[mask - 1], {"context": flip(c, mask)})

    def came_home(first, count, part=0):
        for j in range(first // piece, (first + count) // piece):
            if j == 0:
                going_home[part][j].wait()
            else:
                going_home[part][j].wait_recv()

    out_parts = parts if last else 1
    make_ready = came_home if last else finish_rows
    then = [own] if last else [own, *going_home[0]]
    if size == 4:

        def out_columns(part):
            return pl.ds(part * (width // out_parts), width // out_parts)

        def chunk(k, side, part):
            return every.at[pl.ds(k * rows + side * half, half), out_columns(part)]

        def share(k, side, part):
            source = shared.at[pl.ds(side * half, half), out_columns(part)]
            return send(6 * part + 2 * k + side, source, chunk(k + 1, side, part), k + 1, gather)

        groups = []
        for part in range(out_parts):
            shares = [share(k, side, part) for k in (0, 1) for side in (0, 1)]
            passed = [
                send(6 * part + 4, chunk(1, 0, part), chunk(3, 0, part), 2, gather),
                send(6 * part + 5, chunk(2, 1, part), chunk(3, 1, part), 1, gather),
            ]
            groups.append(shares + passed)
        for part, group in enumerate(groups):
            make_ready(0, half, part)
            group[0].start()
            group[2].start()
            make_ready(half, half, part)
            group[3].start()
            group[1].start()
            if part == out_parts - 1:
                for copy in then:
                    copy.start()
            group[0].wait_recv()
            group[4].start()
            group[3].wait_recv()
            group[5].start()
        for group in groups:
            for at in (1, 2, 4, 5):
                group[at].wait_recv()
        shares = sum(groups, [])
    else:
        make_ready(0, rows)
        shares = [send(k - 1, shared, every.at[pl.ds(k * rows, rows), :], k, gather) for k in range(1, size)]
        for copy in [*shares, *then]:
            copy.start()
        for copy in shares:
            copy.wait_recv()
    own.wait()
    if chips and not last:
        came_home(0, rows)
    if last:
        for copy in small[size - 1 + len(met) :]:
            copy.wait()
        outs[0][...] = gain_rows[:, pl.ds(pl.multiple_of(c * own_width, own_width), own_width)]
        for mask in met:
            outs[0][...] += own_got[mask - 1]
    for copy in copies + shares + crossing[1:] + sum([group[1:] for group in going_home], []):
        copy.wait_send()


def exchange(name, number, a, w, finish, ins, outs, offset=0, chips=0, last=False):
    size = lax.axis_size("tensor")
    rows, width, depth = a.shape[0] // size, w.shape[0], a.shape[1]
    tile = min(512, width)
    parts = width // tile if size == 4 else 1
    links = 6 * parts if size == 4 else size - 1
    whole = pl.BlockSpec(memory_space=pltpu.VMEM)
    anywhere = pl.BlockSpec(memory_space=pl.ANY)
    dma = pltpu.SemaphoreType.DMA
    gain_scratch = []
    if last:
        own, head_width = outs[0][0][1], outs[1][0][1]
        ranks = 2 * chips
        gain_scratch = [
            pltpu.VMEM((rows, width), BF),
            pltpu.VMEM((8, width), F32),
            pltpu.VMEM((8, head_width), F32),
            pltpu.VMEM((size - 1, 8, width), F32),
            pltpu.VMEM((ranks - 1, 8, head_width), F32),
            pltpu.VMEM((ranks - 1, 8, own), F32),
            dma((size - 1 + 2 * (ranks - 1),)),
            dma((size - 1 + 2 * (ranks - 1),)),
        ]
    return pl.pallas_call(
        functools.partial(exchange_kernel, size, width, depth, offset, tile, finish, chips, last, len(ins), len(outs)),
        in_specs=[anywhere, anywhere] + [anywhere if chips and not last and i == 0 else whole for i in range(len(ins))],
        out_specs=[anywhere] + [whole] * len(outs),
        out_shape=[jax.ShapeDtypeStruct((size * rows, width), BF)] + [jax.ShapeDtypeStruct(*out) for out in outs],
        scratch_shapes=[
            pltpu.VMEM((size * rows, depth), BF),
            pltpu.VMEM((width, depth), BF),
            pltpu.VMEM((size - 1, rows, width), BF),
            pltpu.VMEM((size - 1, rows, width), BF),
            pltpu.VMEM((rows, width), F32),
            pltpu.VMEM((rows, width), BF),
            dma((size,)),
            dma((width // tile,)),
            dma((links,)),
            dma((links,)),
            dma((links,)),
            dma((links,)),
            dma,
        ]
        + [dma((chips * parts,))] * (4 if chips else 0)
        + gain_scratch,
        compiler_params=pltpu.CompilerParams(vmem_limit_bytes=VMEM_LIMIT, collective_id=number, has_side_effects=True),
        cost_estimate=pl.CostEstimate(flops=2 * size * rows * width * depth, bytes_accessed=240_000_000, transcendentals=0),
        name=name,
    )(a, w, *ins)


def add_rows(ref, values):
    ref[...] += values[:8] + values[8:]


def finish_attended(at, attended, ins, outs):
    tokens, gain = ins
    outs[0][at, :] = attended
    hidden = tokens[at, :].astype(F32) + attended * norm_factor(attended) * gain[...]
    outs[1][at, :] = hidden
    return hidden


def finish_hidden_grad(at, summed, ins, outs):
    attended, cotangent, gain = ins
    hidden_grad = cotangent[at, :].astype(F32) + summed
    outs[0][at, :] = hidden_grad
    values = attended[at, :]
    grad, gain_rows = norm_back(values, norm_factor(values), gain[...], hidden_grad)
    add_rows(outs[1], gain_rows)
    return grad


def remote(source, target, sems, slot, device):
    return pltpu.make_async_remote_copy(
        src_ref=source,
        dst_ref=target,
        send_sem=sems[0].at[slot],
        recv_sem=sems[1].at[slot],
        device_id=device,
        device_id_type=MESH,
    )


def meet(t, c, size, masks):
    barrier = pltpu.get_barrier_semaphore()
    for k in range(1, size):
        pl.semaphore_signal(barrier, inc=1, device_id={"tensor": flip(t, k)}, device_id_type=MESH)
    for mask in masks:
        pl.semaphore_signal(barrier, inc=1, device_id={"context": flip(c, mask)}, device_id_type=MESH)
    return lambda: pl.semaphore_wait(barrier, size - 1 + len(masks))


class Line:
    def __init__(self, chips, own, buf, up_sems, down_sems, core_sems):
        self.chips, self.own, self.buf = chips, own, buf
        self.sems, self.core_sems = {1: up_sems, -1: down_sems}, core_sems
        self.c = lax.axis_index("context")
        self.s, self.core = self.c // 2, self.c % 2

    def rows(self, chip, part=None):
        base = (2 * chip + self.core) * self.own
        if part is None:
            return pl.ds(pl.multiple_of(base, self.own), self.own)
        half = self.own // 2
        return pl.ds(pl.multiple_of(base + part * half, half), half)

    def hop(self, k, way, chip, part):
        ref = self.buf.at[self.rows(chip, part), :]
        return remote(ref, ref, self.sems[way], 2 * k + part, {"context": self.c + 2 * way})

    def cross(self, k, way, chip, part):
        ref = self.buf.at[self.rows(chip, part), :]
        slot = 0 if k < 0 else 1 + 2 * k + (way < 0)
        return remote(ref, ref, self.core_sems, 2 * slot + part, {"context": flip(self.c, 1)})

    def sends(self, k, way):
        if way > 0:
            return (self.s >= k) & (self.s < self.chips - 1)
        return (self.s + k < self.chips) & (self.s > 0)

    def gets(self, k, way):
        return self.s >= k + 1 if way > 0 else self.s + k + 1 < self.chips

    def each(self, test, k, act):
        for way in (1, -1):
            pl.when(test(k, way))(functools.partial(act, k, way))

    def start(self, k, part):
        self.each(self.sends, k, lambda k, way: self.hop(k, way, self.s - way * k, part).start())

    def begin(self):
        for part in range(2):
            self.start(0, part)
            self.cross(-1, 1, self.s, part).start()

    def advance(self, k, parts=(0, 1)):
        for part in parts:

            def got(k, way):
                chip = self.s - way * (k + 1)
                self.hop(k, way, chip, part).wait_recv()
                self.cross(k, way, chip, part).start()

            self.each(self.gets, k, got)
            if k + 1 < self.chips - 1:
                self.start(k + 1, part)

    def other_core(self, k):
        for part in range(2):
            if k < 0:
                self.cross(-1, 1, self.s, part).wait_recv()
            else:
                self.each(self.gets, k, lambda k, way: self.cross(k, way, self.s - way * (k + 1), part).wait_recv())

    def end(self):
        for part in range(2):
            self.cross(-1, 1, self.s, part).wait_send()
            for k in range(self.chips - 1):
                self.each(self.sends, k, lambda k, way: self.hop(k, way, self.s - way * k, part).wait_send())
                self.each(self.gets, k, lambda k, way: self.cross(k, way, self.s - way * (k + 1), part).wait_send())


def line_sems(chips):
    dma = pltpu.SemaphoreType.DMA
    return [dma((2 * (chips - 1),))] * 4 + [dma((2 * (2 * chips - 1),))] * 2


class Sums:
    def __init__(self, size, t, sent, got, columns, sems, base):
        rows = sent.shape[1]
        low, high = pl.ds(0, rows // 2), pl.ds(rows // 2, rows // 2)
        self.size, self.sent, self.got, self.columns, self.half = size, sent, got, columns, rows // 2

        def send(slot, of, to, at, partner):
            return remote(sent.at[of, at, columns], got.at[to, at, columns], sems, base + slot, {"tensor": flip(t, partner)})

        if size == 4:
            self.copies = [
                send(0, 2, 2, low, 1),
                send(1, 2, 2, high, 2),
                send(2, 0, 0, low, 1),
                send(3, 1, 1, high, 2),
                send(4, 1, 1, low, 2),
                send(5, 0, 0, high, 1),
            ]
            self.after_product = {3: self.copies[:2], 1: self.copies[2:3], 2: self.copies[3:4]}
        else:
            self.copies = [send(k - 1, k - 1, k - 1, pl.ds(0, rows), k) for k in range(1, size)]
            self.after_product = {k: self.copies[k - 1 : k] for k in range(1, size)}

    def pass_on(self):
        if self.size != 4:
            return
        for copy, slot, first, then in ((0, 1, 0, 4), (1, 0, self.half, 5)):
            self.copies[copy].wait_recv()

            def step(i, carry):
                at = pl.ds(pl.multiple_of(first + i * 16, 16), 16)
                summed = self.sent[slot, at, self.columns].astype(F32) + self.got[2, at, self.columns].astype(F32)
                self.sent[slot, at, self.columns] = summed.astype(BF)
                return carry

            lax.fori_loop(0, self.half // 16, step, 0)
            self.copies[then].start()

    def wait(self):
        for copy in self.copies[2:] if self.size == 4 else self.copies:
            copy.wait_recv()


class Gather:
    def __init__(self, size, t, shared, every, sems, own_sem):
        rows = every.shape[0] // size
        half = rows // 2
        self.size = size
        self.own = pltpu.make_async_copy(shared, every.at[pl.ds(0, rows), :], own_sem)

        def chunk(k, side):
            return every.at[pl.ds(k * rows + side * half, half), :]

        def send(slot, source, target, partner):
            return remote(source, target, sems, slot, {"tensor": flip(t, partner)})

        if size == 4:
            self.copies = [send(2 * k + side, shared.at[pl.ds(side * half, half), :], chunk(k + 1, side), k + 1) for k in (0, 1) for side in (0, 1)]
            self.copies += [send(4, chunk(1, 0), chunk(3, 0), 2), send(5, chunk(2, 1), chunk(3, 1), 1)]
            self.ready = (self.copies[0:3:2], self.copies[3:0:-2])
        else:
            self.copies = [send(k - 1, shared, every.at[pl.ds(k * rows, rows), :], k) for k in range(1, size)]
            self.ready = ((), self.copies)

    def start(self, side):
        for copy in self.ready[side]:
            copy.start()
        if side:
            self.own.start()

    def pass_on(self):
        if self.size == 4:
            self.copies[0].wait_recv()
            self.copies[4].start()
            self.copies[3].wait_recv()
            self.copies[5].start()

    def wait(self):
        for at, copy in enumerate(self.copies):
            if self.size != 4 or at not in (0, 3):
                copy.wait_recv()
        self.own.wait()

    def end(self):
        for copy in self.copies:
            copy.wait_send()


def links_of(size):
    return 6 if size == 4 else size - 1


def start_kernel(size, chips, offsets, n_pair, *refs):
    tokens_ref, firsts, refs = refs[0], refs[1 : 1 + len(offsets)], refs[1 + len(offsets) :]
    turned_ref, gains_ref, pair, refs = refs[0], refs[1], refs[2 : 2 + n_pair], refs[2 + n_pair :]
    every, out, both, shard = refs[:4]
    line_refs, gather, coming, own_sem, keep_sem, whole, turned, out_sem = refs[4:10], refs[10:12], refs[12:14], *refs[14:19]
    t, c = lax.axis_index("tensor"), lax.axis_index("context")
    s = c // 2
    rows = shard.shape[0]
    piece = rows // chips
    own = firsts[0].shape[0]
    line = Line(chips, own, whole, line_refs[0:2], line_refs[2:4], line_refs[4:6])
    wait_others = meet(t, c, size, [1, *range(2, 2 * chips, 2)])
    kept = [
        pltpu.make_async_copy(first, whole.at[line.rows(s), pl.ds(offset, first.shape[1])], keep_sem.at[i])
        for i, (first, offset) in enumerate(zip(firsts, offsets))
    ]
    across = pair[0].shape[1]
    kept += [
        pltpu.make_async_copy(part, both.at[:, pl.ds(i * across, across)], keep_sem.at[len(offsets) + i]) for i, part in enumerate(pair)
    ]
    turned_copy = pltpu.make_async_copy(turned_ref, turned, keep_sem.at[len(offsets) + n_pair])
    for copy in [turned_copy, *kept]:
        copy.start()
    after_firsts = sum(first.shape[1] for first in firsts)
    height = turned.shape[0]
    turned_copy.wait()
    whole[line.rows(s), after_firsts : after_firsts + height] = turned[...].astype(F32).T.astype(BF)
    gains = jnp.concatenate([gains_ref[...].astype(F32), jnp.zeros((HD - gains_ref.shape[0], own), F32)], axis=0)
    whole[line.rows(s), after_firsts + height :] = gains.T.astype(BF)
    arrivals = [
        (tokens_ref.at[flip(s, j), pl.ds(pl.multiple_of(t * piece, piece), piece), :], shard.at[pl.ds(j * piece, piece), :])
        for j in range(chips)
    ]
    first = pltpu.make_async_copy(*arrivals[0], coming[0].at[0])
    others = [remote(*arrivals[j], coming, j, {"context": flip(c, 2 * j)}) for j in range(1, chips)]
    wait_others()
    for copy in [first, *others]:
        copy.start()
    for copy in kept:
        copy.wait()
    line.begin()
    first.wait()
    for copy in others:
        copy.wait_recv()
    share = Gather(size, t, shard, every, gather, own_sem)
    share.start(0)
    share.start(1)

    def write(k, way, chip):
        at = pl.ds(pl.multiple_of(chip * 2 * own, 2 * own), 2 * own)
        return pltpu.make_async_copy(whole.at[at, :], out.at[at, :], out_sem.at[0 if k < 0 else 1 + 2 * k + (way < 0)])

    def keep(k):
        line.other_core(k)
        line.each(line.gets, k, lambda k, way: write(k, way, s - way * (k + 1)).start())

    line.advance(0)
    line.other_core(-1)
    write(-1, 1, s).start()
    share.pass_on()
    for k in range(1, chips - 1):
        line.advance(k)
        keep(k - 1)
    share.wait()
    keep(chips - 2)
    line.end()
    share.end()
    for copy in others:
        copy.wait_send()
    write(-1, 1, s).wait()
    for k in range(chips - 1):
        line.each(line.gets, k, lambda k, way: write(k, way, s - way * (k + 1)).wait())


def start(tokens, firsts, turned, gains, pair, chips):
    size = lax.axis_size("tensor")
    seqs, local_len, width = tokens.shape
    rows = seqs * local_len // size
    own = firsts[0].shape[0]
    offsets, across = [], 0
    for first in firsts:
        offsets.append(across)
        across += first.shape[1]
    across += turned.shape[0] + HD
    dma = pltpu.SemaphoreType.DMA
    anywhere, in_vmem = pl.BlockSpec(memory_space=pl.ANY), pl.BlockSpec(memory_space=pltpu.VMEM)
    shape = jax.ShapeDtypeStruct
    return pl.pallas_call(
        functools.partial(start_kernel, size, chips, offsets, len(pair)),
        in_specs=[anywhere] * (2 + len(firsts)) + [in_vmem] + [anywhere] * len(pair),
        out_specs=[anywhere] * 2 + [in_vmem] * 2,
        out_shape=[
            shape((size * rows, width), BF),
            shape((2 * chips * own, across), BF),
            shape((own, sum(part.shape[1] for part in pair)), BF),
            shape((rows, width), BF),
        ],
        scratch_shapes=line_sems(chips)
        + [dma((links_of(size),))] * 2
        + [dma((chips,))] * 2
        + [dma, dma((len(firsts) + len(pair) + 1,))]
        + [pltpu.VMEM((2 * chips * own, across), BF), pltpu.VMEM(turned.shape, BF), dma((2 * chips - 1,))],
        compiler_params=pltpu.CompilerParams(vmem_limit_bytes=VMEM_LIMIT, collective_id=8, has_side_effects=True),
        cost_estimate=pl.CostEstimate(flops=0, bytes_accessed=300_000_000, transcendentals=0),
        name="start",
    )(tokens, *firsts, turned, gains, *pair)


def feed_kernel(size, chips, tile, *refs):
    h_ref, gate_up_w_ref, down_ref, cotangent_ref, residual_ref, gain_ref = refs[:6]
    every, slopes_ref, act_ref, down_all_ref, upstream, output, pieces, gain_rows = refs[6:14]
    h_buf, w_buf, act, down, sent, got, total, mine, stage = refs[14:23]
    h_sem, w_sem, stage_sem, keep_sem, own_sem = refs[23:28]
    line_refs, sums, gather, coming, going = refs[28:34], refs[34:36], refs[36:38], refs[38:40], refs[40:42]
    t, c = lax.axis_index("tensor"), lax.axis_index("context")
    s = c // 2
    rows, width = total.shape
    hidden = act.shape[1]
    own = down_ref.shape[0]
    piece = rows // chips
    tiles = hidden // tile
    order = [3, 1, 2, 0] if size == 4 else [*range(1, size), 0]
    line = Line(chips, own, down, line_refs[0:2], line_refs[2:4], line_refs[4:6])

    def h_copy(k):
        at = pl.ds(k * rows, rows)
        return pltpu.make_async_copy(h_ref.at[at, :], h_buf.at[at, :], h_sem.at[k])

    def w_copy(j, i):
        at = pl.ds(pl.multiple_of(i * hidden + j * tile, tile), tile)
        return pltpu.make_async_copy(gate_up_w_ref.at[:, at], w_buf.at[:, at], w_sem.at[j, i])

    own_rows = line.rows(s)
    own_down = pltpu.make_async_copy(down_ref, down.at[own_rows, :], keep_sem.at[0])
    own_down.start()
    wait_others = meet(t, c, size, [1, *range(2, 2 * chips, 2)])
    h_copy(order[0]).start()
    for j in range(tiles):
        for i in range(2):
            w_copy(j, i).start()
    for k in order[1:]:
        h_copy(k).start()
    gain_rows[...] = jnp.zeros_like(gain_rows)
    own_down.wait()
    wait_others()
    line.begin()

    def stage_copy(slot, i, k, j):
        at = pl.ds(pl.multiple_of(i * hidden + j * tile, tile), tile)
        return pltpu.make_async_copy(stage.at[slot, i], slopes_ref.at[pl.ds(k * rows, rows), at], stage_sem.at[slot, i])

    for n, k in enumerate(order):
        h_copy(k).wait()
        chunk = pl.ds(k * rows, rows)

        def step(j, carry):
            slot = (n * tiles + j) % 2
            if n == 0:
                for i in range(2):
                    w_copy(j, i).wait()

            @pl.when(n * tiles + j >= 2)
            def _():
                for i in range(2):
                    stage_copy(slot, i, k, j).wait()

            gate, up = [
                dot_nn(h_buf[chunk, :], w_buf[:, pl.ds(pl.multiple_of(i * hidden + j * tile, tile), tile)]) for i in range(2)
            ]
            logistic = jax.nn.sigmoid(gate)
            silu = gate * logistic
            act[chunk, pl.ds(pl.multiple_of(j * tile, tile), tile)] = (silu * up).astype(BF)
            stage[slot, 0] = (up * (logistic + silu * (1.0 - logistic))).astype(BF)
            stage[slot, 1] = silu.astype(BF)
            for i in range(2):
                stage_copy(slot, i, k, j).start()
            return carry

        lax.fori_loop(0, tiles, step, 0)
        if n + 1 == size // 2:
            line.advance(0, (0,))
        if n + 1 == size * 3 // 4:
            line.advance(0, (1,))
    for slot in range(2):
        for i in range(2):
            stage_copy(slot, i, 0, 0).wait()
    act_out = pltpu.make_async_copy(act, act_ref, keep_sem.at[1])
    act_out.start()

    rounds = []

    def fed_round(i):
        at = pl.ds(pl.multiple_of(flip(s, i) * 2 * own, 2 * own), 2 * own)
        group = Sums(size, t, sent, got, at, sums, links_of(size) * i)
        for k in order:
            value = dot_nt(act[k * rows : (k + 1) * rows, :], down[at, :])
            if k:
                sent[k - 1, :, at] = value.astype(BF)
                for copy in group.after_product[k]:
                    copy.start()
            else:
                total[:, at] = value
        rounds.append(group)

    if chips > 2:
        line.advance(1, (0,))
    line.other_core(-1)
    fed_round(0)
    line.other_core(0)
    fed_round(1)
    if chips > 2:
        line.advance(1, (1,))
    rounds[0].pass_on()
    rounds[1].pass_on()
    arrivals = [
        (cotangent_ref.at[flip(s, j), pl.ds(pl.multiple_of(t * piece, piece), piece), :], upstream.at[pl.ds(j * piece, piece), :])
        for j in range(chips)
    ]
    first = pltpu.make_async_copy(*arrivals[0], coming[0].at[0])
    others = [remote(*arrivals[j], coming, j, {"context": flip(c, 2 * j)}) for j in range(1, chips)]
    for k in range(1, chips - 1):
        if k > 1:
            line.advance(k)
        if k + 1 == chips - 1:
            for copy in [first, *others]:
                copy.start()
        line.other_core(k)
        fed_round(k + 1)
        rounds[k + 1].pass_on()
    down_out = pltpu.make_async_copy(down, down_all_ref, keep_sem.at[2])
    down_out.start()
    for group in rounds:
        group.wait()
    used = 2 if size == 4 else size - 1

    def finish_rows(side):
        def step(i, carry):
            at = pl.ds(pl.multiple_of(side * (rows // 2) + i * 16, 16), 16)
            fed = total[at, :]
            for other in range(used):
                fed = fed + got[other, at, :].astype(F32)
            factor = norm_factor(fed)
            output[at, :] = (residual_ref[at, :] + fed * factor * gain_ref[...]).astype(BF)
            grad, gains = norm_back(fed, factor, gain_ref[...], upstream[at, :].astype(F32))
            gain_rows[...] += gains[:8] + gains[8:]
            mine[at, :] = grad.astype(BF)
            return carry

        lax.fori_loop(0, rows // 32, step, 0)

    share = Gather(size, t, mine, every, gather, own_sem)
    first.wait()
    for copy in others[: chips // 2 - 1]:
        copy.wait_recv()
    finish_rows(0)
    share.start(0)
    for copy in others[chips // 2 - 1 :]:
        copy.wait_recv()
    finish_rows(1)
    share.start(1)
    kept = pltpu.make_async_copy(output.at[pl.ds(0, piece), :], pieces.at[0], going[0].at[0])
    gone = [
        remote(output.at[pl.ds(j * piece, piece), :], pieces.at[j], going, j, {"context": flip(c, 2 * j)})
        for j in range(1, chips)
    ]
    for copy in [kept, *gone]:
        copy.start()
    share.pass_on()
    share.wait()
    kept.wait()
    for copy in gone:
        copy.wait_recv()
    act_out.wait()
    down_out.wait()
    line.end()
    share.end()
    for copy in [*sum([group.copies for group in rounds], []), *others, *gone]:
        copy.wait_send()


def feed(hidden_low, gate_up_weight, down_shard, cotangent, residual, gain, chips):
    size = lax.axis_size("tensor")
    count, width = hidden_low.shape
    rows = count // size
    own, hidden = down_shard.shape
    ranks = 2 * chips
    tile = min(512, hidden)
    links = links_of(size)
    dma = pltpu.SemaphoreType.DMA
    anywhere, whole = pl.BlockSpec(memory_space=pl.ANY), pl.BlockSpec(memory_space=pltpu.VMEM)
    shape = jax.ShapeDtypeStruct
    return pl.pallas_call(
        functools.partial(feed_kernel, size, chips, tile),
        in_specs=[anywhere] * 4 + [whole] * 2,
        out_specs=[anywhere] * 4 + [whole] * 4,
        out_shape=[
            shape((count, width), BF),
            shape((count, 2 * hidden), BF),
            shape((count, hidden), BF),
            shape((ranks * own, hidden), BF),
            shape((rows, width), BF),
            shape((rows, width), BF),
            shape((chips, rows // chips, width), BF),
            shape((8, width), F32),
        ],
        scratch_shapes=[
            pltpu.VMEM((count, width), BF),
            pltpu.VMEM((width, 2 * hidden), BF),
            pltpu.VMEM((count, hidden), BF),
            pltpu.VMEM((ranks * own, hidden), BF),
            pltpu.VMEM((size - 1, rows, width), BF),
            pltpu.VMEM((size - 1, rows, width), BF),
            pltpu.VMEM((rows, width), F32),
            pltpu.VMEM((rows, width), BF),
            pltpu.VMEM((2, 2, rows, tile), BF),
            dma((size,)),
            dma((hidden // tile, 2)),
            dma((2, 2)),
            dma((3,)),
            dma,
        ]
        + line_sems(chips)
        + [dma((links * chips,))] * 2
        + [dma((links,))] * 2
        + [dma((chips,))] * 4,
        compiler_params=pltpu.CompilerParams(vmem_limit_bytes=VMEM_LIMIT, collective_id=2, has_side_effects=True),
        cost_estimate=pl.CostEstimate(flops=6 * count * width * hidden, bytes_accessed=400_000_000, transcendentals=count * hidden),
        name="feed",
    )(hidden_low, gate_up_weight, down_shard, cotangent, residual, gain)


def turn(values, cosine, sine):
    heads = [values[:, i : i + HD] for i in range(0, values.shape[1], HD)]
    return jnp.concatenate([head * cosine + pltpu.roll(head, HD // 2, 1) * sine for head in heads], axis=1)


def turn_kernel(core_ref, raw_ref, column_ref, gain_ref, cosine_ref, sine_ref, keep_ref, send_ref):
    width = gain_ref.shape[1]
    half = width // 2
    cosine, sine = cosine_ref[...], sine_ref[...]
    first = core_ref[0] == 0
    for i in range(3):
        values = raw_ref[:, i * width : (i + 1) * width]
        if i < 2:
            values = turn(values * column_ref[:, i : i + 1] * gain_ref[i : i + 1, :], cosine, sine)
        low, high = values[:, :half].astype(BF), values[:, half:].astype(BF)
        keep_ref[i] = jnp.where(first, low, high)
        send_ref[i] = jnp.where(first, high, low)


def head_grads(core_ref, own_ref, other_ref, i):
    first = core_ref[0] == 0
    own, other = own_ref[i], other_ref[i]
    return jnp.concatenate([jnp.where(first, own, other), jnp.where(first, other, own)], axis=1).astype(F32)


def inner_kernel(core_ref, own_ref, other_ref, raw_ref, column_ref, gain_ref, cosine_ref, sine_ref, inner_ref, gains_ref):
    width = gain_ref.shape[1]
    cosine, sine = cosine_ref[...], -sine_ref[...]

    @pl.when(pl.program_id(0) == 0)
    def _():
        gains_ref[...] = jnp.zeros_like(gains_ref)

    for i in range(2):
        flat = turn(head_grads(core_ref, own_ref, other_ref, i), cosine, sine) * raw_ref[:, i * width : (i + 1) * width]
        inner_ref[i] = lax.dot_general(
            jnp.ones((8, width), F32),
            flat * gain_ref[i : i + 1, :],
            (((1,), (1,)), ((), ())),
            precision=lax.Precision.HIGHEST,
            preferred_element_type=F32,
        )
        flat = flat * column_ref[:, i : i + 1]
        gains_ref[i] += jnp.sum(flat.reshape(-1, 8, width), axis=0)


def raw_grad_kernel(core_ref, own_ref, other_ref, raw_ref, column_ref, gain_ref, cosine_ref, sine_ref, out_ref):
    width = gain_ref.shape[1]
    cosine, sine = cosine_ref[...], -sine_ref[...]
    for i in range(3):
        values = head_grads(core_ref, own_ref, other_ref, i)
        if i < 2:
            values = turn(values, cosine, sine) * column_ref[:, i : i + 1] * gain_ref[i : i + 1, :]
            values = values - raw_ref[:, i * width : (i + 1) * width] * column_ref[:, i + 2 : i + 3]
        out_ref[:, i * width : (i + 1) * width] = values.astype(BF)


def by_rows(kernel, name, core, ins, outs, rows=256):
    def spec(shape, dim):
        block = tuple(rows if i == dim else extent for i, extent in enumerate(shape))
        return pl.BlockSpec(block, lambda i, core: tuple(i if at == dim else 0 for at in range(len(shape))))

    count = next(out[0][dim] for *out, dim in outs if dim is not None)
    return pl.pallas_call(
        kernel,
        grid_spec=pltpu.PrefetchScalarGridSpec(
            num_scalar_prefetch=1,
            grid=(count // rows,),
            in_specs=[spec((array.shape[0], count, array.shape[2]) if dim == 1 else array.shape, dim) for array, dim in ins],
            out_specs=[spec(shape, dim) for shape, _, dim in outs],
        ),
        out_shape=[jax.ShapeDtypeStruct(shape, dtype) for shape, dtype, _ in outs],
        compiler_params=pltpu.CompilerParams(vmem_limit_bytes=VMEM_LIMIT),
        name=name,
    )(core[None].astype(jnp.int32), *[array for array, _ in ins])


def act_back_kernel(tile, grad_ref, w_ref, slopes_ref, out_ref):
    hidden = w_ref.shape[1]
    for j in range(0, hidden, tile):
        act_grad = dot_nn(grad_ref[...], w_ref[:, j : j + tile])
        for at in (j, hidden + j):
            out_ref[:, at : at + tile] = (act_grad * slopes_ref[:, at : at + tile].astype(F32)).astype(BF)


def act_back(fed_low, w_down, slopes):
    count, width = fed_low.shape
    hidden = w_down.shape[1]
    rows = 256
    return pl.pallas_call(
        functools.partial(act_back_kernel, 512),
        grid=(count // rows,),
        in_specs=[
            pl.BlockSpec((rows, width), lambda i: (i, 0)),
            pl.BlockSpec((width, hidden), lambda i: (0, 0)),
            pl.BlockSpec((rows, 2 * hidden), lambda i: (i, 0)),
        ],
        out_specs=pl.BlockSpec((rows, 2 * hidden), lambda i: (i, 0)),
        out_shape=jax.ShapeDtypeStruct((count, 2 * hidden), BF),
        compiler_params=pltpu.CompilerParams(vmem_limit_bytes=VMEM_LIMIT),
        cost_estimate=pl.CostEstimate(flops=2 * count * width * hidden, bytes_accessed=40_000_000, transcendentals=count * hidden),
        name="act_back",
    )(fed_low, w_down, slopes)


def rank_sums_kernel(chips, size, tile, count, carries, *refs):
    lefts, rights, refs = refs[:count], refs[count : 2 * count], refs[2 * count :]
    if carries:
        carried_ref, out_ref, every_ref, *refs = refs
    else:
        out_ref, *refs = refs
    left_bufs, right_bufs = refs[:count], refs[count : 2 * count]
    passed, got, out, left_sem, right_sem, out_sem, sent_sem, got_sem = refs[2 * count : 2 * count + 8]
    t, c = lax.axis_index("tensor"), lax.axis_index("context")
    core = c % 2
    own = out.shape[1]
    blocks = [(j, core_at) for core_at in (1, 0) for j in range(chips)]

    def left_copy(i, j, core_at):
        rank = 2 * j + (core if core_at == 0 else 1 - core)
        at = pl.ds(pl.multiple_of(rank * own, own), own)
        block = left_bufs[i].at[core_at * chips + j]
        return pltpu.make_async_copy(lefts[i].at[:, at], block, left_sem.at[i, core_at * chips + j])

    tiles = [right.shape[1] // tile for right in rights]

    def right_copy(i, n):
        at = pl.ds(pl.multiple_of(n * tile, tile), tile)
        return pltpu.make_async_copy(rights[i].at[:, at], right_bufs[i].at[:, at], right_sem.at[i, n])

    wait_others = meet(t, c, size if carries else 1, [1])
    for i in range(count):
        left_copy(i, *blocks[0]).start()
        for n in range(tiles[i]):
            right_copy(i, n).start()
        for block in blocks[1:]:
            left_copy(i, *block).start()
    wait_others()
    if carries:
        sent_out, got_out, own_sem = refs[2 * count + 8 :]
        part = carried_ref.at[pl.ds(carries[0], carries[1]), :]
        share = Gather(size, t, part, every_ref, (sent_out, got_out), own_sem)
        share.start(0)
        share.start(1)
    def send(j):
        return remote(passed.at[j], got.at[j], (sent_sem, got_sem), j, {"context": flip(c, 1)})

    def write(j):
        return pltpu.make_async_copy(out.at[j], out_ref.at[pl.ds(pl.multiple_of(j * own, own), own), :], out_sem.at[j])

    def block(core_at, j, carry):
        base = 0
        if core_at == 0:
            send(j).wait_recv()
        for i in range(count):
            left_copy(i, j, core_at).wait()
            left = left_bufs[i][core_at * chips + j].T
            for n in range(tiles[i]):
                if core_at:
                    pl.when(j == 0)(right_copy(i, n).wait)
                to = slice(base + n * tile, base + (n + 1) * tile)
                part = dot_nn(left, right_bufs[i][:, n * tile : (n + 1) * tile])
                if core_at:
                    passed[j, :, to] = part.astype(BF)
                else:
                    out[j, :, to] = (part + got[j, :, to].astype(F32)).astype(BF)
            base += tiles[i] * tile
        (send if core_at else write)(j).start()
        if carries and core_at == 0:
            pl.when(j == 1)(share.pass_on)
        return carry

    lax.fori_loop(0, chips, functools.partial(block, 1), 0)
    lax.fori_loop(0, chips, functools.partial(block, 0), 0)
    for j in range(chips):
        send(j).wait_send()
        write(j).wait()
    if carries:
        share.wait()
        share.end()


def rank_sums(number, pairs, own, carried=None):
    size = lax.axis_size("tensor")
    lefts, rights = [left for left, _ in pairs], [right for _, right in pairs]
    count, width = lefts[0].shape
    chips = width // (2 * own)
    across = sum(right.shape[1] for right in rights)
    tile = min(512, *[right.shape[1] for right in rights])
    most = max(right.shape[1] for right in rights) // tile
    more = [] if carried is None else [carried[0]]
    dma = pltpu.SemaphoreType.DMA
    return pl.pallas_call(
        functools.partial(rank_sums_kernel, chips, size, tile, len(pairs), carried and carried[1:]),
        in_specs=[pl.BlockSpec(memory_space=pl.ANY)] * (2 * len(pairs) + len(more)),
        out_specs=[pl.BlockSpec(memory_space=pl.ANY)] * (1 + len(more)),
        out_shape=[jax.ShapeDtypeStruct((chips * own, across), BF)]
        + [jax.ShapeDtypeStruct((size * carried[2], rows.shape[1]), BF) for rows in more],
        scratch_shapes=[pltpu.VMEM((2 * chips, count, own), BF)] * len(pairs)
        + [pltpu.VMEM(right.shape, BF) for right in rights]
        + [pltpu.VMEM((chips, own, across), BF)] * 3
        + [dma((len(pairs), 2 * chips)), dma((len(pairs), most)), dma((chips,)), dma((chips,)), dma((chips,))]
        + [dma((links_of(size),)), dma((links_of(size),)), dma] * len(more),
        compiler_params=pltpu.CompilerParams(vmem_limit_bytes=VMEM_LIMIT, collective_id=number, has_side_effects=True),
        cost_estimate=pl.CostEstimate(flops=2 * count * width * across, bytes_accessed=60_000_000, transcendentals=0),
        name="rank_sums",
    )(*lefts, *rights, *more)


def columns_of(*values):
    stacked = jnp.stack(values, axis=1)
    return jnp.pad(stacked, ((0, 0), (0, 8 - len(values))))


def in_order(at_ref, source, target, piece, other=None):
    rows = source.shape[0]

    def step(p, carry):
        start = at_ref[p]
        at = pl.ds(pl.multiple_of(start % rows, piece), piece)
        values = source[at, :]
        if other is not None:
            values = jnp.where(start < rows, values, other[at, :])
        target[pl.ds(pl.multiple_of(p * piece, piece), piece), :] = values
        return carry

    lax.fori_loop(0, target.shape[0] // piece, step, 0)


def out_of_order(at_ref, source, target, piece):
    def step(p, carry):
        start = pl.multiple_of(at_ref[p], piece)
        target[pl.ds(start, piece), :] = source[pl.ds(pl.multiple_of(p * piece, piece), piece), :].astype(target.dtype)
        return carry

    lax.fori_loop(0, source.shape[0] // piece, step, 0)


def causal(tile):
    key_at = lax.broadcasted_iota(jnp.int32, (tile, tile), 0)
    query_at = lax.broadcasted_iota(jnp.int32, (tile, tile), 1)
    return query_at >= key_at


def attend_kernel(piece, tile, at_ref, own_ref, other_ref, out_ref, log_ref, query, key, value, value_t, mixed):
    for slot, held in enumerate((query, key, value)):
        in_order(at_ref, own_ref.at[slot], held, piece, other_ref.at[slot])
    value_t[...] = value[...].astype(F32).T.astype(BF)
    allowed = causal(tile)
    for i in range(query.shape[0] // tile):
        low, high = i * tile, (i + 1) * tile
        rows = query[low:high, :]
        near = jnp.where(allowed, dot_nt(key[low:high, :], rows) * HD ** (-0.5), -1e30)
        top = jnp.max(near, axis=0, keepdims=True)
        if i:
            far = dot_nt(key[0:low, :], rows) * HD ** (-0.5)
            top = jnp.maximum(top, jnp.max(far, axis=0, keepdims=True))
        near = jnp.exp(near - top)
        total = jnp.sum(near, axis=0, keepdims=True)
        summed = dot_nn(value_t[:, low:high], near.astype(BF))
        if i:
            far = jnp.exp(far - top)
            total = total + jnp.sum(far, axis=0, keepdims=True)
            summed = summed + dot_nn(value_t[:, 0:low], far.astype(BF))
        mixed[low:high, :] = (summed / total).T
        log_ref[0, :, low:high] = top + jnp.log(total)
    out_of_order(at_ref, mixed, out_ref, piece)


def attend(own, other, at, piece):
    half, width = own.shape[1:]
    rows = 2 * half
    heads = width // HD
    return pl.pallas_call(
        functools.partial(attend_kernel, piece, 256),
        grid_spec=pltpu.PrefetchScalarGridSpec(
            num_scalar_prefetch=1,
            grid=(heads,),
            in_specs=[pl.BlockSpec((3, half, HD), lambda h, at: (0, 0, h))] * 2,
            out_specs=[
                pl.BlockSpec((rows, HD), lambda h, at: (0, h)),
                pl.BlockSpec((1, 1, rows), lambda h, at: (h, 0, 0)),
            ],
            scratch_shapes=[pltpu.VMEM((rows, HD), BF)] * 3 + [pltpu.VMEM((HD, rows), BF), pltpu.VMEM((rows, HD), F32)],
        ),
        out_shape=[jax.ShapeDtypeStruct((rows, width), BF), jax.ShapeDtypeStruct((heads, 1, rows), F32)],
        compiler_params=pltpu.CompilerParams(vmem_limit_bytes=VMEM_LIMIT),
        cost_estimate=pl.CostEstimate(
            flops=2 * 2 * heads * rows * rows * HD, bytes_accessed=8 * rows * width, transcendentals=heads * rows * rows // 2
        ),
        name="attend",
    )(at, own, other)


def attend_back_kernel(
    piece, tile, at_ref, own_ref, other_ref, out_ref, grad_ref, log_ref, dqkv_ref, query, key, value, key_t, grad, mixed, dquery, dkey, dvalue
):
    for slot, held in enumerate((query, key, value)):
        in_order(at_ref, own_ref.at[slot], held, piece, other_ref.at[slot])
    in_order(at_ref, grad_ref, grad, piece)
    in_order(at_ref, out_ref, mixed, piece)
    key_t[...] = key[...].astype(F32).T.astype(BF)
    allowed = causal(tile)
    dkey[...] = jnp.zeros_like(dkey)
    dvalue[...] = jnp.zeros_like(dvalue)
    scale = HD ** (-0.5)
    for i in range(query.shape[0] // tile):
        low, high = i * tile, (i + 1) * tile
        rows = query[low:high, :]
        rows_grad = grad[low:high, :]
        log = log_ref[0, :, low:high]
        spread = jnp.sum((rows_grad.astype(F32) * mixed[low:high, :].astype(F32)).T, axis=0, keepdims=True)
        dquery_t = None
        for start, stop, masked in ((0, low, False), (low, high, True)):
            if start == stop:
                continue
            scores = dot_nt(key[start:stop, :], rows) * scale
            if masked:
                scores = jnp.where(allowed, scores, -1e30)
            probs = jnp.exp(scores - log)
            probs_grad = dot_nt(value[start:stop, :], rows_grad)
            scores_grad = (probs * (probs_grad - spread)).astype(BF)
            dvalue[start:stop, :] += dot_nn(probs.astype(BF), rows_grad)
            dkey[start:stop, :] += dot_nn(scores_grad, rows)
            term = dot_nn(key_t[:, start:stop], scores_grad)
            dquery_t = term if dquery_t is None else dquery_t + term
        dquery[low:high, :] = dquery_t.T * scale
    dkey[...] = dkey[...] * scale
    for slot, held in enumerate((dquery, dkey, dvalue)):
        out_of_order(at_ref, held, dqkv_ref.at[slot], piece)


def attend_back(own, other, out, grad, log, at, piece):
    half, width = own.shape[1:]
    rows = 2 * half
    heads = width // HD
    return pl.pallas_call(
        functools.partial(attend_back_kernel, piece, 256),
        grid_spec=pltpu.PrefetchScalarGridSpec(
            num_scalar_prefetch=1,
            grid=(heads,),
            in_specs=[
                pl.BlockSpec((3, half, HD), lambda h, at: (0, 0, h)),
                pl.BlockSpec((3, half, HD), lambda h, at: (0, 0, h)),
                pl.BlockSpec((rows, HD), lambda h, at: (0, h)),
                pl.BlockSpec((rows, HD), lambda h, at: (0, h)),
                pl.BlockSpec((1, 1, rows), lambda h, at: (h, 0, 0)),
            ],
            out_specs=pl.BlockSpec((3, rows, HD), lambda h, at: (0, 0, h)),
            scratch_shapes=[pltpu.VMEM((rows, HD), BF)] * 3
            + [pltpu.VMEM((HD, rows), BF)]
            + [pltpu.VMEM((rows, HD), BF)] * 2
            + [pltpu.VMEM((rows, HD), F32)] * 3,
        ),
        out_shape=jax.ShapeDtypeStruct((3, rows, width), BF),
        compiler_params=pltpu.CompilerParams(vmem_limit_bytes=VMEM_LIMIT),
        cost_estimate=pl.CostEstimate(
            flops=5 * heads * rows * rows * HD * 2, bytes_accessed=16 * rows * width, transcendentals=heads * rows * rows // 2
        ),
        name="attend_back",
    )(at, own, other, out, grad, log)


def local(
    tokens,
    block_order,
    query_weight,
    key_weight,
    value_weight,
    output_weight,
    gate_weight,
    up_weight,
    down_weight,
    query_gain,
    key_gain,
    attention_gain,
    forward_gain,
    cotangent,
):
    seqs, local_len, width = tokens.shape
    ranks = lax.axis_size("context")
    columns = lax.axis_size("tensor")
    full_len = local_len * ranks
    piece_len = full_len // block_order.shape[0]
    piece = local_len // columns
    shard_rows = seqs * piece
    count = shard_rows * columns
    context = lax.axis_index("context")
    t = lax.axis_index("tensor")
    s, core = context // 2, context % 2
    head_width = query_weight.shape[1]
    half_width = head_width // 2
    hidden_width = gate_weight.shape[1]

    rows, w_first, gate_up_shard, row_shard = start(
        tokens,
        [query_weight, key_weight, value_weight],
        output_weight,
        jnp.stack([attention_gain, forward_gain]),
        [gate_weight, up_weight],
        seqs,
    )
    qkv_width = 3 * head_width
    gains = w_first[:, 4 * head_width :]
    gain_attn, gain_feed = gains[:, 0].astype(F32)[None], gains[:, 1].astype(F32)[None]
    w_gate_up = lax.all_gather(gate_up_shard, "context", axis=0, tiled=True)

    chips = s ^ jnp.arange(seqs, dtype=jnp.int32)
    shards = t ^ jnp.arange(columns, dtype=jnp.int32)
    starts = (2 * chips[None, :] + core) * local_len + shards[:, None] * piece
    stored = (starts[:, :, None] + jnp.arange(piece, dtype=jnp.int32)).reshape(count)
    block = stored // piece_len
    slots = jnp.arange(block_order.shape[0], dtype=jnp.int32)
    place = jnp.sum(jnp.where(block[:, None] == slots[None, :], block_order[None, :], 0), axis=1) * piece_len
    place = place + stored % piece_len
    freq = THETA ** (-jnp.arange(0, HD, 2, dtype=F32) / HD)
    angle = place.astype(F32)[:, None] * freq[None, :]
    cosine = jnp.concatenate([jnp.cos(angle), jnp.cos(angle)], axis=-1)
    sine = jnp.concatenate([-jnp.sin(angle), jnp.sin(angle)], axis=-1)
    per_block = piece_len // piece
    pieces = jnp.arange(full_len // piece, dtype=jnp.int32)
    hits = block_order[None, :] == (pieces // per_block)[:, None]
    block_at = jnp.sum(jnp.where(hits, slots[None, :], 0), axis=1)
    piece_at = block_at * per_block + pieces % per_block
    rank_of, shard_of = piece_at // columns, piece_at % columns
    at = (((rank_of % 2) ^ core) * columns + (shard_of ^ t)) * seqs + ((rank_of // 2) ^ s)
    at = (at * piece).astype(jnp.int32)

    qkv_raw = dot_nn(rows, w_first[:, :qkv_width])
    query_raw = qkv_raw[:, :head_width]
    key_raw = qkv_raw[:, head_width : 2 * head_width]
    totals = sum_over_tensor(jnp.stack([jnp.sum(query_raw * query_raw, axis=1), jnp.sum(key_raw * key_raw, axis=1)]))
    factors = lax.rsqrt(totals / width + EPS)
    scaling = jnp.stack([query_gain, key_gain]).astype(F32)
    keep, send = by_rows(
        turn_kernel,
        "turn",
        core,
        [(qkv_raw, 0), (columns_of(*factors), 0), (scaling, None), (cosine, 0), (sine, 0)],
        [((3, count, half_width), BF, 1)] * 2,
    )
    received = swap(send, "context", 1)
    mixed_heads, log = attend(keep, received, at, piece)

    def to_heads(values):
        keep = lax.dynamic_slice_in_dim(values, core * half_width, half_width, axis=1)
        send = lax.dynamic_slice_in_dim(values, (1 - core) * half_width, half_width, axis=1)
        return jnp.concatenate([keep, swap(send, "context", 1)], axis=0)

    def to_rows(values):
        own, other = values[:count], swap(values[count:], "context", 1)
        return jnp.concatenate([jnp.where(core == 0, own, other), jnp.where(core == 0, other, own)], axis=1)

    mixed_low = to_rows(mixed_heads)

    def chunk(values, k):
        return values[k * shard_rows : (k + 1) * shard_rows]

    order = list(range(columns))
    shard = (shard_rows, width)
    hidden_low, attended, hidden = exchange(
        "attended", 1, mixed_low, w_first, finish_attended, [row_shard, gain_attn], [(shard, F32), (shard, F32)], offset=qkv_width
    )

    fed_low, slopes, act_low, w_down, upstream, _, output_pieces, feed_gain_rows = feed(
        hidden_low, w_gate_up, down_weight.T, cotangent, hidden, gain_feed, seqs
    )

    own = width // ranks
    cores = [list(range(0, ranks, 2)), list(range(1, ranks, 2))]

    def scatter(values):
        return lax.psum_scatter(values, "context", scatter_dimension=0, axis_index_groups=cores, tiled=True)

    output_pieces = output_pieces.reshape(shard)
    split = seqs // 4 * piece
    down_part, first_rows = rank_sums(5, [(fed_low, act_low)], own, (output_pieces, 0, split))
    down_summed = scatter(down_part)
    down_grad = down_summed.astype(F32).T
    gate_up_low = act_back(after(fed_low, down_part), w_down, slopes)
    gate_up_part, other_rows = rank_sums(6, [(hidden_low, gate_up_low)], own, (output_pieces, split, shard_rows - split))
    layer_output = in_place([values.reshape(columns, -1, piece, width) for values in (first_rows, other_rows)], s, t, BF)
    gate_up_summed = scatter(gate_up_part)
    gate_up_low = after(gate_up_low, gate_up_part)
    attended_low, hidden_grad, attn_gain_rows = exchange(
        "hidden_grad",
        3,
        gate_up_low,
        w_gate_up,
        finish_hidden_grad,
        [attended, upstream, gain_attn],
        [(shard, F32), ((8, width), F32)],
    )
    attended_low = after(attended_low, layer_output)
    mixed_grad = dot_nn(attended_low, w_first[:, qkv_width : 4 * head_width]).astype(BF)
    dqkv = attend_back(keep, received, mixed_heads, to_heads(mixed_grad), log, at, piece)
    dqkv_other = swap(dqkv[:, count:], "context", 1)
    inner, head_gain_rows = by_rows(
        inner_kernel,
        "inner",
        core,
        [(dqkv, 1), (dqkv_other, 1), (qkv_raw, 0), (columns_of(*factors), 0), (scaling, None), (cosine, 0), (sine, 0)],
        [((2, 8, count), F32, 2), ((2, 8, head_width), F32, None)],
    )
    inner = sum_over_tensor(inner[:, 0])
    (qkv_low,) = by_rows(
        raw_grad_kernel,
        "raw_grad",
        core,
        [
            (dqkv, 1),
            (dqkv_other, 1),
            (qkv_raw, 0),
            (after(columns_of(*factors, *(inner * factors**3 / width)), down_grad), 0),
            (scaling, None),
            (cosine, 0),
            (sine, 0),
        ],
        [((count, 3 * head_width), BF, 0)],
    )
    (qkv_part,) = rank_sums(7, [(rows, qkv_low), (attended_low, mixed_low)], own)
    qkv_out_summed = scatter(after(qkv_part, gate_up_summed, down_summed))
    every, width_gains, head_gains = exchange(
        "tokens_grad",
        4,
        after(qkv_low, qkv_part),
        w_first,
        None,
        [hidden_grad, attn_gain_rows, feed_gain_rows, head_gain_rows.reshape(16, head_width)],
        [((8, own), F32), ((8, head_width), F32)],
        chips=seqs,
        last=True,
    )
    tokens_grad = in_place([every.reshape(columns, seqs, piece, width)], s, t, F32)

    gate_up_summed, qkv_out_summed = gate_up_summed.astype(F32), qkv_out_summed.astype(F32)
    return (
        layer_output,
        tokens_grad,
        qkv_out_summed[:, :head_width],
        qkv_out_summed[:, head_width : 2 * head_width],
        qkv_out_summed[:, 2 * head_width : 3 * head_width],
        qkv_out_summed[:, 3 * head_width :].T,
        gate_up_summed[:, :hidden_width],
        gate_up_summed[:, hidden_width:],
        down_grad,
        head_gains[0],
        head_gains[1],
        width_gains[0],
        width_gains[1],
    )


def solution(mesh):
    return jax.shard_map(
        local,
        mesh=mesh,
        in_specs=(
            P(None, "context", None),
            P(),
            P("context", "tensor"),
            P("context", "tensor"),
            P("context", "tensor"),
            P("tensor", "context"),
            P("context", "tensor"),
            P("context", "tensor"),
            P("tensor", "context"),
            P("tensor"),
            P("tensor"),
            P("context"),
            P("context"),
            P(None, "context", None),
        ),
        out_specs=(
            P(None, "context", None),
            P(None, "context", None),
            P("context", "tensor"),
            P("context", "tensor"),
            P("context", "tensor"),
            P("tensor", "context"),
            P("context", "tensor"),
            P("context", "tensor"),
            P("tensor", "context"),
            P("tensor"),
            P("tensor"),
            P("context"),
            P("context"),
        ),
        check_vma=False,
    )
```
